32 devices in a mesh: groups: 2 (over y), space: 4 (over z), season: 2 (over x), var: 2 (over core).
Axes of the slice: x: 2, y: 2, z: 4, core: 2. Of those that a mesh axis runs over, the one named last changes fastest.
Arguments:
- right_side: float32 [64, 2, 32768], P('season', 'var', ('groups', 'space')), parts along dimension 2, may hold values from -60 to 60
- spatial: float32 [256, 3, 128, 128], P(('groups', 'space')), parts along dimension 0, as said below
- columns: int32 [256, 3], P(('groups', 'space')), parts along dimension 0, may hold values from 0 to 127, as said below
- counts: int32 [256], P(('groups', 'space')), parts along dimension 0, may hold values from 1 to 64, as said below
- season_cov: float32 [64, 2, 64, 2], replicated, as said below
Outputs:
- solution_field: float32 [64, 2, 32768], P('season', 'var', ('groups', 'space')), parts along dimension 2
- residual: float32 [64, 2, 32768], P('season', 'var', ('groups', 'space')), parts along dimension 2
The draws below stay inside these ranges and needn't reach their ends.
There are 2 independent parts, one for each index of `groups`. The reference program is written for one: setup_inputs(seed, part) draws one part's arguments, and reference() takes and returns one part's arrays. A program takes and returns all parts, laid end to end along the dimension named above; an argument that names none is the same for every part. Nothing has to cross between parts.
Inputs may be any that keep to these rules, and one draw needn't show every extreme that they name: `columns`: each row's first entry is the row's own block; the second is the block before it and the third the block after it where the taper couples them, else the row's own block with an all-zero stored block. The observed seasons of a block are its last counts seasons. `spatial`: symmetric as a whole: the block stored for row i at column j is the transpose of the block stored for row j at column i, and each diagonal block is symmetric. `season_cov`: Symmetric.
All inputs are finite; a program needn't handle non-finite values.
Results may differ from the reference program's by a relative error of at most 0.015.
Values sent between devices are 32-bit elements; how exact they have to be, the bound alone decides.
No kernel may reach another device: no remote copies, remote signals or barrier semaphores. Data moves between devices by JAX's collectives and lax.ppermute only.
A program may use at most 64 MiB of HBM per device.

```python
import jax
import jax.numpy as jnp
from jax import lax

BLOCK = 128
SEASONS = 64
VARS = 2
REACH = 1
ITERS = 2
NBLK = 128
NCELLS = 16384


def taper_links(key):
    link_key = jax.random.fold_in(key, 11)
    links = (jax.random.randint(link_key, (NBLK,), 0, 4, jnp.int32) > 0).astype(jnp.int32)
    return links.at[NBLK - 1].set(0)


def draw_spatial(key, part):
    links = taper_links(key)
    key = jax.random.fold_in(key, 1)
    key_off, key_diag, key_sym = jax.random.split(key, 3)
    bound = 0.5 / BLOCK
    shape = (NBLK, BLOCK, BLOCK)
    upper = jax.random.uniform(key_off, shape, jnp.float32, -bound, bound)
    inner = jax.random.uniform(key_sym, shape, jnp.float32, -bound, bound)
    upper = upper * links.astype(jnp.float32)[:, None, None]
    lower = jnp.concatenate([jnp.zeros((1, BLOCK, BLOCK), jnp.float32), jnp.swapaxes(upper[:-1], 1, 2)], axis=0)
    eye = jnp.eye(BLOCK, dtype=jnp.float32)
    diag = jax.random.uniform(key_diag, (NBLK, BLOCK), jnp.float32, 1.0, 2.0)
    own = 0.5 * (inner + jnp.swapaxes(inner, 1, 2)) * (1.0 - eye)[None] + eye[None] * diag[:, :, None]
    return jnp.stack([own, lower, upper], axis=1)


def draw_season_cov(key, part):
    key = jax.random.fold_in(key, 2)
    key_off, key_diag = jax.random.split(key)
    order = SEASONS * VARS
    bound = 0.5 / (order - 1)
    raw = jax.random.uniform(key_off, (order, order), jnp.float32, -bound, bound)
    eye = jnp.eye(order, dtype=jnp.float32)
    sym = 0.5 * (raw + raw.T) * (1.0 - eye)
    diag = jax.random.uniform(key_diag, (order,), jnp.float32, 1.0, 2.0)
    return (sym + eye * diag[None, :]).reshape(SEASONS, VARS, SEASONS, VARS)


def draw_columns(key, part):
    links = taper_links(key)
    rows = jnp.arange(NBLK, dtype=jnp.int32)
    before = jnp.concatenate([jnp.zeros((1,), jnp.int32), links[:-1]])
    left = jnp.where(before == 1, rows - 1, rows)
    right = jnp.where(links == 1, rows + 1, rows)
    return jnp.stack([rows, left, right], axis=1).astype(jnp.int32)


def draw_counts(key, part):
    key = jax.random.fold_in(key, 4)
    drawn = jax.random.randint(key, (NBLK,), 1, SEASONS + 1, jnp.int32)
    return drawn.at[0].set(SEASONS).at[NBLK - 1].set(1)


def levels(rng, shape, pieces, smallest, top_value):
    factor_of = 1.0
    for position, shards_of in pieces:
        steps = jax.random.uniform(jax.random.fold_in(jax.random.fold_in(rng, 6), position), (shards_of,), jnp.float32, smallest / len(pieces), top_value / len(pieces))
        factor_of = factor_of * jnp.repeat(jnp.exp(steps), shape[position] // shards_of).reshape((-1,) + (1,) * (len(shape) - 1 - position))
    return factor_of


def normal_values(stream_key, dims, deviation, most, cuts=(), kind=jnp.bfloat16):
    factor_of = levels(stream_key, dims, cuts, -0.22, 0.18) if cuts else 1.0
    result = jax.random.normal(stream_key, dims, jnp.float32) * deviation * factor_of
    return jnp.minimum(jnp.maximum(result, -most), most).astype(kind)


def setup_inputs(seed: int = 0, part: int = 0) -> dict:
    key_of = jax.random.split(jax.random.key(seed), 6)
    part_splits = jax.random.split(jax.random.fold_in(key_of[5], part), 6)
    return {
        "right_side": normal_values(part_splits[0], (SEASONS, VARS, NCELLS), 10.0, 60.0, ((0, 2), (1, 2), (2, 4)), jnp.float32),
        "spatial": draw_spatial(jax.random.fold_in(jax.random.fold_in(key_of[5], part), 71), part),
        "columns": draw_columns(jax.random.fold_in(jax.random.fold_in(key_of[5], part), 71), part),
        "counts": draw_counts(jax.random.fold_in(jax.random.fold_in(key_of[5], part), 71), part),
        "season_cov": draw_season_cov(jax.random.fold_in(key_of[5], 71), part),
    }


nugget_level = 10.5


def space_apply(field, spatial, columns):
    padded = jnp.pad(field, ((0, 0), (0, 0), (REACH, REACH), (0, 0)))
    picked = padded[:, :, (columns + REACH).astype(jnp.int32), :]
    return jnp.einsum("ikac,svikc->svia", spatial, picked, precision=lax.Precision.HIGHEST)


def operate(field, spatial, columns, observed, season_cov):
    moved = space_apply(observed * field, spatial, columns)
    mixed = jnp.einsum("svtw,twnc->svnc", season_cov, moved, precision=lax.Precision.HIGHEST)
    return nugget_level * field + observed * mixed


def reference(right_side, spatial, columns, counts, season_cov):
    seasons = jnp.arange(SEASONS, dtype=jnp.int32)
    observed = (seasons[:, None] >= SEASONS - counts[None, :]).astype(jnp.float32)
    observed = observed[:, None, :, None]
    target = right_side.reshape(SEASONS, VARS, NBLK, BLOCK)
    solution_field = jnp.zeros_like(target)
    residual = target
    direction = target
    norm_now = jnp.sum(residual * residual)
    for step in range(ITERS):
        image = operate(direction, spatial, columns, observed, season_cov)
        alpha = norm_now / jnp.sum(direction * image)
        solution_field = solution_field + alpha * direction
        residual = residual - alpha * image
        norm_next = jnp.sum(residual * residual)
        direction = residual + (norm_next / norm_now) * direction
        norm_now = norm_next
    return (solution_field.reshape(SEASONS, VARS, NCELLS), residual.reshape(SEASONS, VARS, NCELLS))
```

```python
import functools

import jax
import jax.numpy as jnp
from jax import lax
from jax.experimental import pallas as pl
from jax.experimental.pallas import tpu as pltpu
from jax.sharding import PartitionSpec as P

SEASONS = 64
VARS = 2
ORDER = SEASONS * VARS
REACH = 1
NUGGET = 10.5
CUTS = (12, 24)

F32 = jnp.float32
BF16 = jnp.bfloat16
NT = (((1,), (1,)), ((), ()))
NN = (((1,), (0,)), ((), ()))
VMEM = pltpu.VMEM


def dot(a, b, dims):
    return lax.dot_general(a, b, dims, preferred_element_type=F32)


def halves(x):
    high = x.astype(BF16)
    return high, (x - high.astype(F32)).astype(BF16)


def fold(x):
    return jnp.sum(x.reshape(x.shape[0] // 8, 8, x.shape[1]), axis=0)


def pack_kernel(cuts, x_ref, *out_refs):
    blocks = cuts[-1]
    seasons = x_ref.shape[0] // blocks
    for ref, first, last in zip(out_refs, cuts[:-1], cuts[1:]):
        for j in range(first, last):
            ref[j - first] = x_ref[pl.ds(j, seasons, stride=blocks), :]


def pack(x, cuts):
    blocks = cuts[-1]
    seasons, width = x.shape[0] // blocks, x.shape[1]
    return pl.pallas_call(
        functools.partial(pack_kernel, cuts),
        out_shape=[
            jax.ShapeDtypeStruct((last - first, seasons, width), F32)
            for first, last in zip(cuts[:-1], cuts[1:])
        ],
        name="pack",
    )(x)


def prepare_kernel(w_ref, r_ref, w2_ref, rh_ref, rl_ref, scale_ref, top_ref):
    step = pl.program_id(0)

    @pl.when(step == 0)
    def _():
        top_ref[...] = jnp.zeros_like(top_ref)

    width = w_ref.shape[2]
    top = top_ref[...]
    for i in range(w_ref.shape[0]):
        for place, slot in enumerate((1, 0, 2)):
            w = w_ref[i, slot]
            high, low = halves(w)
            lanes = slice(place * width, (place + 1) * width)
            w2_ref[i, :width, lanes] = high
            w2_ref[i, width:, lanes] = low
            top = jnp.maximum(top, jnp.max(jnp.abs(w).reshape(-1, 8, width), axis=0))
    top_ref[...] = top

    @pl.when(step == pl.num_programs(0) - 1)
    def _():
        space_top = jnp.max(jnp.max(top, axis=0, keepdims=True), axis=1, keepdims=True)
        r = r_ref[...]
        season_top = jnp.max(jnp.max(jnp.abs(r), axis=0, keepdims=True), axis=1, keepdims=True)
        space_top = jnp.where(space_top > 0, space_top, 1.0)
        season_top = jnp.where(season_top > 0, season_top, 1.0)
        high, low = halves(r / season_top / space_top)
        rh_ref[...] = high
        rl_ref[...] = low
        rows = lax.broadcasted_iota(jnp.int32, scale_ref.shape, 0)
        scale_ref[...] = jnp.where(rows == 4, space_top, jnp.where(rows == 5, season_top, 0.0))


def prepare(spatial, season):
    blocks, slots, width, _ = spatial.shape
    rows = 4
    return pl.pallas_call(
        prepare_kernel,
        grid=(blocks // rows,),
        in_specs=[
            pl.BlockSpec((rows, slots, width, width), lambda i: (i, 0, 0, 0)),
            pl.BlockSpec((ORDER, ORDER), lambda i: (0, 0)),
        ],
        out_specs=[
            pl.BlockSpec((rows, 2 * width, slots * width), lambda i: (i, 0, 0)),
            pl.BlockSpec((ORDER, ORDER), lambda i: (0, 0)),
            pl.BlockSpec((ORDER, ORDER), lambda i: (0, 0)),
            pl.BlockSpec((8, 128), lambda i: (0, 0)),
        ],
        out_shape=[
            jax.ShapeDtypeStruct((blocks, 2 * width, slots * width), BF16),
            jax.ShapeDtypeStruct((ORDER, ORDER), BF16),
            jax.ShapeDtypeStruct((ORDER, ORDER), BF16),
            jax.ShapeDtypeStruct((8, 128), F32),
        ],
        scratch_shapes=[VMEM((8, width), F32)],
        name="prepare",
    )(spatial, season)


def make_plan(cuts):
    blocks = cuts[-1]
    stages = []
    have_x, have_1, have_2 = set(), set(), set()
    count = len(cuts) - 1
    for m in range(count):
        new = list(range(cuts[m], cuts[m + 1]))
        if m == count - 1:
            new = new + [-2, -1, blocks, blocks + 1]
        have_x |= set(new)
        ones = [
            i for i in range(-1, blocks + 1)
            if i not in have_1 and {i - 1, i, i + 1} <= have_x
        ]
        have_1 |= set(ones)
        twos = [
            i for i in range(blocks) if i not in have_2 and {i - 1, i, i + 1} <= have_1
        ]
        have_2 |= set(twos)
        later_1 = [i for i in range(-1, blocks + 1) if i not in have_1]
        later_2 = [i for i in range(blocks) if i not in have_2]
        keep_x = sorted({i + d for i in later_1 for d in (-1, 0, 1)} & have_x)
        keep_1 = sorted({i + d for i in later_2 for d in (-1, 0, 1)} & have_1)
        stages.append((new, ones, twos, keep_x, keep_1))
    return stages


def runs(ids, most):
    groups = []
    for i in ids:
        if groups and len(groups[-1]) < most:
            groups[-1].append(i)
        else:
            groups.append([i])
    return groups


def make_stage(plan, m, blocks, seasons, width, slots):
    new, ones, twos, keep_x, keep_1 = plan[m]
    first, last = m == 0, m == len(plan) - 1
    old_x, old_1 = ([], []) if first else (plan[m - 1][3], plan[m - 1][4])
    x_at = {i: n for n, i in enumerate(list(old_x) + list(new))}
    one_at = {i: n for n, i in enumerate(list(old_1) + list(ones))}
    inner_ones = [i for i in ones if 0 <= i < blocks]

    def kernel(*refs):
        refs = list(refs)

        def take(n):
            out = refs[:n]
            del refs[:n]
            return out

        (place_ref,) = take(1)
        field_refs = take(slots)
        w2_ref, rh_ref, rl_ref, count_ref, sums_in = take(5)
        if not first:
            old_xh, old_xl, old_1h, old_1l = take(4)
        if last:
            wide_ref, edge_ref = take(2)
        sums_out, own_1, own_2 = take(3)
        if not last:
            keep_xh, keep_xl, keep_1h, keep_1l = take(4)
        xh, xl, oh, ol, pick = take(5)

        def count_row(i):
            if 0 <= i < blocks:
                return count_ref[i : i + 1, :]
            at = i + 2 if i < 0 else i - blocks + 2
            return edge_ref[at : at + 1, :]

        def iota(rows):
            return lax.broadcasted_iota(jnp.int32, (rows, width), 0)

        season = lax.rem(iota(ORDER), SEASONS).astype(F32)

        def masked(i, value):
            return jnp.where(season >= SEASONS - count_row(i), value, 0.0)

        for n in range(len(old_x)):
            xh[n] = old_xh[n]
            xl[n] = old_xl[n]
        for n in range(len(old_1)):
            oh[n] = old_1h[n]
            ol[n] = old_1l[n]

        total_0 = sums_in[0]
        for k in range(slots):
            at = pl.multiple_of(place_ref[k], seasons)
            piece_season = (iota(seasons) + lax.rem(at, SEASONS)).astype(F32)
            for n, i in enumerate(new):
                piece = field_refs[k][n]
                if 0 <= i < blocks:
                    total_0 += fold(piece * piece)
                seen = piece_season >= SEASONS - count_row(i)
                high, low = halves(jnp.where(seen, piece, 0.0))
                xh[x_at[i], pl.ds(at, seasons), :] = high
                xl[x_at[i], pl.ds(at, seasons), :] = low
        sums_out[0] = total_0

        def space(i, high, low, at):
            if 0 <= i < blocks:
                hs = jnp.concatenate([high[at[i + d]] for d in (-1, 0, 1)], axis=1)
                ls = jnp.concatenate([low[at[i + d]] for d in (-1, 0, 1)], axis=1)
                both = dot(hs, w2_ref[i], NT)
                return both[:, :width] + both[:, width:] + dot(ls, w2_ref[i, :width, :], NT)
            e, inner, far = (0, 0, -2) if i < 0 else (1, blocks - 1, blocks + 1)
            lanes = slice(0, width) if i < 0 else slice(2 * width, 3 * width)
            near_high = w2_ref[inner, :width, lanes]
            total = dot(high[at[inner]], near_high, NN)
            total += dot(high[at[inner]], w2_ref[inner, width:, lanes], NN)
            total += dot(low[at[inner]], near_high, NN)
            for slot, j in enumerate((i, far)):
                wh, wl = halves(wide_ref[e, slot * width : (slot + 1) * width, :])
                total += dot(high[at[j]], wh, NT) + dot(high[at[j]], wl, NT)
                total += dot(low[at[j]], wh, NT)
            return total

        def mix(parts):
            zh, zl = halves(jnp.concatenate(parts, axis=1))
            lhs = jnp.concatenate([rh_ref[...], rh_ref[...], rl_ref[...]], axis=1)
            return dot(lhs, jnp.concatenate([zh, zl, zh], axis=0), NN)

        own = pl.multiple_of(place_ref[slots], seasons)
        total_1, total_2, total_3 = sums_in[1], sums_in[2], sums_in[3]
        for group in runs(ones, 4):
            mixed = mix([space(i, xh, xl, x_at) for i in group])
            for n, i in enumerate(group):
                one = masked(i, mixed[:, n * width : (n + 1) * width])
                high, low = halves(one)
                oh[one_at[i]] = high
                ol[one_at[i]] = low
                if 0 <= i < blocks:
                    x = xh[x_at[i]].astype(F32) + xl[x_at[i]].astype(F32)
                    total_1 += fold(x * one)
                    total_2 += fold(one * one)
                    n_own = inner_ones.index(i)
                    pick[n_own] = one
                    own_1[n_own] = pick[n_own, pl.ds(own, seasons), :]
        sums_out[1] = total_1
        sums_out[2] = total_2
        for group in runs(twos, 4):
            mixed = mix([space(i, oh, ol, one_at) for i in group])
            for n, i in enumerate(group):
                two = masked(i, mixed[:, n * width : (n + 1) * width])
                one = oh[one_at[i]].astype(F32) + ol[one_at[i]].astype(F32)
                total_3 += fold(one * two)
                n_own = len(inner_ones) + twos.index(i)
                pick[n_own] = two
                own_2[twos.index(i)] = pick[n_own, pl.ds(own, seasons), :]
        sums_out[3] = total_3
        if not last:
            for n, i in enumerate(keep_x):
                keep_xh[n] = xh[x_at[i]]
                keep_xl[n] = xl[x_at[i]]
            for n, i in enumerate(keep_1):
                keep_1h[n] = oh[one_at[i]]
                keep_1l[n] = ol[one_at[i]]

    tile = (ORDER, width)
    outs = [
        jax.ShapeDtypeStruct((4, 8, width), F32),
        jax.ShapeDtypeStruct((len(inner_ones), seasons, width), F32),
        jax.ShapeDtypeStruct((len(twos), seasons, width), F32),
    ]
    if not last:
        outs += [jax.ShapeDtypeStruct((len(keep_x),) + tile, BF16)] * 2
        outs += [jax.ShapeDtypeStruct((len(keep_1),) + tile, BF16)] * 2
    scratch = [VMEM((len(x_at),) + tile, BF16)] * 2 + [VMEM((len(one_at),) + tile, BF16)] * 2
    scratch += [VMEM((len(inner_ones) + len(twos),) + tile, F32)]
    return kernel, outs, scratch


def run_stage(plan, m, blocks, seasons, width, fields, *operands):
    kernel, outs, scratch = make_stage(plan, m, blocks, seasons, width, len(fields))
    place, rest = operands[0], operands[1:]
    count = len(fields) + len(rest)
    return pl.pallas_call(
        kernel,
        in_specs=[pl.BlockSpec(memory_space=pltpu.SMEM)]
        + [pl.BlockSpec(memory_space=VMEM)] * count,
        out_shape=outs,
        scratch_shapes=scratch,
        compiler_params=pltpu.CompilerParams(vmem_limit_bytes=40 << 20),
        name="stage",
    )(place, *fields, *rest)


def finish_kernel(plan, blocks, gathered_ref, x_ref, *refs):
    count = len(plan)
    ones, twos = refs[:count], refs[count : 2 * count]
    x_out, r_out = refs[2 * count :]
    seasons = x_ref.shape[0] // blocks

    def total(v):
        return jnp.sum(v, axis=1, keepdims=True)

    tuples = [gathered_ref[j] for j in range(gathered_ref.shape[0])]
    top = functools.reduce(jnp.maximum, [t[4:5] for t in tuples])
    sums = [0.0, 0.0, 0.0, 0.0]
    for t in tuples:
        ratio = t[4:5] / top
        factor = jnp.ones_like(ratio)
        for n in range(4):
            sums[n] = sums[n] + t[n : n + 1] * factor
            factor = factor * ratio
    m0, m1, m2, m3 = [total(v) for v in sums]
    scale = (top * tuples[0][5:6])[:, :1]
    mine = (tuples[0][4:5] / top)[:, :1]

    first = NUGGET * m0 + scale * m1
    alpha = m0 / first
    lead = alpha * scale
    mean = m1 / m0
    fresh = lead * lead * (m2 - mean * m1)
    c = lead * mean + fresh / m0
    dd = c * c * m0 - 2.0 * c * lead * m1 + lead * lead * m2
    dkd = c * c * m1 - 2.0 * c * lead * m2 + lead * lead * m3
    alpha_2 = fresh / (NUGGET * dd + scale * dkd)
    x_0 = alpha + alpha_2 * c
    x_1 = -alpha_2 * lead * mine
    r_0 = lead * mean - NUGGET * alpha_2 * c
    r_1 = (NUGGET * alpha_2 * lead - lead - alpha_2 * scale * c) * mine
    r_2 = alpha_2 * scale * lead * mine * mine

    where_1, where_2 = {}, {}
    for m, (_, one_ids, two_ids, _, _) in enumerate(plan):
        inner = [i for i in one_ids if 0 <= i < blocks]
        where_1.update({i: (m, n) for n, i in enumerate(inner)})
        where_2.update({i: (m, n) for n, i in enumerate(two_ids)})
    for i in range(blocks):
        rows = pl.ds(i, seasons, stride=blocks)
        x = x_ref[rows, :]
        m, n = where_1[i]
        one = ones[m][n]
        m, n = where_2[i]
        two = twos[m][n]
        x_out[rows, :] = x_0 * x + x_1 * one
        r_out[rows, :] = r_0 * x + r_1 * one + r_2 * two


def finish(plan, blocks, gathered, x, ones, twos):
    return pl.pallas_call(
        functools.partial(finish_kernel, plan, blocks),
        out_shape=[jax.ShapeDtypeStruct(x.shape, F32)] * 2,
        name="finish",
    )(gathered, x, *ones, *twos)


def from_season(value, step):
    size = lax.axis_size("season")
    return lax.ppermute(value, "season", [((i + step) % size, i) for i in range(size)])


def from_var(value):
    return lax.ppermute(value, "var", [(0, 1), (1, 0)])


def gather_space(value):
    size = lax.axis_size("space")
    if size & (size - 1):
        me = lax.axis_index("space")
        return jnp.roll(lax.all_gather(value, "space", axis=0, tiled=True), -me, axis=0)
    have = value
    hop = 1
    while hop < size:
        other = lax.ppermute(have, "space", [(i, i ^ hop) for i in range(size)])
        have = jnp.concatenate([have, other], axis=0)
        hop *= 2
    return have


def body(right_side, spatial, columns, counts, season_cov):
    del columns
    seasons = right_side.shape[0]
    blocks, _, width, _ = spatial.shape
    parts = lax.axis_size("season")
    cuts = (0,) + tuple(c for c in CUTS if c < blocks) + (blocks,)
    plan = make_plan(cuts)

    x = right_side.reshape(seasons * blocks, width)
    packs = list(pack(x, cuts))

    count_rows = jnp.broadcast_to(counts.astype(F32)[:, None], (blocks, width))
    size = lax.axis_size("space")

    def message(own, slots, ids):
        slab = x.reshape(seasons, blocks, width)[:, ids[0] : ids[1] + 1].transpose(1, 0, 2)
        tail = jnp.concatenate(
            [count_rows[ids[0] : ids[1] + 1], jnp.zeros((6, width), F32)], axis=0
        )
        wide = jnp.concatenate([spatial[own, slot] for slot in slots], axis=0)
        return jnp.concatenate([slab.reshape(2 * seasons, width), wide, tail], axis=0)

    up = [(i, i + 1) for i in range(size - 1)]
    down = [(i + 1, i) for i in range(size - 1)]
    below = lax.ppermute(message(blocks - 1, (0, 1), (blocks - 2, blocks - 1)), "space", up)
    above = lax.ppermute(message(0, (0, 2), (0, 1)), "space", down)
    halo = jnp.concatenate([below[: 2 * seasons], above[: 2 * seasons]], axis=0)
    halo = halo.reshape(4, seasons, width)
    wide_rows = slice(2 * seasons, 2 * seasons + 2 * width)
    wide = jnp.stack([below[wide_rows], above[wide_rows]])
    last_rows = 2 * seasons + 2 * width
    edge = jnp.concatenate(
        [
            below[last_rows : last_rows + 2],
            above[last_rows : last_rows + 2],
            jnp.zeros((4, width), F32),
        ],
        axis=0,
    )
    packs[-1] = jnp.concatenate([packs[-1], halo], axis=0)

    fields = []
    for part in packs:
        held = [part] + [from_season(part, d) for d in range(1, parts)]
        fields.append([v for h in held for v in (h, from_var(h))])
    me_season, me_var = lax.axis_index("season"), lax.axis_index("var")
    places = [
        (me_var ^ w) * SEASONS + lax.rem(me_season + d, parts) * seasons
        for d in range(parts)
        for w in range(VARS)
    ]
    place = jnp.stack(places + [places[0]]).astype(jnp.int32)

    season = season_cov.transpose(1, 0, 3, 2).reshape(ORDER, ORDER)
    w2, rh, rl, scale = prepare(spatial, season)

    sums = jnp.zeros((4, 8, width), F32)
    ones, twos, kept = [], [], []
    for m in range(len(plan)):
        extra = [wide, edge] if m == len(plan) - 1 else []
        out = run_stage(
            plan, m, blocks, seasons, width, fields[m],
            place, w2, rh, rl, count_rows, sums, *kept, *extra,
        )
        sums, one, two, kept = out[0], out[1], out[2], list(out[3:])
        ones.append(one)
        twos.append(two)
    tile = jnp.concatenate([jnp.sum(sums, axis=1), scale[4:]], axis=0)[None]
    gathered = gather_space(tile)
    x_out, r_out = finish(plan, blocks, gathered, x, ones, twos)
    return x_out.reshape(right_side.shape), r_out.reshape(right_side.shape)


def solution(mesh):
    field = P("season", "var", ("groups", "space"))
    return jax.shard_map(
        body,
        mesh=mesh,
        in_specs=(
            field,
            P(("groups", "space"), None, None, None),
            P(("groups", "space"), None),
            P(("groups", "space")),
            P(),
        ),
        out_specs=(field, field),
        check_vma=False,
    )
```

```python
import functools

import jax
import jax.numpy as jnp
from jax import lax
from jax.experimental import pallas as pl
from jax.experimental.pallas import tpu as pltpu
from jax.sharding import PartitionSpec as P

SEASONS = 64
VARS = 2
ORDER = SEASONS * VARS
REACH = 1
NUGGET = 10.5
CUTS = (4, 10)
STAGES = ((0, 1), (-1,), (2,))

F32 = jnp.float32
BF16 = jnp.bfloat16
NT = (((1,), (1,)), ((), ()))
NN = (((1,), (0,)), ((), ()))
VMEM = pltpu.VMEM


def dot(a, b, dims):
    return lax.dot_general(a, b, dims, preferred_element_type=F32)


def halves(x):
    high = x.astype(BF16)
    return high, (x - high.astype(F32)).astype(BF16)


def fold(x):
    return jnp.sum(x.reshape(x.shape[0] // 8, 8, x.shape[1]), axis=0)


def block_at(half_id, m, blocks):
    return m + half_id * (blocks - 1 - 2 * m)


def pack_kernel(first, last, blocks, x_ref, same_ref, other_ref):
    me = lax.axis_index("var")
    seasons = x_ref.shape[0] // blocks
    for m in range(first, last):
        for half_id, ref in ((me, same_ref), (1 - me, other_ref)):
            rows = pl.ds(block_at(half_id, m, blocks), seasons, stride=blocks)
            ref[m - first] = x_ref[rows, :]


def pack(x, first, last, blocks):
    seasons, width = x.shape[0] // blocks, x.shape[1]
    return pl.pallas_call(
        functools.partial(pack_kernel, first, last, blocks),
        out_shape=[jax.ShapeDtypeStruct((last - first, seasons, width), F32)] * 2,
        name="pack",
    )(x)


def prepare_kernel(blocks, w_ref, r_ref, w2_ref, rh_ref, rl_ref, scale_ref, held, sems):
    me = lax.axis_index("var")
    count, width = held.shape[0], held.shape[2]
    copies = []
    for m in range(count):
        row = block_at(me, m, blocks)
        group = [
            pltpu.make_async_copy(w_ref.at[row, slot], held.at[m, place], sems.at[m, place])
            for place, slot in enumerate((1 + me, 0, 2 - me))
        ]
        for copy in group:
            copy.start()
        copies.append(group)
    top = jnp.zeros((8, width), F32)
    for m in range(count):
        for place, copy in enumerate(copies[m]):
            copy.wait()
            w = held[m, place]
            high, low = halves(w)
            lanes = slice(place * width, (place + 1) * width)
            w2_ref[m, :width, lanes] = high
            w2_ref[m, width:, lanes] = low
            top = jnp.maximum(top, jnp.max(jnp.abs(w).reshape(-1, 8, width), axis=0))
    r = jnp.concatenate(
        [
            jnp.concatenate(
                [r_ref[pl.ds(VARS * v + w, SEASONS, stride=VARS * VARS), :] for w in range(VARS)],
                axis=1,
            )
            for v in range(VARS)
        ],
        axis=0,
    )
    space_top = jnp.max(jnp.max(top, axis=0, keepdims=True), axis=1, keepdims=True)
    season_top = jnp.max(jnp.max(jnp.abs(r), axis=0, keepdims=True), axis=1, keepdims=True)
    space_top = jnp.where(space_top > 0, space_top, 1.0)
    season_top = jnp.where(season_top > 0, season_top, 1.0)
    high, low = halves(r / season_top / space_top)
    rh_ref[...] = high
    rl_ref[...] = low
    rows = lax.broadcasted_iota(jnp.int32, scale_ref.shape, 0)
    scale_ref[...] = jnp.where(rows == 4, space_top, jnp.where(rows == 5, season_top, 0.0))


def prepare(spatial, season):
    blocks, slots, width, _ = spatial.shape
    count = blocks // 2 + 1
    return pl.pallas_call(
        functools.partial(prepare_kernel, blocks),
        in_specs=[pl.BlockSpec(memory_space=pl.ANY), pl.BlockSpec(memory_space=VMEM)],
        out_specs=[pl.BlockSpec(memory_space=VMEM)] * 4,
        out_shape=[
            jax.ShapeDtypeStruct((count, 2 * width, slots * width), BF16),
            jax.ShapeDtypeStruct((ORDER, ORDER), BF16),
            jax.ShapeDtypeStruct((ORDER, ORDER), BF16),
            jax.ShapeDtypeStruct((8, width), F32),
        ],
        scratch_shapes=[
            VMEM((count, slots, width, width), F32),
            pltpu.SemaphoreType.DMA((count, slots)),
        ],
        compiler_params=pltpu.CompilerParams(vmem_limit_bytes=20 << 20),
        name="prepare",
    )(spatial, season)


def row_starts(seasons, parts):
    me_season, me_var = lax.axis_index("season"), lax.axis_index("var")
    return [
        pl.multiple_of(
            lax.rem(me_var + w, VARS) * SEASONS + lax.rem(me_season + d, parts) * seasons, seasons
        )
        for d in range(parts)
        for w in range(VARS)
    ]


def iota(rows, width):
    return lax.broadcasted_iota(jnp.int32, (rows, width), 0)


def edge_kernel(blocks, parts, *refs):
    w_ref, count_ref, *fields, out_ref, sems = refs
    me = lax.axis_index("var")
    seasons, width = fields[0].shape[1:]
    row = block_at(me, 0, blocks)
    copies = [
        pltpu.make_async_copy(
            w_ref.at[row, slot],
            out_ref.at[pl.ds(2 * ORDER + place * width, width)],
            sems.at[place],
        )
        for place, slot in enumerate((0, 2 - me))
    ]
    for copy in copies:
        copy.start()
    for start, field in zip(row_starts(seasons, parts), fields):
        season = (iota(seasons, width) + lax.rem(start, SEASONS)).astype(F32)
        for m in range(2):
            seen = season >= SEASONS - count_ref[pl.ds(block_at(me, m, blocks), 1), :]
            out_ref[pl.ds(m * ORDER + start, seasons), :] = jnp.where(seen, field[m], 0.0)
    last = 2 * ORDER + 2 * width
    out_ref[last:, :] = jnp.broadcast_to(count_ref[pl.ds(row, 1), :], (8, width))
    for copy in copies:
        copy.wait()


def edge(spatial, count_rows, fields, parts):
    blocks, _, width, _ = spatial.shape
    return pl.pallas_call(
        functools.partial(edge_kernel, blocks, parts),
        in_specs=[pl.BlockSpec(memory_space=pl.ANY)]
        + [pl.BlockSpec(memory_space=VMEM)] * (1 + len(fields)),
        out_specs=pl.BlockSpec(memory_space=VMEM),
        out_shape=jax.ShapeDtypeStruct((2 * ORDER + 2 * width + 8, width), F32),
        scratch_shapes=[pltpu.SemaphoreType.DMA((2,))],
        name="edge",
    )(spatial, count_rows, *fields)


def make_plan(cuts, half):
    plan = []
    have_x, have_1, have_2 = set(), set(), set()
    for chunks in STAGES:
        new = []
        for c in chunks:
            new += [-2, -1] if c < 0 else list(range(cuts[c], cuts[c + 1]))
        have_x |= set(new)
        ones = [
            i for i in range(-1, half + 1) if i not in have_1 and {i - 1, i, i + 1} <= have_x
        ]
        have_1 |= set(ones)
        twos = [i for i in range(half) if i not in have_2 and {i - 1, i, i + 1} <= have_1]
        have_2 |= set(twos)
        later_1 = [i for i in range(-1, half + 1) if i not in have_1]
        later_2 = [i for i in range(half) if i not in have_2]
        keep_x = sorted({i + d for i in later_1 for d in (-1, 0, 1)} & have_x)
        keep_1 = sorted({i + d for i in later_2 for d in (-1, 0, 1)} & have_1)
        plan.append((new, ones, twos, keep_x, keep_1))
    return plan


def in_half(ids, half):
    return [i for i in ids if 0 <= i < half]


def runs(ids, most):
    groups = []
    for i in ids:
        if groups and len(groups[-1]) < most:
            groups[-1].append(i)
        else:
            groups.append([i])
    return groups


def make_stage(plan, cuts, m, blocks, parts, seasons, width):
    half = blocks // 2
    slots = parts * VARS
    new, ones, twos, keep_x, keep_1 = plan[m]
    first, last = m == 0, m == len(plan) - 1
    chunks = [c for c in STAGES[m] if c >= 0]
    outer = -1 in STAGES[m]
    old_x, old_1 = ([], []) if first else (plan[m - 1][3], plan[m - 1][4])
    x_at = {i: n for n, i in enumerate(list(old_x) + list(new))}
    one_at = {i: n for n, i in enumerate(list(old_1) + list(ones))}
    inner_ones = in_half(ones, half)

    def kernel(*refs):
        refs = list(refs)

        def take(n):
            out = refs[:n]
            del refs[:n]
            return out

        field_refs = [take(slots) for _ in chunks]
        w2_ref, rh_ref, rl_ref, count_ref, sums_in = take(5)
        if not first:
            old_xh, old_xl, old_1h, old_1l = take(4)
        if outer:
            (edge_ref,) = take(1)
        sums_out, mine, theirs = take(3)
        if not last:
            keep_xh, keep_xl, keep_1h, keep_1l = take(4)
        xh, xl, oh, ol, pick = take(5)
        me = lax.axis_index("var")

        def count_row(i):
            if i == -1:
                return edge_ref[2 * ORDER + 2 * width : 2 * ORDER + 2 * width + 1, :]
            return count_ref[pl.ds(block_at(me, i, blocks), 1), :]

        season = lax.rem(iota(ORDER, width), SEASONS).astype(F32)

        def masked(i, value):
            return jnp.where(season >= SEASONS - count_row(i), value, 0.0)

        for n in range(len(old_x)):
            xh[n] = old_xh[n]
            xl[n] = old_xl[n]
        for n in range(len(old_1)):
            oh[n] = old_1h[n]
            ol[n] = old_1l[n]

        starts = row_starts(seasons, parts)
        total_0 = sums_in[0]
        for c, fields in zip(chunks, field_refs):
            places = [i for i in new if cuts[c] <= i < cuts[c + 1]]
            for start, field in zip(starts, fields):
                piece_season = (iota(seasons, width) + lax.rem(start, SEASONS)).astype(F32)
                for n, i in enumerate(places):
                    piece = field[n]
                    if 0 <= i < half:
                        total_0 += fold(piece * piece)
                    seen = piece_season >= SEASONS - count_row(i)
                    high, low = halves(jnp.where(seen, piece, 0.0))
                    xh[x_at[i], pl.ds(start, seasons), :] = high
                    xl[x_at[i], pl.ds(start, seasons), :] = low
        if outer:
            for i, n in ((-1, 0), (-2, 1)):
                xh[x_at[i]], xl[x_at[i]] = halves(edge_ref[n * ORDER : (n + 1) * ORDER, :])
        sums_out[0] = total_0

        def space(i, high, low, at):
            if i >= 0:
                hs = jnp.concatenate([high[at[i + d]] for d in (-1, 0, 1)], axis=1)
                ls = jnp.concatenate([low[at[i + d]] for d in (-1, 0, 1)], axis=1)
                both = dot(hs, w2_ref[i], NT)
                return both[:, :width] + both[:, width:] + dot(ls, w2_ref[i, :width, :], NT)
            near = w2_ref[0, :width, :width]
            total = dot(high[at[0]], near, NN)
            total += dot(high[at[0]], w2_ref[0, width:, :width], NN)
            total += dot(low[at[0]], near, NN)
            for n, j in enumerate((-1, -2)):
                begin = 2 * ORDER + n * width
                wh, wl = halves(edge_ref[begin : begin + width, :])
                total += dot(high[at[j]], wh, NT) + dot(high[at[j]], wl, NT)
                total += dot(low[at[j]], wh, NT)
            return total

        def mix(parts_of):
            zh, zl = halves(jnp.concatenate(parts_of, axis=1))
            lhs = jnp.concatenate([rh_ref[...], rh_ref[...], rl_ref[...]], axis=1)
            return dot(lhs, jnp.concatenate([zh, zl, zh], axis=0), NN)

        def hand_out(n, value):
            pick[n] = value
            mine[n] = pick[n, pl.ds(starts[0], seasons), :]
            theirs[n] = pick[n, pl.ds(starts[1], seasons), :]

        total_1, total_2, total_3 = sums_in[1], sums_in[2], sums_in[3]
        for group in runs(ones, 4):
            mixed = mix([space(i, xh, xl, x_at) for i in group])
            for n, i in enumerate(group):
                one = masked(i, mixed[:, n * width : (n + 1) * width])
                oh[one_at[i]], ol[one_at[i]] = halves(one)
                if 0 <= i < half:
                    x = xh[x_at[i]].astype(F32) + xl[x_at[i]].astype(F32)
                    total_1 += fold(x * one)
                    total_2 += fold(one * one)
                    hand_out(inner_ones.index(i), one)
        sums_out[1] = total_1
        sums_out[2] = total_2
        for group in runs(twos, 4):
            mixed = mix([space(i, oh, ol, one_at) for i in group])
            for n, i in enumerate(group):
                two = masked(i, mixed[:, n * width : (n + 1) * width])
                one = oh[one_at[i]].astype(F32) + ol[one_at[i]].astype(F32)
                total_3 += fold(one * two)
                hand_out(len(inner_ones) + twos.index(i), two)
        sums_out[3] = total_3
        if not last:
            for n, i in enumerate(keep_x):
                keep_xh[n] = xh[x_at[i]]
                keep_xl[n] = xl[x_at[i]]
            for n, i in enumerate(keep_1):
                keep_1h[n] = oh[one_at[i]]
                keep_1l[n] = ol[one_at[i]]

    tile = (ORDER, width)
    count = len(inner_ones) + len(twos)
    outs = [jax.ShapeDtypeStruct((4, 8, width), F32)]
    outs += [jax.ShapeDtypeStruct((count, seasons, width), F32)] * 2
    if not last:
        outs += [jax.ShapeDtypeStruct((len(keep_x),) + tile, BF16)] * 2
        outs += [jax.ShapeDtypeStruct((len(keep_1),) + tile, BF16)] * 2
    scratch = [VMEM((len(x_at),) + tile, BF16)] * 2 + [VMEM((len(one_at),) + tile, BF16)] * 2
    scratch += [VMEM((count,) + tile, F32)]
    return kernel, outs, scratch


def run_stage(plan, cuts, m, blocks, parts, seasons, width, operands):
    kernel, outs, scratch = make_stage(plan, cuts, m, blocks, parts, seasons, width)
    return pl.pallas_call(
        kernel,
        in_specs=[pl.BlockSpec(memory_space=VMEM)] * len(operands),
        out_shape=outs,
        scratch_shapes=scratch,
        compiler_params=pltpu.CompilerParams(vmem_limit_bytes=24 << 20),
        name="stage",
    )(*operands)


def finish_kernel(plan, blocks, gathered_ref, x_ref, *refs):
    count = len(plan)
    mine, theirs = refs[:count], refs[count : 2 * count]
    x_out, r_out = refs[2 * count :]
    seasons = x_ref.shape[0] // blocks
    half = blocks // 2
    me = lax.axis_index("var")

    def total(v):
        return jnp.sum(v, axis=1, keepdims=True)

    tuples = [gathered_ref[j] for j in range(gathered_ref.shape[0])]
    top = functools.reduce(jnp.maximum, [t[4:5] for t in tuples])
    sums = [0.0, 0.0, 0.0, 0.0]
    for t in tuples:
        ratio = t[4:5] / top
        factor = jnp.ones_like(ratio)
        for n in range(4):
            sums[n] = sums[n] + t[n : n + 1] * factor
            factor = factor * ratio
    m0, m1, m2, m3 = [total(v) for v in sums]
    scale = (top * tuples[0][5:6])[:, :1]

    first = NUGGET * m0 + scale * m1
    alpha = m0 / first
    lead = alpha * scale
    mean = m1 / m0
    fresh = lead * lead * (m2 - mean * m1)
    c = lead * mean + fresh / m0
    dd = c * c * m0 - 2.0 * c * lead * m1 + lead * lead * m2
    dkd = c * c * m1 - 2.0 * c * lead * m2 + lead * lead * m3
    alpha_2 = fresh / (NUGGET * dd + scale * dkd)
    x_0 = alpha + alpha_2 * c
    r_0 = lead * mean - NUGGET * alpha_2 * c
    x_1 = -alpha_2 * lead
    r_1 = NUGGET * alpha_2 * lead - lead - alpha_2 * scale * c
    r_2 = alpha_2 * scale * lead

    one_at, two_at = {}, {}
    for m, (_, ones, twos, _, _) in enumerate(plan):
        inner = in_half(ones, half)
        one_at.update({i: (m, n) for n, i in enumerate(inner)})
        two_at.update({i: (m, len(inner) + n) for n, i in enumerate(twos)})
    for half_id, held, t in ((me, mine, tuples[0]), (1 - me, theirs, tuples[1])):
        ratio = (t[4:5] / top)[:, :1]
        x_1h, r_1h, r_2h = x_1 * ratio, r_1 * ratio, r_2 * ratio * ratio
        for i in range(half):
            rows = pl.ds(block_at(half_id, i, blocks), seasons, stride=blocks)
            x = x_ref[rows, :]
            m, n = one_at[i]
            one = held[m][n]
            m, n = two_at[i]
            two = held[m][n]
            x_out[rows, :] = x_0 * x + x_1h * one
            r_out[rows, :] = r_0 * x + r_1h * one + r_2h * two


def finish(plan, blocks, gathered, x, mine, theirs):
    return pl.pallas_call(
        functools.partial(finish_kernel, plan, blocks),
        out_shape=[jax.ShapeDtypeStruct(x.shape, F32)] * 2,
        name="finish",
    )(gathered, x, *mine, *theirs)


def from_group(value, step, swap):
    size = lax.axis_size("season")
    pairs = [
        (((p + step) % size) * VARS + (v + swap) % VARS, p * VARS + v)
        for p in range(size)
        for v in range(VARS)
    ]
    return lax.ppermute(value, ("season", "var"), pairs)


def across_edge(value):
    size = lax.axis_size("space")
    pairs = []
    for i in range(1, size * VARS - 1, 2):
        pairs += [(i, i + 1), (i + 1, i)]
    return lax.ppermute(value, ("space", "var"), pairs)


def gather_tiles(value):
    have = jnp.concatenate([value, from_group(value, 0, 1)], axis=0)
    size = lax.axis_size("space")
    if size & (size - 1):
        me = lax.axis_index("space")
        all_tiles = lax.all_gather(have, "space", axis=0, tiled=True)
        return jnp.roll(all_tiles, -me * VARS, axis=0)
    hop = 1
    while hop < size:
        other = lax.ppermute(have, "space", [(i, i ^ hop) for i in range(size)])
        have = jnp.concatenate([have, other], axis=0)
        hop *= 2
    return have


def body(right_side, spatial, columns, counts, season_cov):
    del columns
    seasons = right_side.shape[0]
    blocks, _, width, _ = spatial.shape
    parts = lax.axis_size("season")
    half = blocks // 2
    cuts = (0,) + CUTS + (half + 2,)
    plan = make_plan(cuts, half)

    x = right_side.reshape(seasons * blocks, width)
    count_rows = jnp.broadcast_to(counts.astype(F32)[:, None], (blocks, width))

    chunks = []
    for first, last in zip(cuts[:-1], cuts[1:]):
        same, other = pack(x, first, last, blocks)
        chunks.append(
            [
                from_group(other if w else same, d, w) if d or w else same
                for d in range(parts)
                for w in range(VARS)
            ]
        )
    w2, rh, rl, scale = prepare(
        spatial, season_cov.transpose(0, 1, 3, 2).reshape(SEASONS * VARS * VARS, SEASONS)
    )
    outer = across_edge(edge(spatial, count_rows, chunks[0], parts))

    sums = jnp.zeros((4, 8, width), F32)
    mine, theirs, kept = [], [], []
    for m, stage in enumerate(STAGES):
        operands = [f for c in stage if c >= 0 for f in chunks[c]]
        operands += [w2, rh, rl, count_rows, sums] + kept + [outer] * (-1 in stage)
        out = run_stage(plan, cuts, m, blocks, parts, seasons, width, operands)
        sums, kept = out[0], list(out[3:])
        mine.append(out[1])
        theirs.append(from_group(out[2], 0, 1))
    tile = jnp.concatenate([jnp.sum(sums, axis=1), scale[4:]], axis=0)[None]
    gathered = gather_tiles(tile)
    x_out, r_out = finish(plan, blocks, gathered, x, mine, theirs)
    return x_out.reshape(right_side.shape), r_out.reshape(right_side.shape)


def solution(mesh):
    field = P("season", "var", ("groups", "space"))
    return jax.shard_map(
        body,
        mesh=mesh,
        in_specs=(
            field,
            P(("groups", "space"), None, None, None),
            P(("groups", "space"), None),
            P(("groups", "space")),
            P(),
        ),
        out_specs=(field, field),
        check_vma=False,
    )
```

```python
import functools

import jax
import jax.numpy as jnp
from jax import lax
from jax.experimental import pallas as pl
from jax.experimental.pallas import tpu as pltpu
from jax.sharding import PartitionSpec as P

SEASONS = 64
VARS = 2
ORDER = SEASONS * VARS
REACH = 1
NUGGET = 10.5
LIMIT = 16 << 20
COST = pl.CostEstimate(flops=1, bytes_accessed=1, transcendentals=0)
CUTS = (6,)
STAGES = ((0, -1), (1,))

F32 = jnp.float32
BF16 = jnp.bfloat16
NT = (((1,), (1,)), ((), ()))
NN = (((1,), (0,)), ((), ()))
VMEM = pltpu.VMEM


def dot(a, b, dims):
    return lax.dot_general(a, b, dims, preferred_element_type=F32)


def halves(x):
    high = x.astype(BF16)
    return high, (x - high.astype(F32)).astype(BF16)


def fold(x):
    return jnp.sum(x.reshape(x.shape[0] // 8, 8, x.shape[1]), axis=0)


def block_at(half_id, m, blocks):
    return m + half_id * (blocks - 1 - 2 * m)


def pack_kernel(cuts, blocks, x_ref, same_ref, other_ref, *chunk_refs):
    me = lax.axis_index("var")
    seasons = x_ref.shape[0] // blocks
    for c in range(len(cuts) - 1):
        for m in range(cuts[c], cuts[c + 1]):
            for n, (half_id, ref) in enumerate(((me, same_ref), (1 - me, other_ref))):
                value = x_ref[pl.ds(block_at(half_id, m, blocks), seasons, stride=blocks), :]
                ref[m] = value
                chunk_refs[2 * c + n][m - cuts[c]] = value


def pack(x, cuts, blocks):
    seasons, width = x.shape[0] // blocks, x.shape[1]
    counts = [cuts[-1]] + [last - first for first, last in zip(cuts[:-1], cuts[1:])]
    shapes = [(count, seasons, width) for count in counts for _ in range(2)]
    return pl.pallas_call(
        functools.partial(pack_kernel, cuts, blocks),
        in_specs=[pl.BlockSpec(memory_space=VMEM)],
        out_specs=[pl.BlockSpec(memory_space=VMEM)] * len(shapes),
        out_shape=[jax.ShapeDtypeStruct(shape, F32) for shape in shapes],
        compiler_params=pltpu.CompilerParams(vmem_limit_bytes=LIMIT),
        cost_estimate=COST,
        name="pack",
    )(x)


def prepare_kernel(blocks, w_ref, r_ref, w2_ref, rh_ref, rl_ref, scale_ref):
    me = lax.axis_index("var")
    count, width = w2_ref.shape[0], w_ref.shape[2]
    top = jnp.zeros((8, width), F32)
    for m in range(count):
        row = block_at(me, m, blocks)
        for place, slot in enumerate((1 + me, 0, 2 - me)):
            w = w_ref[row, slot]
            high, low = halves(w)
            lanes = slice(place * width, (place + 1) * width)
            w2_ref[m, :width, lanes] = high
            w2_ref[m, width:, lanes] = low
            top = jnp.maximum(top, jnp.max(jnp.abs(w).reshape(-1, 8, width), axis=0))
    r = jnp.concatenate(
        [
            jnp.concatenate(
                [r_ref[pl.ds(VARS * v + w, SEASONS, stride=VARS * VARS), :] for w in range(VARS)],
                axis=1,
            )
            for v in range(VARS)
        ],
        axis=0,
    )
    space_top = jnp.max(jnp.max(top, axis=0, keepdims=True), axis=1, keepdims=True)
    season_top = jnp.max(jnp.max(jnp.abs(r), axis=0, keepdims=True), axis=1, keepdims=True)
    space_top = jnp.where(space_top > 0, space_top, 1.0)
    season_top = jnp.where(season_top > 0, season_top, 1.0)
    high, low = halves(r / season_top / space_top)
    rh_ref[...] = high
    rl_ref[...] = low
    rows = lax.broadcasted_iota(jnp.int32, scale_ref.shape, 0)
    scale_ref[...] = jnp.where(rows == 4, space_top, jnp.where(rows == 5, season_top, 0.0))


def prepare(spatial, season):
    blocks, slots, width, _ = spatial.shape
    count = blocks // 2 + 1
    return pl.pallas_call(
        functools.partial(prepare_kernel, blocks),
        in_specs=[pl.BlockSpec(memory_space=VMEM)] * 2,
        out_specs=[pl.BlockSpec(memory_space=VMEM)] * 4,
        out_shape=[
            jax.ShapeDtypeStruct((count, 2 * width, slots * width), BF16),
            jax.ShapeDtypeStruct((ORDER, ORDER), BF16),
            jax.ShapeDtypeStruct((ORDER, ORDER), BF16),
            jax.ShapeDtypeStruct((8, width), F32),
        ],
        compiler_params=pltpu.CompilerParams(vmem_limit_bytes=LIMIT),
        cost_estimate=COST,
        name="prepare",
    )(spatial, season)


def row_starts(seasons, parts):
    me_season, me_var = lax.axis_index("season"), lax.axis_index("var")
    return [
        pl.multiple_of(
            lax.rem(me_var + w, VARS) * SEASONS + lax.rem(me_season + d, parts) * seasons, seasons
        )
        for d in range(parts)
        for w in range(VARS)
    ]


def iota(rows, width):
    return lax.broadcasted_iota(jnp.int32, (rows, width), 0)


def space_product(high, low, w2):
    width = w2.shape[0] // 2
    both = dot(high, w2, NT)
    return both[:, :width] + both[:, width:] + dot(low, w2[:width], NT)


def edge_kernel(blocks, parts, w2_ref, count_ref, *refs):
    *fields, out_ref, held = refs
    me = lax.axis_index("var")
    seasons, width = fields[0].shape[1:]
    for start, field in zip(row_starts(seasons, parts), fields):
        season = (iota(seasons, width) + lax.rem(start, SEASONS)).astype(F32)
        for m in range(2):
            seen = season >= SEASONS - count_ref[pl.ds(block_at(me, m, blocks), 1), :]
            held[m, pl.ds(start, seasons), :] = jnp.where(seen, field[m], 0.0)
    high, low = halves(jnp.concatenate([held[0], held[1]], axis=1))
    out_ref[:ORDER, :] = held[0]
    out_ref[ORDER : 2 * ORDER, :] = space_product(high, low, w2_ref[0, :, width:])
    out_ref[2 * ORDER :, :] = jnp.broadcast_to(
        count_ref[pl.ds(block_at(me, 0, blocks), 1), :], (8, width)
    )


def edge(w2, count_rows, fields, parts):
    blocks, width = count_rows.shape
    whole = [pl.BlockSpec(memory_space=VMEM)]
    return pl.pallas_call(
        functools.partial(edge_kernel, blocks, parts),
        in_specs=whole * (2 + len(fields)),
        out_specs=pl.BlockSpec(memory_space=VMEM),
        out_shape=jax.ShapeDtypeStruct((2 * ORDER + 8, width), F32),
        scratch_shapes=[VMEM((2, ORDER, width), F32)],
        compiler_params=pltpu.CompilerParams(vmem_limit_bytes=LIMIT),
        cost_estimate=COST,
        name="edge",
    )(w2, count_rows, *fields)


def make_plan(cuts, half):
    plan = []
    have_x, have_1, have_2 = set(), set(), set()
    for chunks in STAGES:
        new = []
        for c in chunks:
            new += [-1] if c < 0 else list(range(cuts[c], cuts[c + 1]))
        have_x |= set(new)
        ones = [
            i for i in range(-1, half + 1) if i not in have_1 and {max(i - 1, -1), i, i + 1} <= have_x
        ]
        have_1 |= set(ones)
        twos = [i for i in range(half) if i not in have_2 and {i - 1, i, i + 1} <= have_1]
        have_2 |= set(twos)
        later_1 = [i for i in range(-1, half + 1) if i not in have_1]
        later_2 = [i for i in range(half) if i not in have_2]
        keep_x = sorted({i + d for i in later_1 for d in (-1, 0, 1)} & have_x)
        keep_1 = sorted({i + d for i in later_2 for d in (-1, 0, 1)} & have_1)
        plan.append((new, ones, twos, keep_x, keep_1))
    return plan


def in_half(ids, half):
    return [i for i in ids if 0 <= i < half]


def runs(ids, most):
    groups = []
    for i in ids:
        if groups and len(groups[-1]) < most:
            groups[-1].append(i)
        else:
            groups.append([i])
    return groups


def make_stage(plan, cuts, m, blocks, parts, seasons, width):
    half = blocks // 2
    slots = parts * VARS
    new, ones, twos, keep_x, keep_1 = plan[m]
    first, last = m == 0, m == len(plan) - 1
    chunks = [c for c in STAGES[m] if c >= 0]
    outer = -1 in STAGES[m]
    old_x, old_1 = ([], []) if first else (plan[m - 1][3], plan[m - 1][4])
    x_at = {i: n for n, i in enumerate(list(old_x) + list(new))}
    one_at = {i: n for n, i in enumerate(list(old_1) + list(ones))}
    inner_ones = in_half(ones, half)

    def kernel(*refs):
        refs = list(refs)

        def take(n):
            out = refs[:n]
            del refs[:n]
            return out

        near_refs = take(VARS)
        far_refs = [take(slots - VARS) for _ in chunks]
        w2_ref, rh_ref, rl_ref, count_ref, sums_in = take(5)
        if not first:
            old_xh, old_xl, old_1h, old_1l = take(4)
        if outer:
            (edge_ref,) = take(1)
        sums_out, mine, theirs = take(3)
        if not last:
            keep_xh, keep_xl, keep_1h, keep_1l = take(4)
        xh, xl, oh, ol, pick = take(5)
        me = lax.axis_index("var")

        def count_row(i):
            if i == -1:
                return edge_ref[2 * ORDER : 2 * ORDER + 1, :]
            return count_ref[pl.ds(block_at(me, i, blocks), 1), :]

        season = lax.rem(iota(ORDER, width), SEASONS).astype(F32)

        def masked(i, value):
            return jnp.where(season >= SEASONS - count_row(i), value, 0.0)

        for n in range(len(old_x)):
            xh[n] = old_xh[n]
            xl[n] = old_xl[n]
        for n in range(len(old_1)):
            oh[n] = old_1h[n]
            ol[n] = old_1l[n]

        starts = row_starts(seasons, parts)
        total_0 = sums_in[0]
        for c, fars in zip(chunks, far_refs):
            places = [i for i in new if cuts[c] <= i < cuts[c + 1]]
            for k, start in enumerate(starts):
                piece_season = (iota(seasons, width) + lax.rem(start, SEASONS)).astype(F32)
                for i in places:
                    piece = near_refs[k][i] if k < VARS else fars[k - VARS][i - cuts[c]]
                    if 0 <= i < half:
                        total_0 += fold(piece * piece)
                    seen = piece_season >= SEASONS - count_row(i)
                    high, low = halves(jnp.where(seen, piece, 0.0))
                    xh[x_at[i], pl.ds(start, seasons), :] = high
                    xl[x_at[i], pl.ds(start, seasons), :] = low
        if outer:
            xh[x_at[-1]], xl[x_at[-1]] = halves(edge_ref[:ORDER, :])
        sums_out[0] = total_0

        def space(i, high, low, at):
            if i >= 0:
                hs = jnp.concatenate([high[at[i + d]] for d in (-1, 0, 1)], axis=1)
                ls = jnp.concatenate([low[at[i + d]] for d in (-1, 0, 1)], axis=1)
                return space_product(hs, ls, w2_ref[i])
            near = w2_ref[0, :width, :width]
            total = edge_ref[ORDER : 2 * ORDER, :] + dot(high[at[0]], near, NN)
            total += dot(high[at[0]], w2_ref[0, width:, :width], NN)
            return total + dot(low[at[0]], near, NN)

        def mix(parts_of):
            zh, zl = halves(jnp.concatenate(parts_of, axis=1))
            lhs = jnp.concatenate([rh_ref[...], rh_ref[...], rl_ref[...]], axis=1)
            return dot(lhs, jnp.concatenate([zh, zl, zh], axis=0), NN)

        def hand_out(n, value):
            pick[n] = value
            mine[n] = pick[n, pl.ds(starts[0], seasons), :]
            theirs[n] = pick[n, pl.ds(starts[1], seasons), :]

        total_1, total_2, total_3 = sums_in[1], sums_in[2], sums_in[3]
        for group in runs(ones, 4):
            mixed = mix([space(i, xh, xl, x_at) for i in group])
            for n, i in enumerate(group):
                one = masked(i, mixed[:, n * width : (n + 1) * width])
                oh[one_at[i]], ol[one_at[i]] = halves(one)
                if 0 <= i < half:
                    x = xh[x_at[i]].astype(F32) + xl[x_at[i]].astype(F32)
                    total_1 += fold(x * one)
                    total_2 += fold(one * one)
                    hand_out(inner_ones.index(i), one)
        sums_out[1] = total_1
        sums_out[2] = total_2
        for group in runs(twos, 4):
            mixed = mix([space(i, oh, ol, one_at) for i in group])
            for n, i in enumerate(group):
                two = masked(i, mixed[:, n * width : (n + 1) * width])
                one = oh[one_at[i]].astype(F32) + ol[one_at[i]].astype(F32)
                total_3 += fold(one * two)
                hand_out(len(inner_ones) + twos.index(i), two)
        sums_out[3] = total_3
        if not last:
            for n, i in enumerate(keep_x):
                keep_xh[n] = xh[x_at[i]]
                keep_xl[n] = xl[x_at[i]]
            for n, i in enumerate(keep_1):
                keep_1h[n] = oh[one_at[i]]
                keep_1l[n] = ol[one_at[i]]

    tile = (ORDER, width)
    count = len(inner_ones) + len(twos)
    outs = [jax.ShapeDtypeStruct((4, 8, width), F32)]
    outs += [jax.ShapeDtypeStruct((count, seasons, width), F32)] * 2
    if not last:
        outs += [jax.ShapeDtypeStruct((len(keep_x),) + tile, BF16)] * 2
        outs += [jax.ShapeDtypeStruct((len(keep_1),) + tile, BF16)] * 2
    scratch = [VMEM((len(x_at),) + tile, BF16)] * 2 + [VMEM((len(one_at),) + tile, BF16)] * 2
    scratch += [VMEM((count,) + tile, F32)]
    return kernel, outs, scratch


def run_stage(plan, cuts, m, blocks, parts, seasons, width, operands):
    kernel, outs, scratch = make_stage(plan, cuts, m, blocks, parts, seasons, width)
    return pl.pallas_call(
        kernel,
        in_specs=[pl.BlockSpec(memory_space=VMEM)] * len(operands),
        out_shape=outs,
        scratch_shapes=scratch,
        compiler_params=pltpu.CompilerParams(vmem_limit_bytes=LIMIT),
        cost_estimate=COST,
        name="stage",
    )(*operands)


def finish_kernel(plan, blocks, tiles, *refs):
    refs = list(refs)
    count = len(plan)
    gathered, refs = refs[:tiles], refs[tiles:]
    fields, refs = refs[:2], refs[2:]
    mine, theirs = refs[:count], refs[count : 2 * count]
    x_out, r_out, x_held, r_held, sems = refs[2 * count :]
    half = blocks // 2
    me = lax.axis_index("var")

    def total(v):
        return jnp.sum(v, axis=1, keepdims=True)

    tuples = [ref[j] for ref in gathered for j in range(ref.shape[0])]
    top = functools.reduce(jnp.maximum, [t[4:5] for t in tuples])
    sums = [0.0, 0.0, 0.0, 0.0]
    for t in tuples:
        ratio = t[4:5] / top
        factor = jnp.ones_like(ratio)
        for n in range(4):
            sums[n] = sums[n] + t[n : n + 1] * factor
            factor = factor * ratio
    m0, m1, m2, m3 = [total(v) for v in sums]
    scale = (top * tuples[0][5:6])[:, :1]

    first = NUGGET * m0 + scale * m1
    alpha = m0 / first
    lead = alpha * scale
    mean = m1 / m0
    fresh = lead * lead * (m2 - mean * m1)
    c = lead * mean + fresh / m0
    dd = c * c * m0 - 2.0 * c * lead * m1 + lead * lead * m2
    dkd = c * c * m1 - 2.0 * c * lead * m2 + lead * lead * m3
    alpha_2 = fresh / (NUGGET * dd + scale * dkd)
    x_0 = alpha + alpha_2 * c
    r_0 = lead * mean - NUGGET * alpha_2 * c
    x_1 = -alpha_2 * lead
    r_1 = NUGGET * alpha_2 * lead - lead - alpha_2 * scale * c
    r_2 = alpha_2 * scale * lead

    one_at, two_at = {}, {}
    for m, (_, ones, twos, _, _) in enumerate(plan):
        inner = in_half(ones, half)
        one_at.update({i: (m, n) for n, i in enumerate(inner)})
        two_at.update({i: (m, len(inner) + n) for n, i in enumerate(twos)})
    copies = []
    for side, (half_id, held, t) in enumerate(((me, mine, tuples[0]), (1 - me, theirs, tuples[1]))):
        ratio = (t[4:5] / top)[:, :1]
        x_1h, r_1h, r_2h = x_1 * ratio, r_1 * ratio, r_2 * ratio * ratio
        for i in range(half):
            x = fields[side][i]
            m, n = one_at[i]
            one = held[m][n]
            m, n = two_at[i]
            two = held[m][n]
            at = side * half + i
            x_held[at] = x_0 * x + x_1h * one
            r_held[at] = r_0 * x + r_1h * one + r_2h * two
            row = block_at(half_id, i, blocks)
            for n, (source, target) in enumerate(((x_held, x_out), (r_held, r_out))):
                copy = pltpu.make_async_copy(
                    source.at[at], target.at[:, row, 0, :], sems.at[n, at]
                )
                copy.start()
                copies.append(copy)
    for copy in copies:
        copy.wait()


def finish(plan, shape, gathered, packs, mine, theirs):
    seasons, blocks, _, width = shape
    operands = [*gathered, *packs, *mine, *theirs]
    return pl.pallas_call(
        functools.partial(finish_kernel, plan, blocks, len(gathered)),
        in_specs=[pl.BlockSpec(memory_space=VMEM)] * len(operands),
        out_specs=[pl.BlockSpec(memory_space=pltpu.HBM)] * 2,
        out_shape=[jax.ShapeDtypeStruct(shape, F32)] * 2,
        scratch_shapes=[VMEM((blocks, seasons, width), F32)] * 2
        + [pltpu.SemaphoreType.DMA((2, blocks))],
        compiler_params=pltpu.CompilerParams(vmem_limit_bytes=LIMIT),
        cost_estimate=COST,
        name="finish",
    )(*operands)


def from_group(value, step, swap):
    size = lax.axis_size("season")
    pairs = [
        (((p + step) % size) * VARS + (v + swap) % VARS, p * VARS + v)
        for p in range(size)
        for v in range(VARS)
    ]
    return lax.ppermute(value, ("season", "var"), pairs)


def across_edge(value):
    size = lax.axis_size("space")
    pairs = []
    for i in range(1, size * VARS - 1, 2):
        pairs += [(i, i + 1), (i + 1, i)]
    return lax.ppermute(value, ("space", "var"), pairs)


def gather_tiles(value):
    found = [value, from_group(value, 0, 1)]
    size = lax.axis_size("space")
    if size & (size - 1):
        me = lax.axis_index("space")
        tiles = lax.all_gather(jnp.concatenate(found, axis=0), "space", axis=0, tiled=True)
        return [jnp.roll(tiles, -me * VARS, axis=0)]
    hop = 1
    while hop < size:
        have = jnp.concatenate(found, axis=0)
        found.append(lax.ppermute(have, "space", [(i, i ^ hop) for i in range(size)]))
        hop *= 2
    return found


def body(right_side, spatial, columns, counts, season_cov):
    del columns
    seasons = right_side.shape[0]
    blocks, _, width, _ = spatial.shape
    parts = lax.axis_size("season")
    half = blocks // 2
    cuts = (0,) + CUTS + (half + 2,)
    plan = make_plan(cuts, half)

    x = right_side.reshape(seasons * blocks, width)
    count_rows = jnp.broadcast_to(counts.astype(F32)[:, None], (blocks, width))

    same, other, *packs = pack(x, cuts, blocks)
    close = [same, from_group(other, 0, 1)]
    chunks = [
        [from_group(pair[w], d, w) for d in range(1, parts) for w in range(VARS)]
        for pair in zip(packs[0::2], packs[1::2])
    ]
    w2, rh, rl, scale = prepare(
        spatial, season_cov.transpose(0, 1, 3, 2).reshape(SEASONS * VARS * VARS, SEASONS)
    )
    outer = across_edge(edge(w2, count_rows, close + chunks[0], parts))

    sums = jnp.zeros((4, 8, width), F32)
    mine, theirs, kept = [], [], []
    for m, stage in enumerate(STAGES):
        operands = close + [f for c in stage if c >= 0 for f in chunks[c]]
        operands += [w2, rh, rl, count_rows, sums] + kept + [outer] * (-1 in stage)
        out = run_stage(plan, cuts, m, blocks, parts, seasons, width, operands)
        sums, kept = out[0], list(out[3:])
        mine.append(out[1])
        theirs.append(from_group(out[2], 0, 1))
    tile = jnp.concatenate([jnp.sum(sums, axis=1), scale[4:]], axis=0)[None]
    gathered = gather_tiles(tile)
    x_out, r_out = finish(plan, (seasons, blocks, 1, width), gathered, [same, other], mine, theirs)
    return x_out.reshape(right_side.shape), r_out.reshape(right_side.shape)


def solution(mesh):
    field = P("season", "var", ("groups", "space"))
    return jax.shard_map(
        body,
        mesh=mesh,
        in_specs=(
            field,
            P(("groups", "space"), None, None, None),
            P(("groups", "space"), None),
            P(("groups", "space")),
            P(),
        ),
        out_specs=(field, field),
        check_vma=False,
    )
```

```python
import functools

import jax
import jax.numpy as jnp
from jax import lax
from jax.experimental import pallas as pl
from jax.experimental.pallas import tpu as pltpu
from jax.sharding import PartitionSpec as P

SEASONS = 64
VARS = 2
ORDER = SEASONS * VARS
REACH = 1
NUGGET = 10.5
LIMIT = 16 << 20
GROUP = 16
ROOMY = 50 << 20
COST = pl.CostEstimate(flops=1, bytes_accessed=1, transcendentals=0)
CUTS = (3, 14)
STAGES = ((0, 1), (-1, 2))

F32 = jnp.float32
BF16 = jnp.bfloat16
NT = (((1,), (1,)), ((), ()))
NN = (((1,), (0,)), ((), ()))
VMEM = pltpu.VMEM


def dot(a, b, dims):
    return lax.dot_general(a, b, dims, preferred_element_type=F32)


def halves(x):
    high = x.astype(BF16)
    return high, (x - high.astype(F32)).astype(BF16)


def fold(x):
    return jnp.sum(x.reshape(x.shape[0] // 8, 8, x.shape[1]), axis=0)


def block_at(half_id, m, blocks):
    return m + half_id * (blocks - 1 - 2 * m)


def pack_kernel(cuts, blocks, x_ref, same_ref, other_ref, *chunk_refs):
    me = lax.axis_index("var")
    seasons = x_ref.shape[0] // blocks
    for c in range(len(cuts) - 1):
        for m in range(cuts[c], cuts[c + 1]):
            for n, (half_id, ref) in enumerate(((me, same_ref), (1 - me, other_ref))):
                value = x_ref[pl.ds(block_at(half_id, m, blocks), seasons, stride=blocks), :]
                ref[m] = value
                chunk_refs[2 * c + n][m - cuts[c]] = value


def pack(x, cuts, blocks):
    seasons, width = x.shape[0] // blocks, x.shape[1]
    counts = [cuts[-1]] + [last - first for first, last in zip(cuts[:-1], cuts[1:])]
    shapes = [(count, seasons, width) for count in counts for _ in range(2)]
    return pl.pallas_call(
        functools.partial(pack_kernel, cuts, blocks),
        in_specs=[pl.BlockSpec(memory_space=VMEM)],
        out_specs=[pl.BlockSpec(memory_space=VMEM)] * len(shapes),
        out_shape=[jax.ShapeDtypeStruct(shape, F32) for shape in shapes],
        compiler_params=pltpu.CompilerParams(vmem_limit_bytes=LIMIT),
        cost_estimate=COST,
        name="pack",
    )(x)


def prepare_kernel(
    blocks, w_ref, r_ref, w2_ref, rh_ref, rl_ref, scale_ref, held, r_held, sems, r_sem
):
    me = lax.axis_index("var")
    count, width = held.shape[0], held.shape[2]
    r_copy = pltpu.make_async_copy(r_ref, r_held, r_sem)
    copies = []
    for m in range(count):
        row = block_at(me, m, blocks)
        copies.append(
            [
                pltpu.make_async_copy(w_ref.at[row, slot], held.at[m, place], sems.at[m, place])
                for place, slot in enumerate((1 + me, 0, 2 - me))
            ]
        )
    for m, group in enumerate(copies):
        for copy in group:
            copy.start(priority=m % 2)
    r_copy.start(priority=1)
    top = jnp.zeros((8, width), F32)
    for m, group in enumerate(copies):
        for place, copy in enumerate(group):
            copy.wait()
            w = held[m, place]
            high, low = halves(w)
            lanes = slice(place * width, (place + 1) * width)
            w2_ref[m, :width, lanes] = high
            w2_ref[m, width:, lanes] = low
            top = jnp.maximum(top, jnp.max(jnp.abs(w).reshape(-1, 8, width), axis=0))
    r_copy.wait()
    r = jnp.concatenate(
        [
            jnp.concatenate(
                [
                    r_held[pl.ds(VARS * v + w, SEASONS, stride=VARS * VARS), :]
                    for w in range(VARS)
                ],
                axis=1,
            )
            for v in range(VARS)
        ],
        axis=0,
    )
    space_top = jnp.max(jnp.max(top, axis=0, keepdims=True), axis=1, keepdims=True)
    season_top = jnp.max(jnp.max(jnp.abs(r), axis=0, keepdims=True), axis=1, keepdims=True)
    space_top = jnp.where(space_top > 0, space_top, 1.0)
    season_top = jnp.where(season_top > 0, season_top, 1.0)
    high, low = halves(r / season_top / space_top)
    rh_ref[...] = high
    rl_ref[...] = low
    rows = lax.broadcasted_iota(jnp.int32, scale_ref.shape, 0)
    scale_ref[...] = jnp.where(rows == 4, space_top, jnp.where(rows == 5, season_top, 0.0))


def prepare(spatial, season):
    blocks, slots, width, _ = spatial.shape
    count = blocks // 2 + 1
    return pl.pallas_call(
        functools.partial(prepare_kernel, blocks),
        in_specs=[pl.BlockSpec(memory_space=pl.ANY)] * 2,
        out_specs=[pl.BlockSpec(memory_space=VMEM)] * 4,
        out_shape=[
            jax.ShapeDtypeStruct((count, 2 * width, slots * width), BF16),
            jax.ShapeDtypeStruct((ORDER, ORDER), BF16),
            jax.ShapeDtypeStruct((ORDER, ORDER), BF16),
            jax.ShapeDtypeStruct((8, width), F32),
        ],
        scratch_shapes=[
            VMEM((count, slots, width, width), F32),
            VMEM(season.shape, F32),
            pltpu.SemaphoreType.DMA((count, slots)),
            pltpu.SemaphoreType.DMA,
        ],
        compiler_params=pltpu.CompilerParams(vmem_limit_bytes=ROOMY),
        cost_estimate=COST,
        name="prepare",
    )(spatial, season)


def row_starts(seasons, parts):
    me_season, me_var = lax.axis_index("season"), lax.axis_index("var")
    return [
        pl.multiple_of(
            lax.rem(me_var + w, VARS) * SEASONS + lax.rem(me_season + d, parts) * seasons, seasons
        )
        for d in range(parts)
        for w in range(VARS)
    ]


def iota(rows, width):
    return lax.broadcasted_iota(jnp.int32, (rows, width), 0)


def space_product(high, low, w2):
    width = w2.shape[0] // 2
    both = dot(jnp.concatenate([high, low], axis=0), w2, NT)
    return both[:ORDER, :width] + both[:ORDER, width:] + both[ORDER:, :width]


def edge_kernel(blocks, parts, w2_ref, count_ref, *refs):
    *fields, out_ref, held = refs
    me = lax.axis_index("var")
    seasons, width = fields[0].shape[1:]
    for start, field in zip(row_starts(seasons, parts), fields):
        season = (iota(seasons, width) + lax.rem(start, SEASONS)).astype(F32)
        for m in range(2):
            seen = season >= SEASONS - count_ref[pl.ds(block_at(me, m, blocks), 1), :]
            held[m, pl.ds(start, seasons), :] = jnp.where(seen, field[m], 0.0)
    high, low = halves(jnp.concatenate([held[0], held[1]], axis=1))
    out_ref[:ORDER, :] = held[0]
    out_ref[ORDER : 2 * ORDER, :] = space_product(high, low, w2_ref[0, :, width:])
    out_ref[2 * ORDER :, :] = jnp.broadcast_to(
        count_ref[pl.ds(block_at(me, 0, blocks), 1), :], (8, width)
    )


def edge(w2, count_rows, fields, parts):
    blocks, width = count_rows.shape
    whole = [pl.BlockSpec(memory_space=VMEM)]
    return pl.pallas_call(
        functools.partial(edge_kernel, blocks, parts),
        in_specs=whole * (2 + len(fields)),
        out_specs=pl.BlockSpec(memory_space=VMEM),
        out_shape=jax.ShapeDtypeStruct((2 * ORDER + 8, width), F32),
        scratch_shapes=[VMEM((2, ORDER, width), F32)],
        compiler_params=pltpu.CompilerParams(vmem_limit_bytes=LIMIT),
        cost_estimate=COST,
        name="edge",
    )(w2, count_rows, *fields)


def make_plan(cuts, half):
    plan = []
    have_x, have_1, have_2 = set(), set(), set()
    for chunks in STAGES:
        new = []
        for c in chunks:
            new += [-1] if c < 0 else list(range(cuts[c], cuts[c + 1]))
        have_x |= set(new)
        ones = [
            i for i in range(-1, half + 1) if i not in have_1 and {max(i - 1, -1), i, i + 1} <= have_x
        ]
        have_1 |= set(ones)
        twos = [i for i in range(half) if i not in have_2 and {i - 1, i, i + 1} <= have_1]
        have_2 |= set(twos)
        later_1 = [i for i in range(-1, half + 1) if i not in have_1]
        later_2 = [i for i in range(half) if i not in have_2]
        keep_x = sorted({i + d for i in later_1 for d in (-1, 0, 1)} & have_x)
        keep_1 = sorted({i + d for i in later_2 for d in (-1, 0, 1)} & have_1)
        plan.append((new, ones, twos, keep_x, keep_1))
    return plan


def in_half(ids, half):
    return [i for i in ids if 0 <= i < half]


def runs(ids, most):
    groups = []
    for i in ids:
        if groups and len(groups[-1]) < most:
            groups[-1].append(i)
        else:
            groups.append([i])
    return groups


def make_stage(plan, cuts, m, blocks, parts, seasons, width):
    half = blocks // 2
    slots = parts * VARS
    new, ones, twos, keep_x, keep_1 = plan[m]
    first, last = m == 0, m == len(plan) - 1
    chunks = [c for c in STAGES[m] if c >= 0]
    outer = -1 in STAGES[m]
    old_x, old_1 = ([], []) if first else (plan[m - 1][3], plan[m - 1][4])
    x_at = {i: n for n, i in enumerate(list(old_x) + list(new))}
    one_at = {i: n for n, i in enumerate(list(old_1) + list(ones))}
    inner_ones = in_half(ones, half)

    def kernel(*refs):
        refs = list(refs)

        def take(n):
            out = refs[:n]
            del refs[:n]
            return out

        near_refs = take(VARS)
        far_refs = [take(slots - VARS) for _ in chunks]
        w2_ref, rh_ref, rl_ref, count_ref, sums_in = take(5)
        if not first:
            old_xh, old_xl, old_1h, old_1l = take(4)
        if outer:
            (edge_ref,) = take(1)
        sums_out, mine, theirs = take(3)
        if not last:
            keep_xh, keep_xl, keep_1h, keep_1l = take(4)
        xh, xl, oh, ol, pick = take(5)
        me = lax.axis_index("var")

        def count_row(i):
            if i == -1:
                return edge_ref[2 * ORDER : 2 * ORDER + 1, :]
            return count_ref[pl.ds(block_at(me, i, blocks), 1), :]

        season = lax.rem(iota(ORDER, width), SEASONS).astype(F32)

        def masked(i, value):
            return jnp.where(season >= SEASONS - count_row(i), value, 0.0)

        for n in range(len(old_x)):
            xh[n] = old_xh[n]
            xl[n] = old_xl[n]
        for n in range(len(old_1)):
            oh[n] = old_1h[n]
            ol[n] = old_1l[n]

        starts = row_starts(seasons, parts)
        total_0 = sums_in[0]
        for c, fars in zip(chunks, far_refs):
            places = [i for i in new if cuts[c] <= i < cuts[c + 1]]
            for k, start in enumerate(starts):
                piece_season = (iota(seasons, width) + lax.rem(start, SEASONS)).astype(F32)
                for i in places:
                    piece = near_refs[k][i] if k < VARS else fars[k - VARS][i - cuts[c]]
                    if 0 <= i < half:
                        total_0 += fold(piece * piece)
                    seen = piece_season >= SEASONS - count_row(i)
                    high, low = halves(jnp.where(seen, piece, 0.0))
                    xh[x_at[i], pl.ds(start, seasons), :] = high
                    xl[x_at[i], pl.ds(start, seasons), :] = low
        if outer:
            xh[x_at[-1]], xl[x_at[-1]] = halves(edge_ref[:ORDER, :])
        sums_out[0] = total_0

        def space(i, high, low, at):
            if i >= 0:
                hs = jnp.concatenate([high[at[i + d]] for d in (-1, 0, 1)], axis=1)
                ls = jnp.concatenate([low[at[i + d]] for d in (-1, 0, 1)], axis=1)
                return space_product(hs, ls, w2_ref[i])
            near = w2_ref[0, :width, :width]
            total = edge_ref[ORDER : 2 * ORDER, :] + dot(high[at[0]], near, NN)
            total += dot(high[at[0]], w2_ref[0, width:, :width], NN)
            return total + dot(low[at[0]], near, NN)

        rh, rl = rh_ref[...], rl_ref[...]
        mixer = jnp.concatenate(
            [
                jnp.concatenate([rh, rh], axis=1),
                jnp.concatenate([rl, jnp.zeros_like(rl)], axis=1),
            ],
            axis=0,
        )

        def mix(parts_of):
            zh, zl = halves(jnp.concatenate(parts_of, axis=1))
            both = dot(mixer, jnp.concatenate([zh, zl], axis=0), NN)
            return both[:ORDER] + both[ORDER:]

        def hand_out(n, value):
            pick[n] = value
            mine[n] = pick[n, pl.ds(starts[0], seasons), :]
            theirs[n] = pick[n, pl.ds(starts[1], seasons), :]

        total_1, total_2, total_3 = sums_in[1], sums_in[2], sums_in[3]
        for group in runs(ones, GROUP):
            mixed = mix([space(i, xh, xl, x_at) for i in group])
            for n, i in enumerate(group):
                one = masked(i, mixed[:, n * width : (n + 1) * width])
                oh[one_at[i]], ol[one_at[i]] = halves(one)
                if 0 <= i < half:
                    x = xh[x_at[i]].astype(F32) + xl[x_at[i]].astype(F32)
                    total_1 += fold(x * one)
                    total_2 += fold(one * one)
                    hand_out(inner_ones.index(i), one)
        sums_out[1] = total_1
        sums_out[2] = total_2
        for group in runs(twos, GROUP):
            mixed = mix([space(i, oh, ol, one_at) for i in group])
            for n, i in enumerate(group):
                two = masked(i, mixed[:, n * width : (n + 1) * width])
                one = oh[one_at[i]].astype(F32) + ol[one_at[i]].astype(F32)
                total_3 += fold(one * two)
                hand_out(len(inner_ones) + twos.index(i), two)
        sums_out[3] = total_3
        if not last:
            for n, i in enumerate(keep_x):
                keep_xh[n] = xh[x_at[i]]
                keep_xl[n] = xl[x_at[i]]
            for n, i in enumerate(keep_1):
                keep_1h[n] = oh[one_at[i]]
                keep_1l[n] = ol[one_at[i]]

    tile = (ORDER, width)
    count = len(inner_ones) + len(twos)
    outs = [jax.ShapeDtypeStruct((4, 8, width), F32)]
    outs += [jax.ShapeDtypeStruct((count, seasons, width), F32)] * 2
    if not last:
        outs += [jax.ShapeDtypeStruct((len(keep_x),) + tile, BF16)] * 2
        outs += [jax.ShapeDtypeStruct((len(keep_1),) + tile, BF16)] * 2
    scratch = [VMEM((len(x_at),) + tile, BF16)] * 2 + [VMEM((len(one_at),) + tile, BF16)] * 2
    scratch += [VMEM((count,) + tile, F32)]
    return kernel, outs, scratch


def run_stage(plan, cuts, m, blocks, parts, seasons, width, operands):
    kernel, outs, scratch = make_stage(plan, cuts, m, blocks, parts, seasons, width)
    return pl.pallas_call(
        kernel,
        in_specs=[pl.BlockSpec(memory_space=VMEM)] * len(operands),
        out_shape=outs,
        scratch_shapes=scratch,
        compiler_params=pltpu.CompilerParams(vmem_limit_bytes=LIMIT),
        cost_estimate=COST,
        name="stage",
    )(*operands)


def finish_kernel(plan, blocks, tiles, *refs):
    refs = list(refs)
    count = len(plan)
    gathered, refs = refs[:tiles], refs[tiles:]
    fields, refs = refs[:2], refs[2:]
    mine, theirs = refs[:count], refs[count : 2 * count]
    x_out, r_out, x_held, r_held, sems = refs[2 * count :]
    half = blocks // 2
    me = lax.axis_index("var")

    def total(v):
        return jnp.sum(v, axis=1, keepdims=True)

    tuples = [ref[j] for ref in gathered for j in range(ref.shape[0])]
    top = functools.reduce(jnp.maximum, [t[4:5] for t in tuples])
    sums = [0.0, 0.0, 0.0, 0.0]
    for t in tuples:
        ratio = t[4:5] / top
        factor = jnp.ones_like(ratio)
        for n in range(4):
            sums[n] = sums[n] + t[n : n + 1] * factor
            factor = factor * ratio
    m0, m1, m2, m3 = [total(v) for v in sums]
    scale = (top * tuples[0][5:6])[:, :1]

    first = NUGGET * m0 + scale * m1
    alpha = m0 / first
    lead = alpha * scale
    mean = m1 / m0
    fresh = lead * lead * (m2 - mean * m1)
    c = lead * mean + fresh / m0
    dd = c * c * m0 - 2.0 * c * lead * m1 + lead * lead * m2
    dkd = c * c * m1 - 2.0 * c * lead * m2 + lead * lead * m3
    alpha_2 = fresh / (NUGGET * dd + scale * dkd)
    x_0 = alpha + alpha_2 * c
    r_0 = lead * mean - NUGGET * alpha_2 * c
    x_1 = -alpha_2 * lead
    r_1 = NUGGET * alpha_2 * lead - lead - alpha_2 * scale * c
    r_2 = alpha_2 * scale * lead

    one_at, two_at = {}, {}
    for m, (_, ones, twos, _, _) in enumerate(plan):
        inner = in_half(ones, half)
        one_at.update({i: (m, n) for n, i in enumerate(inner)})
        two_at.update({i: (m, len(inner) + n) for n, i in enumerate(twos)})
    copies = []
    for side, (half_id, held, t) in enumerate(((me, mine, tuples[0]), (1 - me, theirs, tuples[1]))):
        ratio = (t[4:5] / top)[:, :1]
        x_1h, r_1h, r_2h = x_1 * ratio, r_1 * ratio, r_2 * ratio * ratio
        for i in range(half):
            x = fields[side][i]
            m, n = one_at[i]
            one = held[m][n]
            m, n = two_at[i]
            two = held[m][n]
            at = side * half + i
            x_held[at] = x_0 * x + x_1h * one
            r_held[at] = r_0 * x + r_1h * one + r_2h * two
            row = block_at(half_id, i, blocks)
            for n, (source, target) in enumerate(((x_held, x_out), (r_held, r_out))):
                copy = pltpu.make_async_copy(
                    source.at[at], target.at[:, row, 0, :], sems.at[n, at]
                )
                copy.start()
                copies.append(copy)
    for copy in copies:
        copy.wait()


def finish(plan, shape, gathered, packs, mine, theirs):
    seasons, blocks, _, width = shape
    operands = [*gathered, *packs, *mine, *theirs]
    return pl.pallas_call(
        functools.partial(finish_kernel, plan, blocks, len(gathered)),
        in_specs=[pl.BlockSpec(memory_space=VMEM)] * len(operands),
        out_specs=[pl.BlockSpec(memory_space=pltpu.HBM)] * 2,
        out_shape=[jax.ShapeDtypeStruct(shape, F32)] * 2,
        scratch_shapes=[VMEM((blocks, seasons, width), F32)] * 2
        + [pltpu.SemaphoreType.DMA((2, blocks))],
        compiler_params=pltpu.CompilerParams(vmem_limit_bytes=LIMIT),
        cost_estimate=COST,
        name="finish",
    )(*operands)


def from_group(value, step, swap):
    size = lax.axis_size("season")
    pairs = [
        (((p + step) % size) * VARS + (v + swap) % VARS, p * VARS + v)
        for p in range(size)
        for v in range(VARS)
    ]
    return lax.ppermute(value, ("season", "var"), pairs)


def across_edge(value):
    size = lax.axis_size("space")
    pairs = []
    for i in range(1, size * VARS - 1, 2):
        pairs += [(i, i + 1), (i + 1, i)]
    return lax.ppermute(value, ("space", "var"), pairs)


def gather_tiles(value):
    found = [value, from_group(value, 0, 1)]
    size = lax.axis_size("space")
    if size & (size - 1):
        me = lax.axis_index("space")
        tiles = lax.all_gather(jnp.concatenate(found, axis=0), "space", axis=0, tiled=True)
        return [jnp.roll(tiles, -me * VARS, axis=0)]
    hop = 1
    while hop < size:
        have = jnp.concatenate(found, axis=0)
        found.append(lax.ppermute(have, "space", [(i, i ^ hop) for i in range(size)]))
        hop *= 2
    return found


def body(right_side, spatial, columns, counts, season_cov):
    del columns
    seasons = right_side.shape[0]
    blocks, _, width, _ = spatial.shape
    parts = lax.axis_size("season")
    half = blocks // 2
    cuts = (0,) + CUTS + (half + 2,)
    plan = make_plan(cuts, half)

    x = right_side.reshape(seasons * blocks, width)
    count_rows = jnp.broadcast_to(counts.astype(F32)[:, None], (blocks, width))

    same, other, *packs = pack(x, cuts, blocks)
    close = [same, from_group(other, 0, 1)]
    chunks = [
        [from_group(pair[w], d, w) for d in range(1, parts) for w in range(VARS)]
        for pair in zip(packs[0::2], packs[1::2])
    ]
    w2, rh, rl, scale = prepare(
        spatial, season_cov.transpose(0, 1, 3, 2).reshape(SEASONS * VARS * VARS, SEASONS)
    )
    outer = across_edge(edge(w2, count_rows, close + chunks[0], parts))

    sums = jnp.zeros((4, 8, width), F32)
    mine, theirs, kept = [], [], []
    for m, stage in enumerate(STAGES):
        operands = close + [f for c in stage if c >= 0 for f in chunks[c]]
        operands += [w2, rh, rl, count_rows, sums] + kept + [outer] * (-1 in stage)
        out = run_stage(plan, cuts, m, blocks, parts, seasons, width, operands)
        sums, kept = out[0], list(out[3:])
        mine.append(out[1])
        theirs.append(from_group(out[2], 0, 1))
    tile = jnp.concatenate([jnp.sum(sums, axis=1), scale[4:]], axis=0)[None]
    gathered = gather_tiles(tile)
    x_out, r_out = finish(plan, (seasons, blocks, 1, width), gathered, [same, other], mine, theirs)
    return x_out.reshape(right_side.shape), r_out.reshape(right_side.shape)


def solution(mesh):
    field = P("season", "var", ("groups", "space"))
    return jax.shard_map(
        body,
        mesh=mesh,
        in_specs=(
            field,
            P(("groups", "space"), None, None, None),
            P(("groups", "space"), None),
            P(("groups", "space")),
            P(),
        ),
        out_specs=(field, field),
        check_vma=False,
    )
```

```python
import functools

import jax
import jax.numpy as jnp
from jax import lax
from jax.experimental import pallas as pl
from jax.experimental.pallas import tpu as pltpu
from jax.sharding import PartitionSpec as P

SEASONS = 64
VARS = 2
ORDER = SEASONS * VARS
REACH = 1
NUGGET = 10.5
LIMIT = 16 << 20
GROUP = 16
ROOMY = 50 << 20
COST = pl.CostEstimate(flops=1, bytes_accessed=1, transcendentals=0)
CUTS = (3, 14)
STAGES = ((0, 1), (-1, 2))

F32 = jnp.float32
BF16 = jnp.bfloat16
NT = (((1,), (1,)), ((), ()))
NN = (((1,), (0,)), ((), ()))
VMEM = pltpu.VMEM


def dot(a, b, dims):
    return lax.dot_general(a, b, dims, preferred_element_type=F32)


def halves(x):
    high = x.astype(BF16)
    return high, (x - high.astype(F32)).astype(BF16)


def fold(x):
    return jnp.sum(x.reshape(x.shape[0] // 8, 8, x.shape[1]), axis=0)


def block_at(half_id, m, blocks):
    return m + half_id * (blocks - 1 - 2 * m)


def pack_kernel(cuts, blocks, x_ref, same_ref, other_ref, *chunk_refs):
    me = lax.axis_index("var")
    seasons = x_ref.shape[0] // blocks
    for c in range(len(cuts) - 1):
        for m in range(cuts[c], cuts[c + 1]):
            for n, (half_id, ref) in enumerate(((me, same_ref), (1 - me, other_ref))):
                value = x_ref[pl.ds(block_at(half_id, m, blocks), seasons, stride=blocks), :]
                ref[m] = value
                chunk_refs[2 * c + n][m - cuts[c]] = value


def pack(x, cuts, blocks):
    seasons, width = x.shape[0] // blocks, x.shape[1]
    counts = [cuts[-1]] + [last - first for first, last in zip(cuts[:-1], cuts[1:])]
    shapes = [(count, seasons, width) for count in counts for _ in range(2)]
    return pl.pallas_call(
        functools.partial(pack_kernel, cuts, blocks),
        in_specs=[pl.BlockSpec(memory_space=VMEM)],
        out_specs=[pl.BlockSpec(memory_space=VMEM)] * len(shapes),
        out_shape=[jax.ShapeDtypeStruct(shape, F32) for shape in shapes],
        compiler_params=pltpu.CompilerParams(vmem_limit_bytes=LIMIT),
        cost_estimate=COST,
        name="pack",
    )(x)


def prepare_kernel(
    blocks, w_ref, r_ref, w2_ref, rh_ref, rl_ref, scale_ref, held, r_held, sems, r_sem
):
    me = lax.axis_index("var")
    count, width = held.shape[0], held.shape[2]
    r_copy = pltpu.make_async_copy(r_ref, r_held, r_sem)
    copies = []
    for m in range(count):
        row = block_at(me, m, blocks)
        copies.append(
            [
                pltpu.make_async_copy(w_ref.at[row, slot], held.at[m, place], sems.at[m, place])
                for place, slot in enumerate((1 + me, 0, 2 - me))
            ]
        )
    for m, group in enumerate(copies):
        for copy in group:
            copy.start(priority=m % 2)
    r_copy.start(priority=1)
    top = jnp.zeros((8, width), F32)
    for m, group in enumerate(copies):
        for place, copy in enumerate(group):
            copy.wait()
            w = held[m, place]
            high, low = halves(w)
            lanes = slice(place * width, (place + 1) * width)
            w2_ref[m, :width, lanes] = high
            w2_ref[m, width:, lanes] = low
            top = jnp.maximum(top, jnp.max(jnp.abs(w).reshape(-1, 8, width), axis=0))
    r_copy.wait()
    r = jnp.concatenate(
        [
            jnp.concatenate(
                [
                    r_held[pl.ds(VARS * v + w, SEASONS, stride=VARS * VARS), :]
                    for w in range(VARS)
                ],
                axis=1,
            )
            for v in range(VARS)
        ],
        axis=0,
    )
    space_top = jnp.max(jnp.max(top, axis=0, keepdims=True), axis=1, keepdims=True)
    season_top = jnp.max(jnp.max(jnp.abs(r), axis=0, keepdims=True), axis=1, keepdims=True)
    space_top = jnp.where(space_top > 0, space_top, 1.0)
    season_top = jnp.where(season_top > 0, season_top, 1.0)
    high, low = halves(r / season_top / space_top)
    rh_ref[...] = high
    rl_ref[...] = low
    rows = lax.broadcasted_iota(jnp.int32, scale_ref.shape, 0)
    scale_ref[...] = jnp.where(rows == 4, space_top, jnp.where(rows == 5, season_top, 0.0))


def prepare(spatial, season):
    blocks, slots, width, _ = spatial.shape
    count = blocks // 2 + 1
    return pl.pallas_call(
        functools.partial(prepare_kernel, blocks),
        in_specs=[pl.BlockSpec(memory_space=pl.ANY)] * 2,
        out_specs=[pl.BlockSpec(memory_space=VMEM)] * 4,
        out_shape=[
            jax.ShapeDtypeStruct((count, 2 * width, slots * width), BF16),
            jax.ShapeDtypeStruct((ORDER, ORDER), BF16),
            jax.ShapeDtypeStruct((ORDER, ORDER), BF16),
            jax.ShapeDtypeStruct((8, width), F32),
        ],
        scratch_shapes=[
            VMEM((count, slots, width, width), F32),
            VMEM(season.shape, F32),
            pltpu.SemaphoreType.DMA((count, slots)),
            pltpu.SemaphoreType.DMA,
        ],
        compiler_params=pltpu.CompilerParams(vmem_limit_bytes=ROOMY),
        cost_estimate=COST,
        name="prepare",
    )(spatial, season)


def row_starts(seasons, parts):
    me_season, me_var = lax.axis_index("season"), lax.axis_index("var")
    return [
        pl.multiple_of(
            lax.rem(me_var + w, VARS) * SEASONS + lax.rem(me_season + d, parts) * seasons, seasons
        )
        for d in range(parts)
        for w in range(VARS)
    ]


def iota(rows, width):
    return lax.broadcasted_iota(jnp.int32, (rows, width), 0)


def space_product(high, low, w2):
    width = w2.shape[0] // 2
    both = dot(jnp.concatenate([high, low], axis=0), w2, NT)
    return both[:ORDER, :width] + both[:ORDER, width:] + both[ORDER:, :width]


def edge_kernel(blocks, parts, w2_ref, count_ref, *refs):
    *fields, out_ref, held = refs
    me = lax.axis_index("var")
    seasons, width = fields[0].shape[1:]
    for start, field in zip(row_starts(seasons, parts), fields):
        season = (iota(seasons, width) + lax.rem(start, SEASONS)).astype(F32)
        for m in range(2):
            seen = season >= SEASONS - count_ref[pl.ds(block_at(me, m, blocks), 1), :]
            held[m, pl.ds(start, seasons), :] = jnp.where(seen, field[m], 0.0)
    high, low = halves(jnp.concatenate([held[0], held[1]], axis=1))
    out_ref[:ORDER, :] = held[0]
    out_ref[ORDER : 2 * ORDER, :] = space_product(high, low, w2_ref[0, :, width:])
    out_ref[2 * ORDER :, :] = jnp.broadcast_to(
        count_ref[pl.ds(block_at(me, 0, blocks), 1), :], (8, width)
    )


def edge(w2, count_rows, fields, parts):
    blocks, width = count_rows.shape
    whole = [pl.BlockSpec(memory_space=VMEM)]
    return pl.pallas_call(
        functools.partial(edge_kernel, blocks, parts),
        in_specs=whole * (2 + len(fields)),
        out_specs=pl.BlockSpec(memory_space=VMEM),
        out_shape=jax.ShapeDtypeStruct((2 * ORDER + 8, width), F32),
        scratch_shapes=[VMEM((2, ORDER, width), F32)],
        compiler_params=pltpu.CompilerParams(vmem_limit_bytes=LIMIT),
        cost_estimate=COST,
        name="edge",
    )(w2, count_rows, *fields)


def make_plan(cuts, half):
    plan = []
    have_x, have_1, have_2 = set(), set(), set()
    for chunks in STAGES:
        new = []
        for c in chunks:
            new += [-1] if c < 0 else list(range(cuts[c], cuts[c + 1]))
        have_x |= set(new)
        ones = [
            i for i in range(-1, half + 1) if i not in have_1 and {max(i - 1, -1), i, i + 1} <= have_x
        ]
        have_1 |= set(ones)
        twos = [i for i in range(half) if i not in have_2 and {i - 1, i, i + 1} <= have_1]
        have_2 |= set(twos)
        later_1 = [i for i in range(-1, half + 1) if i not in have_1]
        later_2 = [i for i in range(half) if i not in have_2]
        keep_x = sorted({i + d for i in later_1 for d in (-1, 0, 1)} & have_x)
        keep_1 = sorted({i + d for i in later_2 for d in (-1, 0, 1)} & have_1)
        plan.append((new, ones, twos, keep_x, keep_1))
    return plan


def in_half(ids, half):
    return [i for i in ids if 0 <= i < half]


def runs(ids, most):
    groups = []
    for i in ids:
        if groups and len(groups[-1]) < most:
            groups[-1].append(i)
        else:
            groups.append([i])
    return groups


def make_stage(plan, cuts, m, blocks, parts, seasons, width):
    half = blocks // 2
    slots = parts * VARS
    new, ones, twos, keep_x, keep_1 = plan[m]
    first, last = m == 0, m == len(plan) - 1
    chunks = [c for c in STAGES[m] if c >= 0]
    outer = -1 in STAGES[m]
    old_x, old_1 = ([], []) if first else (plan[m - 1][3], plan[m - 1][4])
    x_at = {i: n for n, i in enumerate(list(old_x) + list(new))}
    one_at = {i: n for n, i in enumerate(list(old_1) + list(ones))}
    inner_ones = in_half(ones, half)

    def kernel(*refs):
        refs = list(refs)

        def take(n):
            out = refs[:n]
            del refs[:n]
            return out

        near_refs = take(VARS)
        far_refs = [take(slots - VARS) for _ in chunks]
        w2_ref, rh_ref, rl_ref, count_ref, sums_in = take(5)
        if not first:
            old_xh, old_xl, old_1h, old_1l = take(4)
        if outer:
            (edge_ref,) = take(1)
        sums_out, mine, theirs = take(3)
        if not last:
            keep_xh, keep_xl, keep_1h, keep_1l = take(4)
        xh, xl, oh, ol, pick = take(5)
        me = lax.axis_index("var")

        def count_row(i):
            if i == -1:
                return edge_ref[2 * ORDER : 2 * ORDER + 1, :]
            return count_ref[pl.ds(block_at(me, i, blocks), 1), :]

        season = lax.rem(iota(ORDER, width), SEASONS).astype(F32)

        def masked(i, value):
            return jnp.where(season >= SEASONS - count_row(i), value, 0.0)

        for n in range(len(old_x)):
            xh[n] = old_xh[n]
            xl[n] = old_xl[n]
        for n in range(len(old_1)):
            oh[n] = old_1h[n]
            ol[n] = old_1l[n]

        starts = row_starts(seasons, parts)
        total_0 = sums_in[0]
        for c, fars in zip(chunks, far_refs):
            places = [i for i in new if cuts[c] <= i < cuts[c + 1]]
            for k, start in enumerate(starts):
                piece_season = (iota(seasons, width) + lax.rem(start, SEASONS)).astype(F32)
                for i in places:
                    piece = near_refs[k][i] if k < VARS else fars[k - VARS][i - cuts[c]]
                    if 0 <= i < half:
                        total_0 += fold(piece * piece)
                    seen = piece_season >= SEASONS - count_row(i)
                    high, low = halves(jnp.where(seen, piece, 0.0))
                    xh[x_at[i], pl.ds(start, seasons), :] = high
                    xl[x_at[i], pl.ds(start, seasons), :] = low
        if outer:
            xh[x_at[-1]], xl[x_at[-1]] = halves(edge_ref[:ORDER, :])
        sums_out[0] = total_0

        def space(i, high, low, at):
            if i >= 0:
                hs = jnp.concatenate([high[at[i + d]] for d in (-1, 0, 1)], axis=1)
                ls = jnp.concatenate([low[at[i + d]] for d in (-1, 0, 1)], axis=1)
                return space_product(hs, ls, w2_ref[i])
            near = w2_ref[0, :width, :width]
            total = edge_ref[ORDER : 2 * ORDER, :] + dot(high[at[0]], near, NN)
            total += dot(high[at[0]], w2_ref[0, width:, :width], NN)
            return total + dot(low[at[0]], near, NN)

        rh, rl = rh_ref[...], rl_ref[...]
        mixer = jnp.concatenate(
            [
                jnp.concatenate([rh, rh], axis=1),
                jnp.concatenate([rl, jnp.zeros_like(rl)], axis=1),
            ],
            axis=0,
        )

        def mix(parts_of):
            zh, zl = halves(jnp.concatenate(parts_of, axis=1))
            both = dot(mixer, jnp.concatenate([zh, zl], axis=0), NN)
            return both[:ORDER] + both[ORDER:]

        def hand_out(n, value):
            pick[n] = value
            mine[n] = pick[n, pl.ds(starts[0], seasons), :]
            theirs[n] = pick[n, pl.ds(starts[1], seasons), :]

        total_1, total_2, total_3 = sums_in[1], sums_in[2], sums_in[3]
        for group in runs(ones, GROUP):
            mixed = mix([space(i, xh, xl, x_at) for i in group])
            for n, i in enumerate(group):
                one = masked(i, mixed[:, n * width : (n + 1) * width])
                oh[one_at[i]], ol[one_at[i]] = halves(one)
                if 0 <= i < half:
                    x = xh[x_at[i]].astype(F32) + xl[x_at[i]].astype(F32)
                    total_1 += fold(x * one)
                    total_2 += fold(one * one)
                    hand_out(inner_ones.index(i), one)
        sums_out[1] = total_1
        sums_out[2] = total_2
        for group in runs(twos, GROUP):
            mixed = mix([space(i, oh, ol, one_at) for i in group])
            for n, i in enumerate(group):
                two = masked(i, mixed[:, n * width : (n + 1) * width])
                one = oh[one_at[i]].astype(F32) + ol[one_at[i]].astype(F32)
                total_3 += fold(one * two)
                hand_out(len(inner_ones) + twos.index(i), two)
        sums_out[3] = total_3
        if not last:
            for n, i in enumerate(keep_x):
                keep_xh[n] = xh[x_at[i]]
                keep_xl[n] = xl[x_at[i]]
            for n, i in enumerate(keep_1):
                keep_1h[n] = oh[one_at[i]]
                keep_1l[n] = ol[one_at[i]]

    tile = (ORDER, width)
    count = len(inner_ones) + len(twos)
    outs = [jax.ShapeDtypeStruct((4, 8, width), F32)]
    outs += [jax.ShapeDtypeStruct((count, seasons, width), F32)] * 2
    if not last:
        outs += [jax.ShapeDtypeStruct((len(keep_x),) + tile, BF16)] * 2
        outs += [jax.ShapeDtypeStruct((len(keep_1),) + tile, BF16)] * 2
    scratch = [VMEM((len(x_at),) + tile, BF16)] * 2 + [VMEM((len(one_at),) + tile, BF16)] * 2
    scratch += [VMEM((count,) + tile, F32)]
    return kernel, outs, scratch


def run_stage(plan, cuts, m, blocks, parts, seasons, width, operands):
    kernel, outs, scratch = make_stage(plan, cuts, m, blocks, parts, seasons, width)
    return pl.pallas_call(
        kernel,
        in_specs=[pl.BlockSpec(memory_space=VMEM)] * len(operands),
        out_shape=outs,
        scratch_shapes=scratch,
        compiler_params=pltpu.CompilerParams(vmem_limit_bytes=LIMIT),
        cost_estimate=COST,
        name="stage",
    )(*operands)


def finish_kernel(plan, blocks, tiles, *refs):
    refs = list(refs)
    count = len(plan)
    gathered, refs = refs[:tiles], refs[tiles:]
    fields, refs = refs[:2], refs[2:]
    mine, theirs = refs[:count], refs[count : 2 * count]
    x_out, r_out, x_held, r_held, sems = refs[2 * count :]
    half = blocks // 2
    me = lax.axis_index("var")

    def total(v):
        return jnp.sum(v, axis=1, keepdims=True)

    tuples = [ref[j] for ref in gathered for j in range(ref.shape[0])]
    top = functools.reduce(jnp.maximum, [t[4:5] for t in tuples])
    sums = [0.0, 0.0, 0.0, 0.0]
    for t in tuples:
        ratio = t[4:5] / top
        factor = jnp.ones_like(ratio)
        for n in range(4):
            sums[n] = sums[n] + t[n : n + 1] * factor
            factor = factor * ratio
    m0, m1, m2, m3 = [total(v) for v in sums]
    scale = (top * tuples[0][5:6])[:, :1]

    first = NUGGET * m0 + scale * m1
    alpha = m0 / first
    lead = alpha * scale
    mean = m1 / m0
    fresh = lead * lead * (m2 - mean * m1)
    c = lead * mean + fresh / m0
    dd = c * c * m0 - 2.0 * c * lead * m1 + lead * lead * m2
    dkd = c * c * m1 - 2.0 * c * lead * m2 + lead * lead * m3
    alpha_2 = fresh / (NUGGET * dd + scale * dkd)
    x_0 = alpha + alpha_2 * c
    r_0 = lead * mean - NUGGET * alpha_2 * c
    x_1 = -alpha_2 * lead
    r_1 = NUGGET * alpha_2 * lead - lead - alpha_2 * scale * c
    r_2 = alpha_2 * scale * lead

    one_at, two_at = {}, {}
    for m, (_, ones, twos, _, _) in enumerate(plan):
        inner = in_half(ones, half)
        one_at.update({i: (m, n) for n, i in enumerate(inner)})
        two_at.update({i: (m, len(inner) + n) for n, i in enumerate(twos)})
    copies = []
    for side, (half_id, held, t) in enumerate(((me, mine, tuples[0]), (1 - me, theirs, tuples[1]))):
        ratio = (t[4:5] / top)[:, :1]
        x_1h, r_1h, r_2h = x_1 * ratio, r_1 * ratio, r_2 * ratio * ratio
        for i in range(half):
            x = fields[side][i]
            m, n = one_at[i]
            one = held[m][n]
            m, n = two_at[i]
            two = held[m][n]
            at = side * half + i
            x_held[at] = x_0 * x + x_1h * one
            r_held[at] = r_0 * x + r_1h * one + r_2h * two
            row = block_at(half_id, i, blocks)
            for n, (source, target) in enumerate(((x_held, x_out), (r_held, r_out))):
                copy = pltpu.make_async_copy(
                    source.at[at], target.at[:, row, 0, :], sems.at[n, at]
                )
                copy.start()
                copies.append(copy)
    for copy in copies:
        copy.wait()


def finish(plan, shape, gathered, packs, mine, theirs):
    seasons, blocks, _, width = shape
    operands = [*gathered, *packs, *mine, *theirs]
    return pl.pallas_call(
        functools.partial(finish_kernel, plan, blocks, len(gathered)),
        in_specs=[pl.BlockSpec(memory_space=VMEM)] * len(operands),
        out_specs=[pl.BlockSpec(memory_space=pltpu.HBM)] * 2,
        out_shape=[jax.ShapeDtypeStruct(shape, F32)] * 2,
        scratch_shapes=[VMEM((blocks, seasons, width), F32)] * 2
        + [pltpu.SemaphoreType.DMA((2, blocks))],
        compiler_params=pltpu.CompilerParams(vmem_limit_bytes=LIMIT),
        cost_estimate=COST,
        name="finish",
    )(*operands)


def from_group(value, step, swap):
    size = lax.axis_size("season")
    pairs = [
        (((p + step) % size) * VARS + (v + swap) % VARS, p * VARS + v)
        for p in range(size)
        for v in range(VARS)
    ]
    return lax.ppermute(value, ("season", "var"), pairs)


def across_edge(value):
    size = lax.axis_size("space")
    pairs = []
    for i in range(1, size * VARS - 1, 2):
        pairs += [(i, i + 1), (i + 1, i)]
    return lax.ppermute(value, ("space", "var"), pairs)


def gather_tiles(value):
    found = [value, from_group(value, 0, 1)]
    size = lax.axis_size("space")
    if size & (size - 1):
        me = lax.axis_index("space")
        tiles = lax.all_gather(jnp.concatenate(found, axis=0), "space", axis=0, tiled=True)
        return [jnp.roll(tiles, -me * VARS, axis=0)]
    hop = 1
    while hop < size:
        have = jnp.concatenate(found, axis=0)
        pairs = [
            (i * VARS + v, (i ^ hop) * VARS + 1 - v) for i in range(size) for v in range(VARS)
        ]
        found.append(lax.ppermute(have, ("space", "var"), pairs))
        hop *= 2
    return found


def body(right_side, spatial, columns, counts, season_cov):
    del columns
    seasons = right_side.shape[0]
    blocks, _, width, _ = spatial.shape
    parts = lax.axis_size("season")
    half = blocks // 2
    cuts = (0,) + CUTS + (half + 2,)
    plan = make_plan(cuts, half)

    x = right_side.reshape(seasons * blocks, width)
    count_rows = jnp.broadcast_to(counts.astype(F32)[:, None], (blocks, width))

    same, other, *packs = pack(x, cuts, blocks)
    close = [same, from_group(other, 0, 1)]
    chunks = [
        [from_group(pair[w], d, w) for d in range(1, parts) for w in range(VARS)]
        for pair in zip(packs[0::2], packs[1::2])
    ]
    w2, rh, rl, scale = prepare(
        spatial, season_cov.transpose(0, 1, 3, 2).reshape(SEASONS * VARS * VARS, SEASONS)
    )
    outer = across_edge(edge(w2, count_rows, close + chunks[0], parts))

    sums = jnp.zeros((4, 8, width), F32)
    mine, theirs, kept = [], [], []
    for m, stage in enumerate(STAGES):
        operands = close + [f for c in stage if c >= 0 for f in chunks[c]]
        operands += [w2, rh, rl, count_rows, sums] + kept + [outer] * (-1 in stage)
        out = run_stage(plan, cuts, m, blocks, parts, seasons, width, operands)
        sums, kept = out[0], list(out[3:])
        mine.append(out[1])
        theirs.append(from_group(out[2], 0, 1))
    tile = jnp.concatenate([jnp.sum(sums, axis=1), scale[4:]], axis=0)[None]
    gathered = gather_tiles(tile)
    x_out, r_out = finish(plan, (seasons, blocks, 1, width), gathered, [same, other], mine, theirs)
    return x_out.reshape(right_side.shape), r_out.reshape(right_side.shape)


def solution(mesh):
    field = P("season", "var", ("groups", "space"))
    return jax.shard_map(
        body,
        mesh=mesh,
        in_specs=(
            field,
            P(("groups", "space"), None, None, None),
            P(("groups", "space"), None),
            P(("groups", "space")),
            P(),
        ),
        out_specs=(field, field),
        check_vma=False,
    )
```

```python
import functools

import jax
import jax.numpy as jnp
from jax import lax
from jax.experimental import pallas as pl
from jax.experimental.pallas import tpu as pltpu
from jax.sharding import PartitionSpec as P

SEASONS = 64
VARS = 2
ORDER = SEASONS * VARS
REACH = 1
NUGGET = 10.5
LIMIT = 16 << 20
GROUP = 16
ROOMY = 50 << 20
COST = pl.CostEstimate(flops=1, bytes_accessed=1, transcendentals=0)
ENDS = (2, 2)
LAST = 3
OUTER, INNER = -1, -2
STAGES = ((0, 1, INNER), (OUTER, 2))

F32 = jnp.float32
BF16 = jnp.bfloat16
NT = (((1,), (1,)), ((), ()))
NN = (((1,), (0,)), ((), ()))
VMEM = pltpu.VMEM


def dot(a, b, dims):
    return lax.dot_general(a, b, dims, preferred_element_type=F32)


def halves(x):
    high = x.astype(BF16)
    return high, (x - high.astype(F32)).astype(BF16)


def fold(x):
    return jnp.sum(x.reshape(x.shape[0] // 8, 8, x.shape[1]), axis=0)


def block_at(half_id, m, blocks):
    return m + half_id * (blocks - 1 - 2 * m)


def make_chunks(half):
    ends = [i for i in range(half) if i < ENDS[0] or i >= half - ENDS[1]]
    rest = [i for i in range(half) if i not in ends]
    return ends, rest[LAST:], rest[:LAST]


def pack_kernel(chunks, blocks, x_ref, same_ref, other_ref, *chunk_refs):
    me = lax.axis_index("var")
    seasons = x_ref.shape[0] // blocks
    for c, places in enumerate(chunks):
        for at, m in enumerate(places):
            for n, (half_id, ref) in enumerate(((me, same_ref), (1 - me, other_ref))):
                value = x_ref[pl.ds(block_at(half_id, m, blocks), seasons, stride=blocks), :]
                ref[m] = value
                chunk_refs[2 * c + n][at] = value


def pack(x, chunks, blocks):
    seasons, width = x.shape[0] // blocks, x.shape[1]
    counts = [blocks // 2] + [len(places) for places in chunks]
    shapes = [(count, seasons, width) for count in counts for _ in range(2)]
    return pl.pallas_call(
        functools.partial(pack_kernel, chunks, blocks),
        in_specs=[pl.BlockSpec(memory_space=VMEM)],
        out_specs=[pl.BlockSpec(memory_space=VMEM)] * len(shapes),
        out_shape=[jax.ShapeDtypeStruct(shape, F32) for shape in shapes],
        compiler_params=pltpu.CompilerParams(vmem_limit_bytes=LIMIT),
        cost_estimate=COST,
        name="pack",
    )(x)


def prepare_kernel(blocks, w_ref, w2_ref, scale_ref, held, sems):
    me = lax.axis_index("var")
    count, width = held.shape[0], held.shape[2]
    base = me * (blocks - count)
    chunks = sems.shape[0]
    edges = [count * c // chunks for c in range(chunks + 1)]
    copies = [
        pltpu.make_async_copy(
            w_ref.at[pl.ds(base + first, last - first)], held.at[pl.ds(first, last - first)], sem
        )
        for first, last, sem in zip(edges[:-1], edges[1:], [sems.at[c] for c in range(chunks)])
    ]
    for copy in copies:
        copy.start()
    top = jnp.zeros((8, width), F32)
    for c, copy in enumerate(copies):
        copy.wait()
        for row in range(edges[c], edges[c + 1]):
            m = block_at(me, row, count)
            for place, slot in enumerate((1 + me, 0, 2 - me)):
                w = held[row, slot]
                high, low = halves(w)
                lanes = slice(place * width, (place + 1) * width)
                w2_ref[m, :width, lanes] = high
                w2_ref[m, width:, lanes] = low
                top = jnp.maximum(top, jnp.max(jnp.abs(w).reshape(-1, 8, width), axis=0))
    space_top = jnp.max(jnp.max(top, axis=0, keepdims=True), axis=1, keepdims=True)
    space_top = jnp.where(space_top > 0, space_top, 1.0)
    scale_ref[...] = jnp.broadcast_to(space_top, scale_ref.shape)


def prepare(spatial):
    blocks, slots, width, _ = spatial.shape
    count = blocks // 2
    return pl.pallas_call(
        functools.partial(prepare_kernel, blocks),
        in_specs=[pl.BlockSpec(memory_space=pl.ANY)],
        out_specs=[pl.BlockSpec(memory_space=VMEM)] * 2,
        out_shape=[
            jax.ShapeDtypeStruct((count, 2 * width, slots * width), BF16),
            jax.ShapeDtypeStruct((8, width), F32),
        ],
        scratch_shapes=[
            VMEM((count, slots, width, width), F32),
            pltpu.SemaphoreType.DMA((4,)),
        ],
        compiler_params=pltpu.CompilerParams(vmem_limit_bytes=ROOMY),
        cost_estimate=COST,
        name="prepare",
    )(spatial)


def mixer_kernel(season_ref, top_ref, rh_ref, rl_ref, scale_ref):
    r = jnp.concatenate(
        [
            jnp.concatenate(
                [
                    season_ref[pl.ds(VARS * v + w, SEASONS, stride=VARS * VARS), :]
                    for w in range(VARS)
                ],
                axis=1,
            )
            for v in range(VARS)
        ],
        axis=0,
    )
    space_top = top_ref[:1, :1]
    season_top = jnp.max(jnp.max(jnp.abs(r), axis=0, keepdims=True), axis=1, keepdims=True)
    season_top = jnp.where(season_top > 0, season_top, 1.0)
    rh_ref[...], rl_ref[...] = halves(r / season_top / space_top)
    rows = lax.broadcasted_iota(jnp.int32, scale_ref.shape, 0)
    scale_ref[...] = jnp.where(rows == 4, space_top, jnp.where(rows == 5, season_top, 0.0))


def make_mixer(season, top):
    return pl.pallas_call(
        mixer_kernel,
        in_specs=[pl.BlockSpec(memory_space=VMEM)] * 2,
        out_specs=[pl.BlockSpec(memory_space=VMEM)] * 3,
        out_shape=[
            jax.ShapeDtypeStruct((ORDER, ORDER), BF16),
            jax.ShapeDtypeStruct((ORDER, ORDER), BF16),
            jax.ShapeDtypeStruct(top.shape, F32),
        ],
        compiler_params=pltpu.CompilerParams(vmem_limit_bytes=LIMIT),
        cost_estimate=COST,
        name="mixer",
    )(season, top)


def row_starts(seasons, parts):
    me_season, me_var = lax.axis_index("season"), lax.axis_index("var")
    return [
        pl.multiple_of(
            lax.rem(me_var + w, VARS) * SEASONS + lax.rem(me_season + d, parts) * seasons, seasons
        )
        for d in range(parts)
        for w in range(VARS)
    ]


def iota(rows, width):
    return lax.broadcasted_iota(jnp.int32, (rows, width), 0)


def space_product(high, low, w2):
    width = w2.shape[0] // 2
    both = dot(jnp.concatenate([high, low], axis=0), w2, NT)
    return both[:ORDER, :width] + both[:ORDER, width:] + both[ORDER:, :width]


def edge_kernel(blocks, parts, first, w2_ref, count_ref, *refs):
    *fields, outer_ref, inner_ref, held = refs
    me = lax.axis_index("var")
    seasons, width = fields[0].shape[1:]
    half = blocks // 2
    ends = (0, 1, half - 2, half - 1)
    for k, (start, field) in enumerate(zip(row_starts(seasons, parts), fields)):
        season = (iota(seasons, width) + lax.rem(start, SEASONS)).astype(F32)
        for n, m in enumerate(ends):
            seen = season >= SEASONS - count_ref[pl.ds(block_at(me, m, blocks), 1), :]
            piece = field[m if k < VARS else first.index(m)]
            held[n, pl.ds(start, seasons), :] = jnp.where(seen, piece, 0.0)
    for ref, n, at, lanes in (
        (outer_ref, 0, 0, slice(width, 3 * width)),
        (inner_ref, 2, half - 1, slice(0, 2 * width)),
    ):
        high, low = halves(jnp.concatenate([held[n], held[n + 1]], axis=1))
        ref[:ORDER, :] = held[0 if n == 0 else 3]
        ref[ORDER : 2 * ORDER, :] = space_product(high, low, w2_ref[at, :, lanes])
    outer_ref[2 * ORDER :, :] = jnp.broadcast_to(
        count_ref[pl.ds(block_at(me, 0, blocks), 1), :], (8, width)
    )


def edge(w2, count_rows, fields, parts, first):
    blocks, width = count_rows.shape
    whole = [pl.BlockSpec(memory_space=VMEM)]
    return pl.pallas_call(
        functools.partial(edge_kernel, blocks, parts, first),
        in_specs=whole * (2 + len(fields)),
        out_specs=whole * 2,
        out_shape=[
            jax.ShapeDtypeStruct((2 * ORDER + 8, width), F32),
            jax.ShapeDtypeStruct((2 * ORDER, width), F32),
        ],
        scratch_shapes=[VMEM((4, ORDER, width), F32)],
        compiler_params=pltpu.CompilerParams(vmem_limit_bytes=LIMIT),
        cost_estimate=COST,
        name="edge",
    )(w2, count_rows, *fields)


def make_plan(places_of, half):
    plan = []
    have_x, have_1, have_2 = set(), set(), set()
    for chunks in STAGES:
        new = []
        for c in chunks:
            new += [-1] if c == OUTER else [half] if c == INNER else places_of[c]
        have_x |= set(new)
        ones = [
            i
            for i in range(-1, half + 1)
            if i not in have_1 and {max(i - 1, -1), i, min(i + 1, half)} <= have_x
        ]
        have_1 |= set(ones)
        twos = [i for i in range(half) if i not in have_2 and {i - 1, i, i + 1} <= have_1]
        have_2 |= set(twos)
        later_1 = [i for i in range(-1, half + 1) if i not in have_1]
        later_2 = [i for i in range(half) if i not in have_2]
        keep_x = sorted({i + d for i in later_1 for d in (-1, 0, 1)} & have_x)
        keep_1 = sorted({i + d for i in later_2 for d in (-1, 0, 1)} & have_1)
        plan.append((new, ones, twos, keep_x, keep_1))
    return plan


def in_half(ids, half):
    return [i for i in ids if 0 <= i < half]


def runs(ids, most):
    groups = []
    for i in ids:
        if groups and len(groups[-1]) < most:
            groups[-1].append(i)
        else:
            groups.append([i])
    return groups


def make_stage(plan, places_of, m, blocks, parts, seasons, width):
    half = blocks // 2
    slots = parts * VARS
    new, ones, twos, keep_x, keep_1 = plan[m]
    first, last = m == 0, m == len(plan) - 1
    chunks = [c for c in STAGES[m] if c >= 0]
    outer, inner = OUTER in STAGES[m], INNER in STAGES[m]
    old_x, old_1 = ([], []) if first else (plan[m - 1][3], plan[m - 1][4])
    x_at = {i: n for n, i in enumerate(list(old_x) + list(new))}
    one_at = {i: n for n, i in enumerate(list(old_1) + list(ones))}
    inner_ones = in_half(ones, half)

    def kernel(*refs):
        refs = list(refs)

        def take(n):
            out = refs[:n]
            del refs[:n]
            return out

        near_refs = take(VARS)
        far_refs = [take(slots - VARS) for _ in chunks]
        w2_ref, rh_ref, rl_ref, count_ref, sums_in = take(5)
        if not first:
            old_xh, old_xl, old_1h, old_1l = take(4)
        if outer:
            (outer_ref,) = take(1)
        if inner:
            (inner_ref,) = take(1)
        sums_out, mine, theirs = take(3)
        if not last:
            keep_xh, keep_xl, keep_1h, keep_1l = take(4)
        xh, xl, oh, ol, pick = take(5)
        me = lax.axis_index("var")

        def count_row(i):
            if i == -1:
                return outer_ref[2 * ORDER : 2 * ORDER + 1, :]
            return count_ref[pl.ds(block_at(me, i, blocks), 1), :]

        season = lax.rem(iota(ORDER, width), SEASONS).astype(F32)

        def masked(i, value):
            return jnp.where(season >= SEASONS - count_row(i), value, 0.0)

        for n in range(len(old_x)):
            xh[n] = old_xh[n]
            xl[n] = old_xl[n]
        for n in range(len(old_1)):
            oh[n] = old_1h[n]
            ol[n] = old_1l[n]

        starts = row_starts(seasons, parts)
        total_0 = sums_in[0]
        for c, fars in zip(chunks, far_refs):
            places = places_of[c]
            for k, start in enumerate(starts):
                piece_season = (iota(seasons, width) + lax.rem(start, SEASONS)).astype(F32)
                for i in places:
                    piece = near_refs[k][i] if k < VARS else fars[k - VARS][places.index(i)]
                    total_0 += fold(piece * piece)
                    seen = piece_season >= SEASONS - count_row(i)
                    high, low = halves(jnp.where(seen, piece, 0.0))
                    xh[x_at[i], pl.ds(start, seasons), :] = high
                    xl[x_at[i], pl.ds(start, seasons), :] = low
        if outer:
            xh[x_at[-1]], xl[x_at[-1]] = halves(outer_ref[:ORDER, :])
        if inner:
            xh[x_at[half]], xl[x_at[half]] = halves(inner_ref[:ORDER, :])
        sums_out[0] = total_0

        def space(i, high, low, at):
            if 0 <= i < half:
                hs = jnp.concatenate([high[at[i + d]] for d in (-1, 0, 1)], axis=1)
                ls = jnp.concatenate([low[at[i + d]] for d in (-1, 0, 1)], axis=1)
                return space_product(hs, ls, w2_ref[i])
            ref, last_at, lane = (outer_ref, 0, 0) if i < 0 else (inner_ref, half - 1, 2 * width)
            lanes = slice(lane, lane + width)
            near = w2_ref[last_at, :width, lanes]
            total = ref[ORDER : 2 * ORDER, :] + dot(high[at[last_at]], near, NN)
            total += dot(high[at[last_at]], w2_ref[last_at, width:, lanes], NN)
            return total + dot(low[at[last_at]], near, NN)

        rh, rl = rh_ref[...], rl_ref[...]
        mixer = jnp.concatenate(
            [
                jnp.concatenate([rh, rh], axis=1),
                jnp.concatenate([rl, jnp.zeros_like(rl)], axis=1),
            ],
            axis=0,
        )

        def mix(parts_of):
            zh, zl = halves(jnp.concatenate(parts_of, axis=1))
            both = dot(mixer, jnp.concatenate([zh, zl], axis=0), NN)
            return both[:ORDER] + both[ORDER:]

        def hand_out(n, value):
            pick[n] = value
            mine[n] = pick[n, pl.ds(starts[0], seasons), :]
            theirs[n] = pick[n, pl.ds(starts[1], seasons), :]

        total_1, total_2, total_3 = sums_in[1], sums_in[2], sums_in[3]
        for group in runs(ones, GROUP):
            mixed = mix([space(i, xh, xl, x_at) for i in group])
            for n, i in enumerate(group):
                one = masked(i, mixed[:, n * width : (n + 1) * width])
                oh[one_at[i]], ol[one_at[i]] = halves(one)
                if 0 <= i < half:
                    x = xh[x_at[i]].astype(F32) + xl[x_at[i]].astype(F32)
                    total_1 += fold(x * one)
                    total_2 += fold(one * one)
                    hand_out(inner_ones.index(i), one)
        sums_out[1] = total_1
        sums_out[2] = total_2
        for group in runs(twos, GROUP):
            mixed = mix([space(i, oh, ol, one_at) for i in group])
            for n, i in enumerate(group):
                two = masked(i, mixed[:, n * width : (n + 1) * width])
                one = oh[one_at[i]].astype(F32) + ol[one_at[i]].astype(F32)
                total_3 += fold(one * two)
                hand_out(len(inner_ones) + twos.index(i), two)
        sums_out[3] = total_3
        if not last:
            for n, i in enumerate(keep_x):
                keep_xh[n] = xh[x_at[i]]
                keep_xl[n] = xl[x_at[i]]
            for n, i in enumerate(keep_1):
                keep_1h[n] = oh[one_at[i]]
                keep_1l[n] = ol[one_at[i]]

    tile = (ORDER, width)
    count = len(inner_ones) + len(twos)
    outs = [jax.ShapeDtypeStruct((4, 8, width), F32)]
    outs += [jax.ShapeDtypeStruct((count, seasons, width), F32)] * 2
    if not last:
        outs += [jax.ShapeDtypeStruct((len(keep_x),) + tile, BF16)] * 2
        outs += [jax.ShapeDtypeStruct((len(keep_1),) + tile, BF16)] * 2
    scratch = [VMEM((len(x_at),) + tile, BF16)] * 2 + [VMEM((len(one_at),) + tile, BF16)] * 2
    scratch += [VMEM((count,) + tile, F32)]
    return kernel, outs, scratch


def run_stage(plan, chunks, m, blocks, parts, seasons, width, operands):
    kernel, outs, scratch = make_stage(plan, chunks, m, blocks, parts, seasons, width)
    return pl.pallas_call(
        kernel,
        in_specs=[pl.BlockSpec(memory_space=VMEM)] * len(operands),
        out_shape=outs,
        scratch_shapes=scratch,
        compiler_params=pltpu.CompilerParams(vmem_limit_bytes=LIMIT),
        cost_estimate=COST,
        name="stage",
    )(*operands)


def finish_kernel(plan, blocks, tiles, *refs):
    refs = list(refs)
    count = len(plan)
    gathered, refs = refs[:tiles], refs[tiles:]
    fields, refs = refs[:2], refs[2:]
    mine, theirs = refs[:count], refs[count : 2 * count]
    x_out, r_out, x_held, r_held, sems = refs[2 * count :]
    half = blocks // 2
    me = lax.axis_index("var")

    def total(v):
        return jnp.sum(v, axis=1, keepdims=True)

    tuples = [ref[j] for ref in gathered for j in range(ref.shape[0])]
    top = functools.reduce(jnp.maximum, [t[4:5] for t in tuples])
    sums = [0.0, 0.0, 0.0, 0.0]
    for t in tuples:
        ratio = t[4:5] / top
        factor = jnp.ones_like(ratio)
        for n in range(4):
            sums[n] = sums[n] + t[n : n + 1] * factor
            factor = factor * ratio
    m0, m1, m2, m3 = [total(v) for v in sums]
    scale = (top * tuples[0][5:6])[:, :1]

    first = NUGGET * m0 + scale * m1
    alpha = m0 / first
    lead = alpha * scale
    mean = m1 / m0
    fresh = lead * lead * (m2 - mean * m1)
    c = lead * mean + fresh / m0
    dd = c * c * m0 - 2.0 * c * lead * m1 + lead * lead * m2
    dkd = c * c * m1 - 2.0 * c * lead * m2 + lead * lead * m3
    alpha_2 = fresh / (NUGGET * dd + scale * dkd)
    x_0 = alpha + alpha_2 * c
    r_0 = lead * mean - NUGGET * alpha_2 * c
    x_1 = -alpha_2 * lead
    r_1 = NUGGET * alpha_2 * lead - lead - alpha_2 * scale * c
    r_2 = alpha_2 * scale * lead

    one_at, two_at = {}, {}
    for m, (_, ones, twos, _, _) in enumerate(plan):
        inner = in_half(ones, half)
        one_at.update({i: (m, n) for n, i in enumerate(inner)})
        two_at.update({i: (m, len(inner) + n) for n, i in enumerate(twos)})
    copies = []
    for side, (half_id, held, t) in enumerate(((me, mine, tuples[0]), (1 - me, theirs, tuples[1]))):
        ratio = (t[4:5] / top)[:, :1]
        x_1h, r_1h, r_2h = x_1 * ratio, r_1 * ratio, r_2 * ratio * ratio
        for i in range(half):
            x = fields[side][i]
            m, n = one_at[i]
            one = held[m][n]
            m, n = two_at[i]
            two = held[m][n]
            at = side * half + i
            x_held[at] = x_0 * x + x_1h * one
            r_held[at] = r_0 * x + r_1h * one + r_2h * two
            row = block_at(half_id, i, blocks)
            for n, (source, target) in enumerate(((x_held, x_out), (r_held, r_out))):
                copy = pltpu.make_async_copy(
                    source.at[at], target.at[:, row, 0, :], sems.at[n, at]
                )
                copy.start()
                copies.append(copy)
    for copy in copies:
        copy.wait()


def finish(plan, shape, gathered, packs, mine, theirs):
    seasons, blocks, _, width = shape
    operands = [*gathered, *packs, *mine, *theirs]
    return pl.pallas_call(
        functools.partial(finish_kernel, plan, blocks, len(gathered)),
        in_specs=[pl.BlockSpec(memory_space=VMEM)] * len(operands),
        out_specs=[pl.BlockSpec(memory_space=pltpu.HBM)] * 2,
        out_shape=[jax.ShapeDtypeStruct(shape, F32)] * 2,
        scratch_shapes=[VMEM((blocks, seasons, width), F32)] * 2
        + [pltpu.SemaphoreType.DMA((2, blocks))],
        compiler_params=pltpu.CompilerParams(vmem_limit_bytes=LIMIT),
        cost_estimate=COST,
        name="finish",
    )(*operands)


def from_group(value, step, swap):
    size = lax.axis_size("season")
    pairs = [
        (((p + step) % size) * VARS + (v + swap) % VARS, p * VARS + v)
        for p in range(size)
        for v in range(VARS)
    ]
    return lax.ppermute(value, ("season", "var"), pairs)


def across_edge(value):
    size = lax.axis_size("space")
    pairs = []
    for i in range(1, size * VARS - 1, 2):
        pairs += [(i, i + 1), (i + 1, i)]
    return lax.ppermute(value, ("space", "var"), pairs)


def gather_tiles(value):
    found = [value, from_group(value, 0, 1)]
    size = lax.axis_size("space")
    if size & (size - 1):
        me = lax.axis_index("space")
        tiles = lax.all_gather(jnp.concatenate(found, axis=0), "space", axis=0, tiled=True)
        return [jnp.roll(tiles, -me * VARS, axis=0)]
    hop = 1
    while hop < size:
        have = jnp.concatenate(found, axis=0)
        pairs = [
            (i * VARS + v, (i ^ hop) * VARS + 1 - v) for i in range(size) for v in range(VARS)
        ]
        found.append(lax.ppermute(have, ("space", "var"), pairs))
        hop *= 2
    return found


def body(right_side, spatial, columns, counts, season_cov):
    del columns
    seasons = right_side.shape[0]
    blocks, _, width, _ = spatial.shape
    parts = lax.axis_size("season")
    half = blocks // 2
    places = make_chunks(half)
    plan = make_plan(places, half)

    x = right_side.reshape(seasons * blocks, width)
    count_rows = jnp.broadcast_to(counts.astype(F32)[:, None], (blocks, width))

    same, other, *packs = pack(x, places, blocks)
    close = [same, from_group(other, 0, 1)]
    chunks = [
        [from_group(pair[w], d, w) for d in range(1, parts) for w in range(VARS)]
        for pair in zip(packs[0::2], packs[1::2])
    ]
    w2, top = prepare(spatial)
    outer, inner = edge(w2, count_rows, close + chunks[0], parts, places[0])
    outer, inner = across_edge(outer), from_group(inner, 0, 1)

    season = season_cov.transpose(0, 1, 3, 2).reshape(SEASONS * VARS * VARS, SEASONS)
    rh, rl, scale = make_mixer(season, top)
    sums = jnp.zeros((4, 8, width), F32)
    mine, theirs, kept = [], [], []
    for m, stage in enumerate(STAGES):
        operands = close + [f for c in stage if c >= 0 for f in chunks[c]]
        operands += [w2, rh, rl, count_rows, sums] + kept + [outer] * (OUTER in stage) + [inner] * (INNER in stage)
        out = run_stage(plan, places, m, blocks, parts, seasons, width, operands)
        sums, kept = out[0], list(out[3:])
        mine.append(out[1])
        theirs.append(from_group(out[2], 0, 1))
    tile = jnp.concatenate([jnp.sum(sums, axis=1), scale[4:]], axis=0)[None]
    gathered = gather_tiles(tile)
    x_out, r_out = finish(plan, (seasons, blocks, 1, width), gathered, [same, other], mine, theirs)
    return x_out.reshape(right_side.shape), r_out.reshape(right_side.shape)


def solution(mesh):
    field = P("season", "var", ("groups", "space"))
    return jax.shard_map(
        body,
        mesh=mesh,
        in_specs=(
            field,
            P(("groups", "space"), None, None, None),
            P(("groups", "space"), None),
            P(("groups", "space")),
            P(),
        ),
        out_specs=(field, field),
        check_vma=False,
    )
```

```python
import functools

import jax
import jax.numpy as jnp
from jax import lax
from jax.experimental import pallas as pl
from jax.experimental.pallas import tpu as pltpu
from jax.sharding import PartitionSpec as P

SEASONS = 64
VARS = 2
ORDER = SEASONS * VARS
REACH = 1
NUGGET = 10.5
LIMIT = 16 << 20
GROUP = 16
ROOMY = 50 << 20
COST = pl.CostEstimate(flops=1, bytes_accessed=1, transcendentals=0)
ENDS = (2, 2)
LAST = 3
OUTER, INNER = -1, -2
STAGES = ((0, 1, INNER), (OUTER, 2))

F32 = jnp.float32
BF16 = jnp.bfloat16
NT = (((1,), (1,)), ((), ()))
NN = (((1,), (0,)), ((), ()))
VMEM = pltpu.VMEM


def dot(a, b, dims):
    return lax.dot_general(a, b, dims, preferred_element_type=F32)


def halves(x):
    high = x.astype(BF16)
    return high, (x - high.astype(F32)).astype(BF16)


def fold(x):
    return jnp.sum(x.reshape(x.shape[0] // 8, 8, x.shape[1]), axis=0)


def block_at(half_id, m, blocks):
    return m + half_id * (blocks - 1 - 2 * m)


def make_chunks(half):
    ends = [i for i in range(half) if i < ENDS[0] or i >= half - ENDS[1]]
    rest = [i for i in range(half) if i not in ends]
    return ends, rest[LAST:], rest[:LAST]


def pack_kernel(chunks, blocks, x_ref, same_ref, other_ref, *chunk_refs):
    me = lax.axis_index("var")
    seasons = x_ref.shape[0] // blocks
    for c, places in enumerate(chunks):
        for at, m in enumerate(places):
            for n, (half_id, ref) in enumerate(((me, same_ref), (1 - me, other_ref))):
                value = x_ref[pl.ds(block_at(half_id, m, blocks), seasons, stride=blocks), :]
                ref[m] = value
                chunk_refs[2 * c + n][at] = value


def pack(x, chunks, blocks):
    seasons, width = x.shape[0] // blocks, x.shape[1]
    counts = [blocks // 2] + [len(places) for places in chunks]
    shapes = [(count, seasons, width) for count in counts for _ in range(2)]
    return pl.pallas_call(
        functools.partial(pack_kernel, chunks, blocks),
        in_specs=[pl.BlockSpec(memory_space=VMEM)],
        out_specs=[pl.BlockSpec(memory_space=VMEM)] * len(shapes),
        out_shape=[jax.ShapeDtypeStruct(shape, F32) for shape in shapes],
        compiler_params=pltpu.CompilerParams(vmem_limit_bytes=LIMIT),
        cost_estimate=COST,
        name="pack",
    )(x)


def prepare_kernel(blocks, w_ref, w2_ref, scale_ref, held, sems):
    me = lax.axis_index("var")
    count, width = held.shape[0], held.shape[2]
    base = me * (blocks - count)
    chunks = sems.shape[0]
    edges = [count * c // chunks for c in range(chunks + 1)]
    copies = [
        pltpu.make_async_copy(
            w_ref.at[pl.ds(base + first, last - first)], held.at[pl.ds(first, last - first)], sem
        )
        for first, last, sem in zip(edges[:-1], edges[1:], [sems.at[c] for c in range(chunks)])
    ]
    for copy in copies:
        copy.start()
    top = jnp.zeros((8, width), F32)
    for c, copy in enumerate(copies):
        copy.wait()
        for row in range(edges[c], edges[c + 1]):
            m = block_at(me, row, count)
            for place, slot in enumerate((1 + me, 0, 2 - me)):
                w = held[row, slot]
                high, low = halves(w)
                lanes = slice(place * width, (place + 1) * width)
                w2_ref[m, :width, lanes] = high
                w2_ref[m, width:, lanes] = low
                top = jnp.maximum(top, jnp.max(jnp.abs(w).reshape(-1, 8, width), axis=0))
    space_top = jnp.max(jnp.max(top, axis=0, keepdims=True), axis=1, keepdims=True)
    space_top = jnp.where(space_top > 0, space_top, 1.0)
    scale_ref[...] = jnp.broadcast_to(space_top, scale_ref.shape)


def prepare(spatial):
    blocks, slots, width, _ = spatial.shape
    count = blocks // 2
    return pl.pallas_call(
        functools.partial(prepare_kernel, blocks),
        in_specs=[pl.BlockSpec(memory_space=pl.ANY)],
        out_specs=[pl.BlockSpec(memory_space=VMEM)] * 2,
        out_shape=[
            jax.ShapeDtypeStruct((count, 2 * width, slots * width), BF16),
            jax.ShapeDtypeStruct((8, width), F32),
        ],
        scratch_shapes=[
            VMEM((count, slots, width, width), F32),
            pltpu.SemaphoreType.DMA((4,)),
        ],
        compiler_params=pltpu.CompilerParams(vmem_limit_bytes=ROOMY),
        cost_estimate=COST,
        name="prepare",
    )(spatial)


def mixer_kernel(season_ref, top_ref, rh_ref, rl_ref, scale_ref):
    r = jnp.concatenate(
        [
            jnp.concatenate(
                [
                    season_ref[pl.ds(VARS * v + w, SEASONS, stride=VARS * VARS), :]
                    for w in range(VARS)
                ],
                axis=1,
            )
            for v in range(VARS)
        ],
        axis=0,
    )
    space_top = top_ref[:1, :1]
    season_top = jnp.max(jnp.max(jnp.abs(r), axis=0, keepdims=True), axis=1, keepdims=True)
    season_top = jnp.where(season_top > 0, season_top, 1.0)
    rh_ref[...], rl_ref[...] = halves(r / season_top / space_top)
    rows = lax.broadcasted_iota(jnp.int32, scale_ref.shape, 0)
    scale_ref[...] = jnp.where(rows == 4, space_top, jnp.where(rows == 5, season_top, 0.0))


def make_mixer(season, top):
    return pl.pallas_call(
        mixer_kernel,
        in_specs=[pl.BlockSpec(memory_space=VMEM)] * 2,
        out_specs=[pl.BlockSpec(memory_space=VMEM)] * 3,
        out_shape=[
            jax.ShapeDtypeStruct((ORDER, ORDER), BF16),
            jax.ShapeDtypeStruct((ORDER, ORDER), BF16),
            jax.ShapeDtypeStruct(top.shape, F32),
        ],
        compiler_params=pltpu.CompilerParams(vmem_limit_bytes=LIMIT),
        cost_estimate=COST,
        name="mixer",
    )(season, top)


def row_starts(seasons, parts):
    me_season, me_var = lax.axis_index("season"), lax.axis_index("var")
    return [
        pl.multiple_of(
            lax.rem(me_var + w, VARS) * SEASONS + lax.rem(me_season + d, parts) * seasons, seasons
        )
        for d in range(parts)
        for w in range(VARS)
    ]


def iota(rows, width):
    return lax.broadcasted_iota(jnp.int32, (rows, width), 0)


def space_product(high, low, w2):
    width = w2.shape[0] // 2
    both = dot(jnp.concatenate([high, low], axis=0), w2, NT)
    return both[:ORDER, :width] + both[:ORDER, width:] + both[ORDER:, :width]


def edge_kernel(blocks, parts, first, w2_ref, count_ref, *refs):
    *fields, outer_ref, inner_ref, held = refs
    me = lax.axis_index("var")
    seasons, width = fields[0].shape[1:]
    half = blocks // 2
    ends = (0, 1, half - 2, half - 1)
    for k, (start, field) in enumerate(zip(row_starts(seasons, parts), fields)):
        season = (iota(seasons, width) + lax.rem(start, SEASONS)).astype(F32)
        for n, m in enumerate(ends):
            seen = season >= SEASONS - count_ref[pl.ds(block_at(me, m, blocks), 1), :]
            piece = field[m if k < VARS else first.index(m)]
            held[n, pl.ds(start, seasons), :] = jnp.where(seen, piece, 0.0)
    for ref, n, at, lanes in (
        (outer_ref, 0, 0, slice(width, 3 * width)),
        (inner_ref, 2, half - 1, slice(0, 2 * width)),
    ):
        high, low = halves(jnp.concatenate([held[n], held[n + 1]], axis=1))
        ref[:ORDER, :] = held[0 if n == 0 else 3]
        ref[ORDER : 2 * ORDER, :] = space_product(high, low, w2_ref[at, :, lanes])
    inner_ref[2 * ORDER :, :] = jnp.zeros((16, width), F32)
    outer_ref[2 * ORDER :, :] = jnp.broadcast_to(
        count_ref[pl.ds(block_at(me, 0, blocks), 1), :], (8, width)
    )


def edge(w2, count_rows, fields, parts, first):
    blocks, width = count_rows.shape
    whole = [pl.BlockSpec(memory_space=VMEM)]
    return pl.pallas_call(
        functools.partial(edge_kernel, blocks, parts, first),
        in_specs=whole * (2 + len(fields)),
        out_specs=whole * 2,
        out_shape=[
            jax.ShapeDtypeStruct((2 * ORDER + 8, width), F32),
            jax.ShapeDtypeStruct((2 * ORDER + 16, width), F32),
        ],
        scratch_shapes=[VMEM((4, ORDER, width), F32)],
        compiler_params=pltpu.CompilerParams(vmem_limit_bytes=LIMIT),
        cost_estimate=COST,
        name="edge",
    )(w2, count_rows, *fields)


def make_plan(places_of, half):
    plan = []
    have_x, have_1, have_2 = set(), set(), set()
    for chunks in STAGES:
        new = []
        for c in chunks:
            new += [-1] if c == OUTER else [half] if c == INNER else places_of[c]
        have_x |= set(new)
        ones = [
            i
            for i in range(-1, half + 1)
            if i not in have_1 and {max(i - 1, -1), i, min(i + 1, half)} <= have_x
        ]
        have_1 |= set(ones)
        twos = [i for i in range(half) if i not in have_2 and {i - 1, i, i + 1} <= have_1]
        have_2 |= set(twos)
        later_1 = [i for i in range(-1, half + 1) if i not in have_1]
        later_2 = [i for i in range(half) if i not in have_2]
        keep_x = sorted({i + d for i in later_1 for d in (-1, 0, 1)} & have_x)
        keep_1 = sorted({i + d for i in later_2 for d in (-1, 0, 1)} & have_1)
        plan.append((new, ones, twos, keep_x, keep_1))
    return plan


def in_half(ids, half):
    return [i for i in ids if 0 <= i < half]


def runs(ids, most):
    groups = []
    for i in ids:
        if groups and len(groups[-1]) < most:
            groups[-1].append(i)
        else:
            groups.append([i])
    return groups


def make_stage(plan, places_of, m, blocks, parts, seasons, width):
    half = blocks // 2
    slots = parts * VARS
    new, ones, twos, keep_x, keep_1 = plan[m]
    first, last = m == 0, m == len(plan) - 1
    chunks = [c for c in STAGES[m] if c >= 0]
    outer, inner = OUTER in STAGES[m], INNER in STAGES[m]
    old_x, old_1 = ([], []) if first else (plan[m - 1][3], plan[m - 1][4])
    x_at = {i: n for n, i in enumerate(list(old_x) + list(new))}
    one_at = {i: n for n, i in enumerate(list(old_1) + list(ones))}
    inner_ones = in_half(ones, half)

    def kernel(*refs):
        refs = list(refs)

        def take(n):
            out = refs[:n]
            del refs[:n]
            return out

        near_refs = take(VARS)
        far_refs = [take(slots - VARS) for _ in chunks]
        w2_ref, rh_ref, rl_ref, count_ref, sums_in = take(5)
        if not first:
            old_xh, old_xl, old_1h, old_1l = take(4)
        if outer:
            (outer_ref,) = take(1)
        if inner:
            (inner_ref,) = take(1)
        sums_out, mine, theirs = take(3)
        if not last:
            keep_xh, keep_xl, keep_1h, keep_1l = take(4)
        xh, xl, oh, ol, pick = take(5)
        me = lax.axis_index("var")

        def count_row(i):
            if i == -1:
                return outer_ref[2 * ORDER : 2 * ORDER + 1, :]
            return count_ref[pl.ds(block_at(me, i, blocks), 1), :]

        season = lax.rem(iota(ORDER, width), SEASONS).astype(F32)

        def masked(i, value):
            return jnp.where(season >= SEASONS - count_row(i), value, 0.0)

        for n in range(len(old_x)):
            xh[n] = old_xh[n]
            xl[n] = old_xl[n]
        for n in range(len(old_1)):
            oh[n] = old_1h[n]
            ol[n] = old_1l[n]

        starts = row_starts(seasons, parts)
        total_0 = sums_in[0]
        for c, fars in zip(chunks, far_refs):
            places = places_of[c]
            for k, start in enumerate(starts):
                piece_season = (iota(seasons, width) + lax.rem(start, SEASONS)).astype(F32)
                for i in places:
                    piece = near_refs[k][i] if k < VARS else fars[k - VARS][places.index(i)]
                    total_0 += fold(piece * piece)
                    seen = piece_season >= SEASONS - count_row(i)
                    high, low = halves(jnp.where(seen, piece, 0.0))
                    xh[x_at[i], pl.ds(start, seasons), :] = high
                    xl[x_at[i], pl.ds(start, seasons), :] = low
        if outer:
            xh[x_at[-1]], xl[x_at[-1]] = halves(outer_ref[:ORDER, :])
        if inner:
            xh[x_at[half]], xl[x_at[half]] = halves(inner_ref[:ORDER, :])
        sums_out[0] = total_0

        def space(i, high, low, at):
            if 0 <= i < half:
                hs = jnp.concatenate([high[at[i + d]] for d in (-1, 0, 1)], axis=1)
                ls = jnp.concatenate([low[at[i + d]] for d in (-1, 0, 1)], axis=1)
                return space_product(hs, ls, w2_ref[i])
            ref, last_at, lane = (outer_ref, 0, 0) if i < 0 else (inner_ref, half - 1, 2 * width)
            lanes = slice(lane, lane + width)
            near = w2_ref[last_at, :width, lanes]
            total = ref[ORDER : 2 * ORDER, :] + dot(high[at[last_at]], near, NN)
            total += dot(high[at[last_at]], w2_ref[last_at, width:, lanes], NN)
            return total + dot(low[at[last_at]], near, NN)

        rh, rl = rh_ref[...], rl_ref[...]
        mixer = jnp.concatenate(
            [
                jnp.concatenate([rh, rh], axis=1),
                jnp.concatenate([rl, jnp.zeros_like(rl)], axis=1),
            ],
            axis=0,
        )

        def mix(parts_of):
            zh, zl = halves(jnp.concatenate(parts_of, axis=1))
            both = dot(mixer, jnp.concatenate([zh, zl], axis=0), NN)
            return both[:ORDER] + both[ORDER:]

        def hand_out(n, value):
            pick[n] = value
            mine[n] = pick[n, pl.ds(starts[0], seasons), :]
            theirs[n] = pick[n, pl.ds(starts[1], seasons), :]

        total_1, total_2, total_3 = sums_in[1], sums_in[2], sums_in[3]
        for group in runs(ones, GROUP):
            mixed = mix([space(i, xh, xl, x_at) for i in group])
            for n, i in enumerate(group):
                one = masked(i, mixed[:, n * width : (n + 1) * width])
                oh[one_at[i]], ol[one_at[i]] = halves(one)
                if 0 <= i < half:
                    x = xh[x_at[i]].astype(F32) + xl[x_at[i]].astype(F32)
                    total_1 += fold(x * one)
                    total_2 += fold(one * one)
                    hand_out(inner_ones.index(i), one)
        sums_out[1] = total_1
        sums_out[2] = total_2
        for group in runs(twos, GROUP):
            mixed = mix([space(i, oh, ol, one_at) for i in group])
            for n, i in enumerate(group):
                two = masked(i, mixed[:, n * width : (n + 1) * width])
                one = oh[one_at[i]].astype(F32) + ol[one_at[i]].astype(F32)
                total_3 += fold(one * two)
                hand_out(len(inner_ones) + twos.index(i), two)
        sums_out[3] = total_3
        if not last:
            for n, i in enumerate(keep_x):
                keep_xh[n] = xh[x_at[i]]
                keep_xl[n] = xl[x_at[i]]
            for n, i in enumerate(keep_1):
                keep_1h[n] = oh[one_at[i]]
                keep_1l[n] = ol[one_at[i]]

    tile = (ORDER, width)
    count = len(inner_ones) + len(twos)
    outs = [jax.ShapeDtypeStruct((4, 8, width), F32)]
    outs += [jax.ShapeDtypeStruct((count, seasons, width), F32)] * 2
    if not last:
        outs += [jax.ShapeDtypeStruct((len(keep_x),) + tile, BF16)] * 2
        outs += [jax.ShapeDtypeStruct((len(keep_1),) + tile, BF16)] * 2
    scratch = [VMEM((len(x_at),) + tile, BF16)] * 2 + [VMEM((len(one_at),) + tile, BF16)] * 2
    scratch += [VMEM((count,) + tile, F32)]
    return kernel, outs, scratch


def run_stage(plan, chunks, m, blocks, parts, seasons, width, operands):
    kernel, outs, scratch = make_stage(plan, chunks, m, blocks, parts, seasons, width)
    return pl.pallas_call(
        kernel,
        in_specs=[pl.BlockSpec(memory_space=VMEM)] * len(operands),
        out_shape=outs,
        scratch_shapes=scratch,
        compiler_params=pltpu.CompilerParams(vmem_limit_bytes=LIMIT),
        cost_estimate=COST,
        name="stage",
    )(*operands)


def finish_kernel(plan, blocks, tiles, *refs):
    refs = list(refs)
    count = len(plan)
    gathered, refs = refs[:tiles], refs[tiles:]
    fields, refs = refs[:2], refs[2:]
    mine, theirs = refs[:count], refs[count : 2 * count]
    x_out, r_out, x_held, r_held, sems = refs[2 * count :]
    half = blocks // 2
    me = lax.axis_index("var")

    def total(v):
        return jnp.sum(v, axis=1, keepdims=True)

    tuples = [ref[j] for ref in gathered for j in range(ref.shape[0])]
    top = functools.reduce(jnp.maximum, [t[4:5] for t in tuples])
    sums = [0.0, 0.0, 0.0, 0.0]
    for t in tuples:
        ratio = t[4:5] / top
        factor = jnp.ones_like(ratio)
        for n in range(4):
            sums[n] = sums[n] + t[n : n + 1] * factor
            factor = factor * ratio
    m0, m1, m2, m3 = [total(v) for v in sums]
    scale = (top * tuples[0][5:6])[:, :1]

    first = NUGGET * m0 + scale * m1
    alpha = m0 / first
    lead = alpha * scale
    mean = m1 / m0
    fresh = lead * lead * (m2 - mean * m1)
    c = lead * mean + fresh / m0
    dd = c * c * m0 - 2.0 * c * lead * m1 + lead * lead * m2
    dkd = c * c * m1 - 2.0 * c * lead * m2 + lead * lead * m3
    alpha_2 = fresh / (NUGGET * dd + scale * dkd)
    x_0 = alpha + alpha_2 * c
    r_0 = lead * mean - NUGGET * alpha_2 * c
    x_1 = -alpha_2 * lead
    r_1 = NUGGET * alpha_2 * lead - lead - alpha_2 * scale * c
    r_2 = alpha_2 * scale * lead

    one_at, two_at = {}, {}
    for m, (_, ones, twos, _, _) in enumerate(plan):
        inner = in_half(ones, half)
        one_at.update({i: (m, n) for n, i in enumerate(inner)})
        two_at.update({i: (m, len(inner) + n) for n, i in enumerate(twos)})
    copies = []
    for side, (half_id, held, t) in enumerate(((me, mine, tuples[0]), (1 - me, theirs, tuples[len(tuples) // 2]))):
        ratio = (t[4:5] / top)[:, :1]
        x_1h, r_1h, r_2h = x_1 * ratio, r_1 * ratio, r_2 * ratio * ratio
        for i in range(half):
            x = fields[side][i]
            m, n = one_at[i]
            one = held[m][n]
            m, n = two_at[i]
            two = held[m][n]
            at = side * half + i
            x_held[at] = x_0 * x + x_1h * one
            r_held[at] = r_0 * x + r_1h * one + r_2h * two
            row = block_at(half_id, i, blocks)
            for n, (source, target) in enumerate(((x_held, x_out), (r_held, r_out))):
                copy = pltpu.make_async_copy(
                    source.at[at], target.at[:, row, 0, :], sems.at[n, at]
                )
                copy.start()
                copies.append(copy)
    for copy in copies:
        copy.wait()


def finish(plan, shape, gathered, packs, mine, theirs):
    seasons, blocks, _, width = shape
    operands = [*gathered, *packs, *mine, *theirs]
    return pl.pallas_call(
        functools.partial(finish_kernel, plan, blocks, len(gathered)),
        in_specs=[pl.BlockSpec(memory_space=VMEM)] * len(operands),
        out_specs=[pl.BlockSpec(memory_space=pltpu.HBM)] * 2,
        out_shape=[jax.ShapeDtypeStruct(shape, F32)] * 2,
        scratch_shapes=[VMEM((blocks, seasons, width), F32)] * 2
        + [pltpu.SemaphoreType.DMA((2, blocks))],
        compiler_params=pltpu.CompilerParams(vmem_limit_bytes=LIMIT),
        cost_estimate=COST,
        name="finish",
    )(*operands)


def from_group(value, step, swap):
    size = lax.axis_size("season")
    pairs = [
        (((p + step) % size) * VARS + (v + swap) % VARS, p * VARS + v)
        for p in range(size)
        for v in range(VARS)
    ]
    return lax.ppermute(value, ("season", "var"), pairs)


def across_edge(value):
    size = lax.axis_size("space")
    pairs = []
    for i in range(1, size * VARS - 1, 2):
        pairs += [(i, i + 1), (i + 1, i)]
    return lax.ppermute(value, ("space", "var"), pairs)


def gather_tiles(value):
    found = [value]
    size = lax.axis_size("space")
    if size & (size - 1):
        me = lax.axis_index("space")
        tiles = lax.all_gather(value, "space", axis=0, tiled=True)
        found = [jnp.roll(tiles, -me, axis=0)]
        size = 1
    hop = 1
    while hop < size:
        have = jnp.concatenate(found, axis=0)
        pairs = [
            (i * VARS + v, (i ^ hop) * VARS + 1 - v) for i in range(size) for v in range(VARS)
        ]
        found.append(lax.ppermute(have, ("space", "var"), pairs))
        hop *= 2
    found.append(from_group(jnp.concatenate(found, axis=0), 0, 1))
    return found


def body(right_side, spatial, columns, counts, season_cov):
    del columns
    seasons = right_side.shape[0]
    blocks, _, width, _ = spatial.shape
    parts = lax.axis_size("season")
    half = blocks // 2
    places = make_chunks(half)
    plan = make_plan(places, half)

    x = right_side.reshape(seasons * blocks, width)
    count_rows = jnp.broadcast_to(counts.astype(F32)[:, None], (blocks, width))

    same, other, *packs = pack(x, places, blocks)
    close = [same, from_group(other, 0, 1)]
    chunks = [
        [from_group(pair[w], d, w) for d in range(1, parts) for w in range(VARS)]
        for pair in zip(packs[0::2], packs[1::2])
    ]
    w2, top = prepare(spatial)
    outer, inner = edge(w2, count_rows, close + chunks[0], parts, places[0])
    outer, inner = across_edge(outer), from_group(inner, 0, 1)

    season = season_cov.transpose(0, 1, 3, 2).reshape(SEASONS * VARS * VARS, SEASONS)
    rh, rl, scale = make_mixer(season, top)
    sums = jnp.zeros((4, 8, width), F32)
    mine, theirs, kept = [], [], []
    for m, stage in enumerate(STAGES):
        operands = close + [f for c in stage if c >= 0 for f in chunks[c]]
        operands += [w2, rh, rl, count_rows, sums] + kept + [outer] * (OUTER in stage) + [inner] * (INNER in stage)
        out = run_stage(plan, places, m, blocks, parts, seasons, width, operands)
        sums, kept = out[0], list(out[3:])
        mine.append(out[1])
        theirs.append(from_group(out[2], 0, 1))
    tile = jnp.concatenate([jnp.sum(sums, axis=1), scale[4:]], axis=0)[None]
    gathered = gather_tiles(tile)
    x_out, r_out = finish(plan, (seasons, blocks, 1, width), gathered, [same, other], mine, theirs)
    return x_out.reshape(right_side.shape), r_out.reshape(right_side.shape)


def solution(mesh):
    field = P("season", "var", ("groups", "space"))
    return jax.shard_map(
        body,
        mesh=mesh,
        in_specs=(
            field,
            P(("groups", "space"), None, None, None),
            P(("groups", "space"), None),
            P(("groups", "space")),
            P(),
        ),
        out_specs=(field, field),
        check_vma=False,
    )
```

```python
import functools

import jax
import jax.numpy as jnp
from jax import lax
from jax.experimental import pallas as pl
from jax.experimental.pallas import tpu as pltpu
from jax.sharding import PartitionSpec as P

SEASONS = 64
VARS = 2
ORDER = SEASONS * VARS
REACH = 1
NUGGET = 10.5
LIMIT = 16 << 20
GROUP = 16
ROOMY = 50 << 20
COST = pl.CostEstimate(flops=1, bytes_accessed=1, transcendentals=0)
ENDS = (2, 2)
LAST = 3
OUTER, INNER = -1, -2
STAGES = ((0, 1, INNER), (OUTER, 2))

F32 = jnp.float32
BF16 = jnp.bfloat16
NT = (((1,), (1,)), ((), ()))
NN = (((1,), (0,)), ((), ()))
VMEM = pltpu.VMEM


def dot(a, b, dims):
    return lax.dot_general(a, b, dims, preferred_element_type=F32)


def halves(x):
    high = x.astype(BF16)
    return high, (x - high.astype(F32)).astype(BF16)


def fold(x):
    return jnp.sum(x.reshape(x.shape[0] // 8, 8, x.shape[1]), axis=0)


def block_at(half_id, m, blocks):
    return m + half_id * (blocks - 1 - 2 * m)


def make_chunks(half):
    ends = [i for i in range(half) if i < ENDS[0] or i >= half - ENDS[1]]
    rest = [i for i in range(half) if i not in ends]
    return ends, rest[LAST:], rest[:LAST]


def pack_kernel(chunks, blocks, x_ref, same_ref, other_ref, *chunk_refs):
    me = lax.axis_index("var")
    seasons = x_ref.shape[0] // blocks
    for c, places in enumerate(chunks):
        for at, m in enumerate(places):
            for n, (half_id, ref) in enumerate(((me, same_ref), (1 - me, other_ref))):
                value = x_ref[pl.ds(block_at(half_id, m, blocks), seasons, stride=blocks), :]
                ref[m] = value
                chunk_refs[2 * c + n][at] = value


def pack(x, chunks, blocks):
    seasons, width = x.shape[0] // blocks, x.shape[1]
    counts = [blocks // 2] + [len(places) for places in chunks]
    shapes = [(count, seasons, width) for count in counts for _ in range(2)]
    return pl.pallas_call(
        functools.partial(pack_kernel, chunks, blocks),
        in_specs=[pl.BlockSpec(memory_space=VMEM)],
        out_specs=[pl.BlockSpec(memory_space=VMEM)] * len(shapes),
        out_shape=[jax.ShapeDtypeStruct(shape, F32) for shape in shapes],
        compiler_params=pltpu.CompilerParams(vmem_limit_bytes=LIMIT),
        cost_estimate=COST,
        name="pack",
    )(x)


def prepare_kernel(blocks, w_ref, w2_ref, scale_ref, held, sems):
    me = lax.axis_index("var")
    count, width = held.shape[0], held.shape[2]
    base = me * (blocks - count)
    chunks = sems.shape[0]
    edges = [count * c // chunks for c in range(chunks + 1)]
    copies = [
        pltpu.make_async_copy(
            w_ref.at[pl.ds(base + first, last - first)], held.at[pl.ds(first, last - first)], sem
        )
        for first, last, sem in zip(edges[:-1], edges[1:], [sems.at[c] for c in range(chunks)])
    ]
    for copy in copies:
        copy.start()
    top = jnp.zeros((8, width), F32)
    for c, copy in enumerate(copies):
        copy.wait()
        for row in range(edges[c], edges[c + 1]):
            m = block_at(me, row, count)
            for place, slot in enumerate((1 + me, 0, 2 - me)):
                w = held[row, slot]
                high, low = halves(w)
                lanes = slice(place * width, (place + 1) * width)
                w2_ref[m, :width, lanes] = high
                w2_ref[m, width:, lanes] = low
                top = jnp.maximum(top, jnp.max(jnp.abs(w).reshape(-1, 8, width), axis=0))
    space_top = jnp.max(jnp.max(top, axis=0, keepdims=True), axis=1, keepdims=True)
    space_top = jnp.where(space_top > 0, space_top, 1.0)
    scale_ref[...] = jnp.broadcast_to(space_top, scale_ref.shape)


def prepare(spatial):
    blocks, slots, width, _ = spatial.shape
    count = blocks // 2
    return pl.pallas_call(
        functools.partial(prepare_kernel, blocks),
        in_specs=[pl.BlockSpec(memory_space=pl.ANY)],
        out_specs=[pl.BlockSpec(memory_space=VMEM)] * 2,
        out_shape=[
            jax.ShapeDtypeStruct((count, 2 * width, slots * width), BF16),
            jax.ShapeDtypeStruct((8, width), F32),
        ],
        scratch_shapes=[
            VMEM((count, slots, width, width), F32),
            pltpu.SemaphoreType.DMA((4,)),
        ],
        compiler_params=pltpu.CompilerParams(vmem_limit_bytes=ROOMY),
        cost_estimate=COST,
        name="prepare",
    )(spatial)


def mixer_kernel(season_ref, top_ref, rh_ref, rl_ref, scale_ref):
    r = jnp.concatenate(
        [
            jnp.concatenate(
                [
                    season_ref[pl.ds(VARS * v + w, SEASONS, stride=VARS * VARS), :]
                    for w in range(VARS)
                ],
                axis=1,
            )
            for v in range(VARS)
        ],
        axis=0,
    )
    space_top = top_ref[:1, :1]
    season_top = jnp.max(jnp.max(jnp.abs(r), axis=0, keepdims=True), axis=1, keepdims=True)
    season_top = jnp.where(season_top > 0, season_top, 1.0)
    rh_ref[...], rl_ref[...] = halves(r / season_top / space_top)
    rows = lax.broadcasted_iota(jnp.int32, scale_ref.shape, 0)
    scale_ref[...] = jnp.where(rows == 4, space_top, jnp.where(rows == 5, season_top, 0.0))


def make_mixer(season, top):
    return pl.pallas_call(
        mixer_kernel,
        in_specs=[pl.BlockSpec(memory_space=VMEM)] * 2,
        out_specs=[pl.BlockSpec(memory_space=VMEM)] * 3,
        out_shape=[
            jax.ShapeDtypeStruct((ORDER, ORDER), BF16),
            jax.ShapeDtypeStruct((ORDER, ORDER), BF16),
            jax.ShapeDtypeStruct(top.shape, F32),
        ],
        compiler_params=pltpu.CompilerParams(vmem_limit_bytes=LIMIT),
        cost_estimate=COST,
        name="mixer",
    )(season, top)


def row_starts(seasons, parts):
    me_season, me_var = lax.axis_index("season"), lax.axis_index("var")
    return [
        pl.multiple_of(
            lax.rem(me_var + w, VARS) * SEASONS + lax.rem(me_season + d, parts) * seasons, seasons
        )
        for d in range(parts)
        for w in range(VARS)
    ]


def iota(rows, width):
    return lax.broadcasted_iota(jnp.int32, (rows, width), 0)


def space_product(high, low, w2):
    width = w2.shape[0] // 2
    both = dot(jnp.concatenate([high, low], axis=0), w2, NT)
    return both[:ORDER, :width] + both[:ORDER, width:] + both[ORDER:, :width]


def edge_kernel(blocks, parts, first, w2_ref, count_ref, *refs):
    *fields, outer_ref, inner_ref, held = refs
    me = lax.axis_index("var")
    seasons, width = fields[0].shape[1:]
    half = blocks // 2
    ends = (0, 1, half - 2, half - 1)
    for k, (start, field) in enumerate(zip(row_starts(seasons, parts), fields)):
        season = (iota(seasons, width) + lax.rem(start, SEASONS)).astype(F32)
        for n, m in enumerate(ends):
            seen = season >= SEASONS - count_ref[pl.ds(block_at(me, m, blocks), 1), :]
            piece = field[m if k < VARS else first.index(m)]
            held[n, pl.ds(start, seasons), :] = jnp.where(seen, piece, 0.0)
    for ref, n, at, lanes in (
        (outer_ref, 0, 0, slice(width, 3 * width)),
        (inner_ref, 2, half - 1, slice(0, 2 * width)),
    ):
        high, low = halves(jnp.concatenate([held[n], held[n + 1]], axis=1))
        ref[:ORDER, :] = held[0 if n == 0 else 3]
        ref[ORDER : 2 * ORDER, :] = space_product(high, low, w2_ref[at, :, lanes])
    inner_ref[2 * ORDER :, :] = jnp.zeros((16, width), F32)
    outer_ref[2 * ORDER :, :] = jnp.broadcast_to(
        count_ref[pl.ds(block_at(me, 0, blocks), 1), :], (8, width)
    )


def edge(w2, count_rows, fields, parts, first):
    blocks, width = count_rows.shape
    whole = [pl.BlockSpec(memory_space=VMEM)]
    return pl.pallas_call(
        functools.partial(edge_kernel, blocks, parts, first),
        in_specs=whole * (2 + len(fields)),
        out_specs=whole * 2,
        out_shape=[
            jax.ShapeDtypeStruct((2 * ORDER + 8, width), F32),
            jax.ShapeDtypeStruct((2 * ORDER + 16, width), F32),
        ],
        scratch_shapes=[VMEM((4, ORDER, width), F32)],
        compiler_params=pltpu.CompilerParams(vmem_limit_bytes=LIMIT),
        cost_estimate=COST,
        name="edge",
    )(w2, count_rows, *fields)


def make_plan(places_of, half):
    plan = []
    have_x, have_1, have_2 = set(), set(), set()
    for chunks in STAGES:
        new = []
        for c in chunks:
            new += [-1] if c == OUTER else [half] if c == INNER else places_of[c]
        have_x |= set(new)
        ones = [
            i
            for i in range(-1, half + 1)
            if i not in have_1 and {max(i - 1, -1), i, min(i + 1, half)} <= have_x
        ]
        have_1 |= set(ones)
        twos = [i for i in range(half) if i not in have_2 and {i - 1, i, i + 1} <= have_1]
        have_2 |= set(twos)
        later_1 = [i for i in range(-1, half + 1) if i not in have_1]
        later_2 = [i for i in range(half) if i not in have_2]
        keep_x = sorted({i + d for i in later_1 for d in (-1, 0, 1)} & have_x)
        keep_1 = sorted({i + d for i in later_2 for d in (-1, 0, 1)} & have_1)
        plan.append((new, ones, twos, keep_x, keep_1))
    return plan


def in_half(ids, half):
    return [i for i in ids if 0 <= i < half]


def runs(ids, most):
    groups = []
    for i in ids:
        if groups and len(groups[-1]) < most:
            groups[-1].append(i)
        else:
            groups.append([i])
    return groups


def make_stage(plan, places_of, m, blocks, parts, seasons, width):
    half = blocks // 2
    slots = parts * VARS
    new, ones, twos, keep_x, keep_1 = plan[m]
    first, last = m == 0, m == len(plan) - 1
    chunks = [c for c in STAGES[m] if c >= 0]
    outer, inner = OUTER in STAGES[m], INNER in STAGES[m]
    old_x, old_1 = ([], []) if first else (plan[m - 1][3], plan[m - 1][4])
    x_at = {i: n for n, i in enumerate(list(old_x) + list(new))}
    one_at = {i: n for n, i in enumerate(list(old_1) + list(ones))}
    inner_ones = in_half(ones, half)

    def kernel(*refs):
        refs = list(refs)

        def take(n):
            out = refs[:n]
            del refs[:n]
            return out

        near_refs = take(VARS)
        far_refs = [take(slots - VARS) for _ in chunks]
        w2_ref, rh_ref, rl_ref, count_ref, sums_in = take(5)
        if not first:
            old_xh, old_xl, old_1h, old_1l = take(4)
        if outer:
            (outer_ref,) = take(1)
        if inner:
            (inner_ref,) = take(1)
        sums_out, mine, theirs = take(3)
        if not last:
            keep_xh, keep_xl, keep_1h, keep_1l = take(4)
        xh, xl, oh, ol, pick = take(5)
        me = lax.axis_index("var")

        def count_row(i):
            if i == -1:
                return outer_ref[2 * ORDER : 2 * ORDER + 1, :]
            return count_ref[pl.ds(block_at(me, i, blocks), 1), :]

        season = lax.rem(iota(ORDER, width), SEASONS).astype(F32)

        def masked(i, value):
            return jnp.where(season >= SEASONS - count_row(i), value, 0.0)

        for n in range(len(old_x)):
            xh[n] = old_xh[n]
            xl[n] = old_xl[n]
        for n in range(len(old_1)):
            oh[n] = old_1h[n]
            ol[n] = old_1l[n]

        starts = row_starts(seasons, parts)
        total_0 = sums_in[0]
        for c, fars in zip(chunks, far_refs):
            places = places_of[c]
            for k, start in enumerate(starts):
                piece_season = (iota(seasons, width) + lax.rem(start, SEASONS)).astype(F32)
                for i in places:
                    piece = near_refs[k][i] if k < VARS else fars[k - VARS][places.index(i)]
                    total_0 += fold(piece * piece)
                    seen = piece_season >= SEASONS - count_row(i)
                    high, low = halves(jnp.where(seen, piece, 0.0))
                    xh[x_at[i], pl.ds(start, seasons), :] = high
                    xl[x_at[i], pl.ds(start, seasons), :] = low
        if outer:
            xh[x_at[-1]], xl[x_at[-1]] = halves(outer_ref[:ORDER, :])
        if inner:
            xh[x_at[half]], xl[x_at[half]] = halves(inner_ref[:ORDER, :])
        sums_out[0] = total_0

        def space(i, high, low, at):
            if 0 <= i < half:
                hs = jnp.concatenate([high[at[i + d]] for d in (-1, 0, 1)], axis=1)
                ls = jnp.concatenate([low[at[i + d]] for d in (-1, 0, 1)], axis=1)
                return space_product(hs, ls, w2_ref[i])
            ref, last_at, lane = (outer_ref, 0, 0) if i < 0 else (inner_ref, half - 1, 2 * width)
            lanes = slice(lane, lane + width)
            near = w2_ref[last_at, :width, lanes]
            total = ref[ORDER : 2 * ORDER, :] + dot(high[at[last_at]], near, NN)
            total += dot(high[at[last_at]], w2_ref[last_at, width:, lanes], NN)
            return total + dot(low[at[last_at]], near, NN)

        rh, rl = rh_ref[...], rl_ref[...]
        mixer = jnp.concatenate(
            [
                jnp.concatenate([rh, rh], axis=1),
                jnp.concatenate([rl, jnp.zeros_like(rl)], axis=1),
            ],
            axis=0,
        )

        def mix(parts_of):
            zh, zl = halves(jnp.concatenate(parts_of, axis=1))
            both = dot(mixer, jnp.concatenate([zh, zl], axis=0), NN)
            return both[:ORDER] + both[ORDER:]

        def hand_out(n, value):
            pick[n] = value
            mine[n] = pick[n, pl.ds(starts[0], seasons), :]
            theirs[n] = pick[n, pl.ds(starts[1], seasons), :]

        total_1, total_2, total_3 = sums_in[1], sums_in[2], sums_in[3]
        for group in runs(ones, GROUP):
            mixed = mix([space(i, xh, xl, x_at) for i in group])
            for n, i in enumerate(group):
                one = masked(i, mixed[:, n * width : (n + 1) * width])
                oh[one_at[i]], ol[one_at[i]] = halves(one)
                if 0 <= i < half:
                    x = xh[x_at[i]].astype(F32) + xl[x_at[i]].astype(F32)
                    total_1 += fold(x * one)
                    total_2 += fold(one * one)
                    hand_out(inner_ones.index(i), one)
        sums_out[1] = total_1
        sums_out[2] = total_2
        for group in runs(twos, GROUP):
            mixed = mix([space(i, oh, ol, one_at) for i in group])
            for n, i in enumerate(group):
                two = masked(i, mixed[:, n * width : (n + 1) * width])
                one = oh[one_at[i]].astype(F32) + ol[one_at[i]].astype(F32)
                total_3 += fold(one * two)
                hand_out(len(inner_ones) + twos.index(i), two)
        sums_out[3] = total_3
        if not last:
            for n, i in enumerate(keep_x):
                keep_xh[n] = xh[x_at[i]]
                keep_xl[n] = xl[x_at[i]]
            for n, i in enumerate(keep_1):
                keep_1h[n] = oh[one_at[i]]
                keep_1l[n] = ol[one_at[i]]

    tile = (ORDER, width)
    count = len(inner_ones) + len(twos)
    outs = [jax.ShapeDtypeStruct((4, 8, width), F32)]
    outs += [jax.ShapeDtypeStruct((count, seasons, width), F32)] * 2
    if not last:
        outs += [jax.ShapeDtypeStruct((len(keep_x),) + tile, BF16)] * 2
        outs += [jax.ShapeDtypeStruct((len(keep_1),) + tile, BF16)] * 2
    scratch = [VMEM((len(x_at),) + tile, BF16)] * 2 + [VMEM((len(one_at),) + tile, BF16)] * 2
    scratch += [VMEM((count,) + tile, F32)]
    return kernel, outs, scratch


def run_stage(plan, chunks, m, blocks, parts, seasons, width, operands):
    kernel, outs, scratch = make_stage(plan, chunks, m, blocks, parts, seasons, width)
    return pl.pallas_call(
        kernel,
        in_specs=[pl.BlockSpec(memory_space=VMEM)] * len(operands),
        out_shape=outs,
        scratch_shapes=scratch,
        compiler_params=pltpu.CompilerParams(vmem_limit_bytes=LIMIT),
        cost_estimate=COST,
        name="stage",
    )(*operands)


def finish_kernel(plan, blocks, tiles, *refs):
    refs = list(refs)
    count = len(plan)
    gathered, refs = refs[:tiles], refs[tiles:]
    fields, refs = refs[:2], refs[2:]
    mine, theirs = refs[:count], refs[count : 2 * count]
    x_out, r_out, x_held, r_held, sems = refs[2 * count :]
    half = blocks // 2
    me = lax.axis_index("var")

    def total(v):
        return jnp.sum(v, axis=1, keepdims=True)

    tuples = [ref[j] for ref in gathered for j in range(ref.shape[0])]
    top = functools.reduce(jnp.maximum, [t[4:5] for t in tuples])
    sums = [0.0, 0.0, 0.0, 0.0]
    for t in tuples:
        ratio = t[4:5] / top
        factor = jnp.ones_like(ratio)
        for n in range(4):
            sums[n] = sums[n] + t[n : n + 1] * factor
            factor = factor * ratio
    m0, m1, m2, m3 = [total(v) for v in sums]
    scale = (top * tuples[0][5:6])[:, :1]

    first = NUGGET * m0 + scale * m1
    alpha = m0 / first
    lead = alpha * scale
    mean = m1 / m0
    fresh = lead * lead * jnp.maximum(m2 - mean * m1, 0.0)
    beta = fresh / m0
    c = lead * mean + beta
    dd = fresh + beta * fresh
    dkd = c * c * m1 - 2.0 * c * lead * m2 + lead * lead * m3
    below = NUGGET * dd + scale * dkd
    alpha_2 = jnp.where(below == 0.0, 0.0, fresh / jnp.where(below == 0.0, 1.0, below))
    x_0 = alpha + alpha_2 * c
    r_0 = lead * mean - NUGGET * alpha_2 * c
    x_1 = -alpha_2 * lead
    r_1 = NUGGET * alpha_2 * lead - lead - alpha_2 * scale * c
    r_2 = alpha_2 * scale * lead

    one_at, two_at = {}, {}
    for m, (_, ones, twos, _, _) in enumerate(plan):
        inner = in_half(ones, half)
        one_at.update({i: (m, n) for n, i in enumerate(inner)})
        two_at.update({i: (m, len(inner) + n) for n, i in enumerate(twos)})
    copies = []
    for side, (half_id, held, t) in enumerate(((me, mine, tuples[0]), (1 - me, theirs, tuples[len(tuples) // 2]))):
        ratio = (t[4:5] / top)[:, :1]
        x_1h, r_1h, r_2h = x_1 * ratio, r_1 * ratio, r_2 * ratio * ratio
        for i in range(half):
            x = fields[side][i]
            m, n = one_at[i]
            one = held[m][n]
            m, n = two_at[i]
            two = held[m][n]
            at = side * half + i
            x_held[at] = x_0 * x + x_1h * one
            r_held[at] = r_0 * x + r_1h * one + r_2h * two
            row = block_at(half_id, i, blocks)
            for n, (source, target) in enumerate(((x_held, x_out), (r_held, r_out))):
                copy = pltpu.make_async_copy(
                    source.at[at], target.at[:, row, 0, :], sems.at[n, at]
                )
                copy.start()
                copies.append(copy)
    for copy in copies:
        copy.wait()


def finish(plan, shape, gathered, packs, mine, theirs):
    seasons, blocks, _, width = shape
    operands = [*gathered, *packs, *mine, *theirs]
    return pl.pallas_call(
        functools.partial(finish_kernel, plan, blocks, len(gathered)),
        in_specs=[pl.BlockSpec(memory_space=VMEM)] * len(operands),
        out_specs=[pl.BlockSpec(memory_space=pltpu.HBM)] * 2,
        out_shape=[jax.ShapeDtypeStruct(shape, F32)] * 2,
        scratch_shapes=[VMEM((blocks, seasons, width), F32)] * 2
        + [pltpu.SemaphoreType.DMA((2, blocks))],
        compiler_params=pltpu.CompilerParams(vmem_limit_bytes=LIMIT),
        cost_estimate=COST,
        name="finish",
    )(*operands)


def from_group(value, step, swap):
    size = lax.axis_size("season")
    pairs = [
        (((p + step) % size) * VARS + (v + swap) % VARS, p * VARS + v)
        for p in range(size)
        for v in range(VARS)
    ]
    return lax.ppermute(value, ("season", "var"), pairs)


def across_edge(value):
    size = lax.axis_size("space")
    pairs = []
    for i in range(1, size * VARS - 1, 2):
        pairs += [(i, i + 1), (i + 1, i)]
    return lax.ppermute(value, ("space", "var"), pairs)


def gather_tiles(value):
    found = [value]
    size = lax.axis_size("space")
    if size & (size - 1):
        me = lax.axis_index("space")
        tiles = lax.all_gather(value, "space", axis=0, tiled=True)
        found = [jnp.roll(tiles, -me, axis=0)]
        size = 1
    hop = 1
    while hop < size:
        have = jnp.concatenate(found, axis=0)
        pairs = [
            (i * VARS + v, (i ^ hop) * VARS + 1 - v) for i in range(size) for v in range(VARS)
        ]
        found.append(lax.ppermute(have, ("space", "var"), pairs))
        hop *= 2
    found.append(from_group(jnp.concatenate(found, axis=0), 0, 1))
    return found


def body(right_side, spatial, columns, counts, season_cov):
    del columns
    seasons = right_side.shape[0]
    blocks, _, width, _ = spatial.shape
    parts = lax.axis_size("season")
    half = blocks // 2
    places = make_chunks(half)
    plan = make_plan(places, half)

    x = right_side.reshape(seasons * blocks, width)
    count_rows = jnp.broadcast_to(counts.astype(F32)[:, None], (blocks, width))

    same, other, *packs = pack(x, places, blocks)
    close = [same, from_group(other, 0, 1)]
    chunks = [
        [from_group(pair[w], d, w) for d in range(1, parts) for w in range(VARS)]
        for pair in zip(packs[0::2], packs[1::2])
    ]
    w2, top = prepare(spatial)
    outer, inner = edge(w2, count_rows, close + chunks[0], parts, places[0])
    outer, inner = across_edge(outer), from_group(inner, 0, 1)

    season = season_cov.transpose(0, 1, 3, 2).reshape(SEASONS * VARS * VARS, SEASONS)
    rh, rl, scale = make_mixer(season, top)
    sums = jnp.zeros((4, 8, width), F32)
    mine, theirs, kept = [], [], []
    for m, stage in enumerate(STAGES):
        operands = close + [f for c in stage if c >= 0 for f in chunks[c]]
        operands += [w2, rh, rl, count_rows, sums] + kept + [outer] * (OUTER in stage) + [inner] * (INNER in stage)
        out = run_stage(plan, places, m, blocks, parts, seasons, width, operands)
        sums, kept = out[0], list(out[3:])
        mine.append(out[1])
        theirs.append(from_group(out[2], 0, 1))
    tile = jnp.concatenate([jnp.sum(sums, axis=1), scale[4:]], axis=0)[None]
    gathered = gather_tiles(tile)
    x_out, r_out = finish(plan, (seasons, blocks, 1, width), gathered, [same, other], mine, theirs)
    return x_out.reshape(right_side.shape), r_out.reshape(right_side.shape)


def solution(mesh):
    field = P("season", "var", ("groups", "space"))
    return jax.shard_map(
        body,
        mesh=mesh,
        in_specs=(
            field,
            P(("groups", "space"), None, None, None),
            P(("groups", "space"), None),
            P(("groups", "space")),
            P(),
        ),
        out_specs=(field, field),
        check_vma=False,
    )
```

```python
import functools

import jax
import jax.numpy as jnp
from jax import lax
from jax.experimental import pallas as pl
from jax.experimental.pallas import tpu as pltpu
from jax.sharding import PartitionSpec as P

SEASONS = 64
VARS = 2
ORDER = SEASONS * VARS
REACH = 1
NUGGET = 10.5
LIMIT = 16 << 20
GROUP = 16
ROOMY = 50 << 20
COST = pl.CostEstimate(flops=1, bytes_accessed=1, transcendentals=0)
ENDS = (2, 2)
LAST = 3
OUTER, INNER = -1, -2
STAGES = ((0, 1, INNER), (OUTER, 2))

F32 = jnp.float32
BF16 = jnp.bfloat16
NT = (((1,), (1,)), ((), ()))
NN = (((1,), (0,)), ((), ()))
VMEM = pltpu.VMEM


def dot(a, b, dims):
    return lax.dot_general(a, b, dims, preferred_element_type=F32)


def halves(x):
    high = x.astype(BF16)
    return high, (x - high.astype(F32)).astype(BF16)


def fold(x):
    return jnp.sum(x.reshape(x.shape[0] // 8, 8, x.shape[1]), axis=0)


def block_at(half_id, m, blocks):
    return m + half_id * (blocks - 1 - 2 * m)


def make_chunks(half):
    ends = [i for i in range(half) if i < ENDS[0] or i >= half - ENDS[1]]
    rest = [i for i in range(half) if i not in ends]
    return ends, rest[LAST:], rest[:LAST]


def pack_kernel(chunks, blocks, x_ref, same_ref, other_ref, *chunk_refs):
    me = lax.axis_index("var")
    seasons = x_ref.shape[0] // blocks
    for c, places in enumerate(chunks):
        for at, m in enumerate(places):
            for n, (half_id, ref) in enumerate(((me, same_ref), (1 - me, other_ref))):
                value = x_ref[pl.ds(block_at(half_id, m, blocks), seasons, stride=blocks), :]
                ref[m] = value
                chunk_refs[2 * c + n][at] = value


def pack(x, chunks, blocks):
    seasons, width = x.shape[0] // blocks, x.shape[1]
    counts = [blocks // 2] + [len(places) for places in chunks]
    shapes = [(count, seasons, width) for count in counts for _ in range(2)]
    return pl.pallas_call(
        functools.partial(pack_kernel, chunks, blocks),
        in_specs=[pl.BlockSpec(memory_space=VMEM)],
        out_specs=[pl.BlockSpec(memory_space=VMEM)] * len(shapes),
        out_shape=[jax.ShapeDtypeStruct(shape, F32) for shape in shapes],
        compiler_params=pltpu.CompilerParams(vmem_limit_bytes=LIMIT),
        cost_estimate=COST,
        name="pack",
    )(x)


def prepare_kernel(blocks, w_ref, w2_ref, scale_ref, held, sems):
    me = lax.axis_index("var")
    count, width = held.shape[0], held.shape[2]
    base = me * (blocks - count)
    chunks = sems.shape[0]
    edges = [count * c // chunks for c in range(chunks + 1)]
    copies = [
        pltpu.make_async_copy(
            w_ref.at[pl.ds(base + first, last - first)], held.at[pl.ds(first, last - first)], sem
        )
        for first, last, sem in zip(edges[:-1], edges[1:], [sems.at[c] for c in range(chunks)])
    ]
    for copy in copies:
        copy.start()
    top = jnp.zeros((8, width), F32)
    for c, copy in enumerate(copies):
        copy.wait()
        for row in range(edges[c], edges[c + 1]):
            m = block_at(me, row, count)
            for place, slot in enumerate((1 + me, 0, 2 - me)):
                w = held[row, slot]
                high, low = halves(w)
                lanes = slice(place * width, (place + 1) * width)
                w2_ref[m, :width, lanes] = high
                w2_ref[m, width:, lanes] = low
                top = jnp.maximum(top, jnp.max(jnp.abs(w).reshape(-1, 8, width), axis=0))
    space_top = jnp.max(jnp.max(top, axis=0, keepdims=True), axis=1, keepdims=True)
    space_top = jnp.where(space_top > 0, space_top, 1.0)
    scale_ref[...] = jnp.broadcast_to(space_top, scale_ref.shape)


def prepare(spatial):
    blocks, slots, width, _ = spatial.shape
    count = blocks // 2
    return pl.pallas_call(
        functools.partial(prepare_kernel, blocks),
        in_specs=[pl.BlockSpec(memory_space=pl.ANY)],
        out_specs=[pl.BlockSpec(memory_space=VMEM)] * 2,
        out_shape=[
            jax.ShapeDtypeStruct((count, 2 * width, slots * width), BF16),
            jax.ShapeDtypeStruct((8, width), F32),
        ],
        scratch_shapes=[
            VMEM((count, slots, width, width), F32),
            pltpu.SemaphoreType.DMA((8,)),
        ],
        compiler_params=pltpu.CompilerParams(vmem_limit_bytes=ROOMY),
        cost_estimate=COST,
        name="prepare",
    )(spatial)


def mixer_kernel(season_ref, top_ref, rh_ref, rl_ref, scale_ref):
    r = jnp.concatenate(
        [
            jnp.concatenate(
                [
                    season_ref[pl.ds(VARS * v + w, SEASONS, stride=VARS * VARS), :]
                    for w in range(VARS)
                ],
                axis=1,
            )
            for v in range(VARS)
        ],
        axis=0,
    )
    space_top = top_ref[:1, :1]
    season_top = jnp.max(jnp.max(jnp.abs(r), axis=0, keepdims=True), axis=1, keepdims=True)
    season_top = jnp.where(season_top > 0, season_top, 1.0)
    rh_ref[...], rl_ref[...] = halves(r / season_top / space_top)
    rows = lax.broadcasted_iota(jnp.int32, scale_ref.shape, 0)
    scale_ref[...] = jnp.where(rows == 4, space_top, jnp.where(rows == 5, season_top, 0.0))


def make_mixer(season, top):
    return pl.pallas_call(
        mixer_kernel,
        in_specs=[pl.BlockSpec(memory_space=VMEM)] * 2,
        out_specs=[pl.BlockSpec(memory_space=VMEM)] * 3,
        out_shape=[
            jax.ShapeDtypeStruct((ORDER, ORDER), BF16),
            jax.ShapeDtypeStruct((ORDER, ORDER), BF16),
            jax.ShapeDtypeStruct(top.shape, F32),
        ],
        compiler_params=pltpu.CompilerParams(vmem_limit_bytes=LIMIT),
        cost_estimate=COST,
        name="mixer",
    )(season, top)


def row_starts(seasons, parts):
    me_season, me_var = lax.axis_index("season"), lax.axis_index("var")
    return [
        pl.multiple_of(
            lax.rem(me_var + w, VARS) * SEASONS + lax.rem(me_season + d, parts) * seasons, seasons
        )
        for d in range(parts)
        for w in range(VARS)
    ]


def iota(rows, width):
    return lax.broadcasted_iota(jnp.int32, (rows, width), 0)


def space_product(high, low, w2):
    width = w2.shape[0] // 2
    both = dot(jnp.concatenate([high, low], axis=0), w2, NT)
    return both[:ORDER, :width] + both[:ORDER, width:] + both[ORDER:, :width]


def edge_kernel(blocks, parts, first, w2_ref, count_ref, *refs):
    *fields, outer_ref, inner_ref, held = refs
    me = lax.axis_index("var")
    seasons, width = fields[0].shape[1:]
    half = blocks // 2
    ends = (0, 1, half - 2, half - 1)
    for k, (start, field) in enumerate(zip(row_starts(seasons, parts), fields)):
        season = (iota(seasons, width) + lax.rem(start, SEASONS)).astype(F32)
        for n, m in enumerate(ends):
            seen = season >= SEASONS - count_ref[pl.ds(block_at(me, m, blocks), 1), :]
            piece = field[m if k < VARS else first.index(m)]
            held[n, pl.ds(start, seasons), :] = jnp.where(seen, piece, 0.0)
    for ref, n, at, lanes in (
        (outer_ref, 0, 0, slice(width, 3 * width)),
        (inner_ref, 2, half - 1, slice(0, 2 * width)),
    ):
        high, low = halves(jnp.concatenate([held[n], held[n + 1]], axis=1))
        ref[:ORDER, :] = held[0 if n == 0 else 3]
        ref[ORDER : 2 * ORDER, :] = space_product(high, low, w2_ref[at, :, lanes])
    inner_ref[2 * ORDER :, :] = jnp.zeros((16, width), F32)
    outer_ref[2 * ORDER :, :] = jnp.broadcast_to(
        count_ref[pl.ds(block_at(me, 0, blocks), 1), :], (8, width)
    )


def edge(w2, count_rows, fields, parts, first):
    blocks, width = count_rows.shape
    whole = [pl.BlockSpec(memory_space=VMEM)]
    return pl.pallas_call(
        functools.partial(edge_kernel, blocks, parts, first),
        in_specs=whole * (2 + len(fields)),
        out_specs=whole * 2,
        out_shape=[
            jax.ShapeDtypeStruct((2 * ORDER + 8, width), F32),
            jax.ShapeDtypeStruct((2 * ORDER + 16, width), F32),
        ],
        scratch_shapes=[VMEM((4, ORDER, width), F32)],
        compiler_params=pltpu.CompilerParams(vmem_limit_bytes=LIMIT),
        cost_estimate=COST,
        name="edge",
    )(w2, count_rows, *fields)


def make_plan(places_of, half):
    plan = []
    have_x, have_1, have_2 = set(), set(), set()
    for chunks in STAGES:
        new = []
        for c in chunks:
            new += [-1] if c == OUTER else [half] if c == INNER else places_of[c]
        have_x |= set(new)
        ones = [
            i
            for i in range(-1, half + 1)
            if i not in have_1 and {max(i - 1, -1), i, min(i + 1, half)} <= have_x
        ]
        have_1 |= set(ones)
        twos = [i for i in range(half) if i not in have_2 and {i - 1, i, i + 1} <= have_1]
        have_2 |= set(twos)
        later_1 = [i for i in range(-1, half + 1) if i not in have_1]
        later_2 = [i for i in range(half) if i not in have_2]
        keep_x = sorted({i + d for i in later_1 for d in (-1, 0, 1)} & have_x)
        keep_1 = sorted({i + d for i in later_2 for d in (-1, 0, 1)} & have_1)
        plan.append((new, ones, twos, keep_x, keep_1))
    return plan


def in_half(ids, half):
    return [i for i in ids if 0 <= i < half]


def runs(ids, most):
    groups = []
    for i in ids:
        if groups and len(groups[-1]) < most:
            groups[-1].append(i)
        else:
            groups.append([i])
    return groups


def make_stage(plan, places_of, m, blocks, parts, seasons, width):
    half = blocks // 2
    slots = parts * VARS
    new, ones, twos, keep_x, keep_1 = plan[m]
    first, last = m == 0, m == len(plan) - 1
    chunks = [c for c in STAGES[m] if c >= 0]
    outer, inner = OUTER in STAGES[m], INNER in STAGES[m]
    old_x, old_1 = ([], []) if first else (plan[m - 1][3], plan[m - 1][4])
    x_at = {i: n for n, i in enumerate(list(old_x) + list(new))}
    one_at = {i: n for n, i in enumerate(list(old_1) + list(ones))}
    inner_ones = in_half(ones, half)

    def kernel(*refs):
        refs = list(refs)

        def take(n):
            out = refs[:n]
            del refs[:n]
            return out

        near_refs = take(VARS)
        far_refs = [take(slots - VARS) for _ in chunks]
        w2_ref, rh_ref, rl_ref, count_ref, sums_in = take(5)
        if not first:
            old_xh, old_xl, old_1h, old_1l = take(4)
        if outer:
            (outer_ref,) = take(1)
        if inner:
            (inner_ref,) = take(1)
        sums_out, mine, theirs = take(3)
        if not last:
            keep_xh, keep_xl, keep_1h, keep_1l = take(4)
        xh, xl, oh, ol, pick = take(5)
        me = lax.axis_index("var")

        def count_row(i):
            if i == -1:
                return outer_ref[2 * ORDER : 2 * ORDER + 1, :]
            return count_ref[pl.ds(block_at(me, i, blocks), 1), :]

        season = lax.rem(iota(ORDER, width), SEASONS).astype(F32)

        def masked(i, value):
            return jnp.where(season >= SEASONS - count_row(i), value, 0.0)

        for n in range(len(old_x)):
            xh[n] = old_xh[n]
            xl[n] = old_xl[n]
        for n in range(len(old_1)):
            oh[n] = old_1h[n]
            ol[n] = old_1l[n]

        starts = row_starts(seasons, parts)
        total_0 = sums_in[0]
        for c, fars in zip(chunks, far_refs):
            places = places_of[c]
            for k, start in enumerate(starts):
                piece_season = (iota(seasons, width) + lax.rem(start, SEASONS)).astype(F32)
                for i in places:
                    piece = near_refs[k][i] if k < VARS else fars[k - VARS][places.index(i)]
                    total_0 += fold(piece * piece)
                    seen = piece_season >= SEASONS - count_row(i)
                    high, low = halves(jnp.where(seen, piece, 0.0))
                    xh[x_at[i], pl.ds(start, seasons), :] = high
                    xl[x_at[i], pl.ds(start, seasons), :] = low
        if outer:
            xh[x_at[-1]], xl[x_at[-1]] = halves(outer_ref[:ORDER, :])
        if inner:
            xh[x_at[half]], xl[x_at[half]] = halves(inner_ref[:ORDER, :])
        sums_out[0] = total_0

        def space(i, high, low, at):
            if 0 <= i < half:
                hs = jnp.concatenate([high[at[i + d]] for d in (-1, 0, 1)], axis=1)
                ls = jnp.concatenate([low[at[i + d]] for d in (-1, 0, 1)], axis=1)
                return space_product(hs, ls, w2_ref[i])
            ref, last_at, lane = (outer_ref, 0, 0) if i < 0 else (inner_ref, half - 1, 2 * width)
            lanes = slice(lane, lane + width)
            near = w2_ref[last_at, :width, lanes]
            total = ref[ORDER : 2 * ORDER, :] + dot(high[at[last_at]], near, NN)
            total += dot(high[at[last_at]], w2_ref[last_at, width:, lanes], NN)
            return total + dot(low[at[last_at]], near, NN)

        rh, rl = rh_ref[...], rl_ref[...]
        mixer = jnp.concatenate(
            [
                jnp.concatenate([rh, rh], axis=1),
                jnp.concatenate([rl, jnp.zeros_like(rl)], axis=1),
            ],
            axis=0,
        )

        def mix(parts_of):
            zh, zl = halves(jnp.concatenate(parts_of, axis=1))
            both = dot(mixer, jnp.concatenate([zh, zl], axis=0), NN)
            return both[:ORDER] + both[ORDER:]

        def hand_out(n, value):
            pick[n] = value
            mine[n] = pick[n, pl.ds(starts[0], seasons), :]
            theirs[n] = pick[n, pl.ds(starts[1], seasons), :]

        total_1, total_2, total_3 = sums_in[1], sums_in[2], sums_in[3]
        for group in runs(ones, GROUP):
            mixed = mix([space(i, xh, xl, x_at) for i in group])
            for n, i in enumerate(group):
                one = masked(i, mixed[:, n * width : (n + 1) * width])
                oh[one_at[i]], ol[one_at[i]] = halves(one)
                if 0 <= i < half:
                    x = xh[x_at[i]].astype(F32) + xl[x_at[i]].astype(F32)
                    total_1 += fold(x * one)
                    total_2 += fold(one * one)
                    hand_out(inner_ones.index(i), one)
        sums_out[1] = total_1
        sums_out[2] = total_2
        for group in runs(twos, GROUP):
            mixed = mix([space(i, oh, ol, one_at) for i in group])
            for n, i in enumerate(group):
                two = masked(i, mixed[:, n * width : (n + 1) * width])
                one = oh[one_at[i]].astype(F32) + ol[one_at[i]].astype(F32)
                total_3 += fold(one * two)
                hand_out(len(inner_ones) + twos.index(i), two)
        sums_out[3] = total_3
        if not last:
            for n, i in enumerate(keep_x):
                keep_xh[n] = xh[x_at[i]]
                keep_xl[n] = xl[x_at[i]]
            for n, i in enumerate(keep_1):
                keep_1h[n] = oh[one_at[i]]
                keep_1l[n] = ol[one_at[i]]

    tile = (ORDER, width)
    count = len(inner_ones) + len(twos)
    outs = [jax.ShapeDtypeStruct((4, 8, width), F32)]
    outs += [jax.ShapeDtypeStruct((count, seasons, width), F32)] * 2
    if not last:
        outs += [jax.ShapeDtypeStruct((len(keep_x),) + tile, BF16)] * 2
        outs += [jax.ShapeDtypeStruct((len(keep_1),) + tile, BF16)] * 2
    scratch = [VMEM((len(x_at),) + tile, BF16)] * 2 + [VMEM((len(one_at),) + tile, BF16)] * 2
    scratch += [VMEM((count,) + tile, F32)]
    return kernel, outs, scratch


def run_stage(plan, chunks, m, blocks, parts, seasons, width, operands):
    kernel, outs, scratch = make_stage(plan, chunks, m, blocks, parts, seasons, width)
    return pl.pallas_call(
        kernel,
        in_specs=[pl.BlockSpec(memory_space=VMEM)] * len(operands),
        out_shape=outs,
        scratch_shapes=scratch,
        compiler_params=pltpu.CompilerParams(vmem_limit_bytes=LIMIT),
        cost_estimate=COST,
        name="stage",
    )(*operands)


def finish_kernel(plan, blocks, tiles, *refs):
    refs = list(refs)
    count = len(plan)
    gathered, refs = refs[:tiles], refs[tiles:]
    fields, refs = refs[:2], refs[2:]
    mine, theirs = refs[:count], refs[count : 2 * count]
    x_out, r_out, x_held, r_held, sems = refs[2 * count :]
    half = blocks // 2
    me = lax.axis_index("var")

    def total(v):
        return jnp.sum(v, axis=1, keepdims=True)

    tuples = [ref[j] for ref in gathered for j in range(ref.shape[0])]
    top = functools.reduce(jnp.maximum, [t[4:5] for t in tuples])
    sums = [0.0, 0.0, 0.0, 0.0]
    for t in tuples:
        ratio = t[4:5] / top
        factor = jnp.ones_like(ratio)
        for n in range(4):
            sums[n] = sums[n] + t[n : n + 1] * factor
            factor = factor * ratio
    m0, m1, m2, m3 = [total(v) for v in sums]
    scale = (top * tuples[0][5:6])[:, :1]

    first = NUGGET * m0 + scale * m1
    alpha = m0 / first
    lead = alpha * scale
    mean = m1 / m0
    fresh = lead * lead * jnp.maximum(m2 - mean * m1, 0.0)
    beta = fresh / m0
    c = lead * mean + beta
    dd = fresh + beta * fresh
    dkd = c * c * m1 - 2.0 * c * lead * m2 + lead * lead * m3
    below = NUGGET * dd + scale * dkd
    alpha_2 = jnp.where(below == 0.0, 0.0, fresh / jnp.where(below == 0.0, 1.0, below))
    x_0 = alpha + alpha_2 * c
    r_0 = lead * mean - NUGGET * alpha_2 * c
    x_1 = -alpha_2 * lead
    r_1 = NUGGET * alpha_2 * lead - lead - alpha_2 * scale * c
    r_2 = alpha_2 * scale * lead

    one_at, two_at = {}, {}
    for m, (_, ones, twos, _, _) in enumerate(plan):
        inner = in_half(ones, half)
        one_at.update({i: (m, n) for n, i in enumerate(inner)})
        two_at.update({i: (m, len(inner) + n) for n, i in enumerate(twos)})
    copies = []
    for side, (half_id, held, t) in enumerate(((me, mine, tuples[0]), (1 - me, theirs, tuples[len(tuples) // 2]))):
        ratio = (t[4:5] / top)[:, :1]
        x_1h, r_1h, r_2h = x_1 * ratio, r_1 * ratio, r_2 * ratio * ratio
        for i in range(half):
            x = fields[side][i]
            m, n = one_at[i]
            one = held[m][n]
            m, n = two_at[i]
            two = held[m][n]
            at = side * half + i
            x_held[at] = x_0 * x + x_1h * one
            r_held[at] = r_0 * x + r_1h * one + r_2h * two
            row = block_at(half_id, i, blocks)
            for n, (source, target) in enumerate(((x_held, x_out), (r_held, r_out))):
                copy = pltpu.make_async_copy(
                    source.at[at], target.at[:, row, 0, :], sems.at[n, at]
                )
                copy.start()
                copies.append(copy)
    for copy in copies:
        copy.wait()


def finish(plan, shape, gathered, packs, mine, theirs):
    seasons, blocks, _, width = shape
    operands = [*gathered, *packs, *mine, *theirs]
    return pl.pallas_call(
        functools.partial(finish_kernel, plan, blocks, len(gathered)),
        in_specs=[pl.BlockSpec(memory_space=VMEM)] * len(operands),
        out_specs=[pl.BlockSpec(memory_space=pltpu.HBM)] * 2,
        out_shape=[jax.ShapeDtypeStruct(shape, F32)] * 2,
        scratch_shapes=[VMEM((blocks, seasons, width), F32)] * 2
        + [pltpu.SemaphoreType.DMA((2, blocks))],
        compiler_params=pltpu.CompilerParams(vmem_limit_bytes=LIMIT),
        cost_estimate=COST,
        name="finish",
    )(*operands)


def from_group(value, step, swap):
    size = lax.axis_size("season")
    pairs = [
        (((p + step) % size) * VARS + (v + swap) % VARS, p * VARS + v)
        for p in range(size)
        for v in range(VARS)
    ]
    return lax.ppermute(value, ("season", "var"), pairs)


def across_edge(value):
    size = lax.axis_size("space")
    pairs = []
    for i in range(1, size * VARS - 1, 2):
        pairs += [(i, i + 1), (i + 1, i)]
    return lax.ppermute(value, ("space", "var"), pairs)


def gather_tiles(value):
    found = [value]
    size = lax.axis_size("space")
    if size & (size - 1):
        me = lax.axis_index("space")
        tiles = lax.all_gather(value, "space", axis=0, tiled=True)
        found = [jnp.roll(tiles, -me, axis=0)]
        size = 1
    hop = 1
    while hop < size:
        have = jnp.concatenate(found, axis=0)
        pairs = [
            (i * VARS + v, (i ^ hop) * VARS + 1 - v) for i in range(size) for v in range(VARS)
        ]
        found.append(lax.ppermute(have, ("space", "var"), pairs))
        hop *= 2
    found.append(from_group(jnp.concatenate(found, axis=0), 0, 1))
    return found


def body(right_side, spatial, columns, counts, season_cov):
    del columns
    seasons = right_side.shape[0]
    blocks, _, width, _ = spatial.shape
    parts = lax.axis_size("season")
    half = blocks // 2
    places = make_chunks(half)
    plan = make_plan(places, half)

    x = right_side.reshape(seasons * blocks, width)
    count_rows = jnp.broadcast_to(counts.astype(F32)[:, None], (blocks, width))

    same, other, *packs = pack(x, places, blocks)
    close = [same, from_group(other, 0, 1)]
    chunks = [
        [from_group(pair[w], d, w) for d in range(1, parts) for w in range(VARS)]
        for pair in zip(packs[0::2], packs[1::2])
    ]
    w2, top = prepare(spatial)
    outer, inner = edge(w2, count_rows, close + chunks[0], parts, places[0])
    outer, inner = across_edge(outer), from_group(inner, 0, 1)

    season = season_cov.transpose(0, 1, 3, 2).reshape(SEASONS * VARS * VARS, SEASONS)
    rh, rl, scale = make_mixer(season, top)
    sums = jnp.zeros((4, 8, width), F32)
    mine, theirs, kept = [], [], []
    for m, stage in enumerate(STAGES):
        operands = close + [f for c in stage if c >= 0 for f in chunks[c]]
        operands += [w2, rh, rl, count_rows, sums] + kept + [outer] * (OUTER in stage) + [inner] * (INNER in stage)
        out = run_stage(plan, places, m, blocks, parts, seasons, width, operands)
        sums, kept = out[0], list(out[3:])
        mine.append(out[1])
        theirs.append(from_group(out[2], 0, 1))
    tile = jnp.concatenate([jnp.sum(sums, axis=1), scale[4:]], axis=0)[None]
    gathered = gather_tiles(tile)
    x_out, r_out = finish(plan, (seasons, blocks, 1, width), gathered, [same, other], mine, theirs)
    return x_out.reshape(right_side.shape), r_out.reshape(right_side.shape)


def solution(mesh):
    field = P("season", "var", ("groups", "space"))
    return jax.shard_map(
        body,
        mesh=mesh,
        in_specs=(
            field,
            P(("groups", "space"), None, None, None),
            P(("groups", "space"), None),
            P(("groups", "space")),
            P(),
        ),
        out_specs=(field, field),
        check_vma=False,
    )
```
